32 devices in a mesh: seq: 8 (over z, y), head: 4 (over x, core).
Axes of the slice: x: 2, y: 2, z: 4, core: 2. Of those that a mesh axis runs over, the one named last changes fastest.
Arguments:
- tiles: bfloat16 [6, 4096, 768], P(None, ('seq', 'head')), may hold values from -6 to 6
- coords: int32 [6, 4096, 2], P(None, ('seq', 'head')), may hold values from 0 to 255
- lengths: int32 [6], replicated, may hold values from 1024 to 4096, as said below
- padding_mask: int32 [6, 4096], replicated, may hold values from 0 to 1, as said below
- ln1_gain: float32 [768], replicated, may hold values from 0.1 to 1.9
- ln1_bias: float32 [768], replicated, may hold values from -4 to 4
- query_key_value_weight: bfloat16 [768, 3, 768], P(None, None, 'head'), may hold values from -0.21875 to 0.21875
- qv_bias: float32 [2, 768], P(None, 'head'), may hold values from -6 to 6
- attention_output_weight: bfloat16 [768, 768], P('head'), may hold values from -4 to 4
- attention_output_bias: float32 [768], replicated, may hold values from -4 to 4
- ln2_gain: float32 [768], replicated, may hold values from 0.1 to 1.9
- ln2_bias: float32 [768], replicated, may hold values from -4 to 4
- mlp_entry_matrix: bfloat16 [768, 3072], P(None, 'head'), may hold values from -0.21875 to 0.21875
- mlp_entry_offset: float32 [3072], P('head'), may hold values from -6 to 6
- feed_output_weight: bfloat16 [3072, 768], P('head'), may hold values from -0.109375 to 0.109375
- feed_output_bias: float32 [768], replicated, may hold values from -4 to 4
- cotangent: bfloat16 [6, 4096, 768], P(None, ('seq', 'head')), may hold values from -6 to 6
Outputs:
- output: bfloat16 [6, 4096, 768], P(None, ('seq', 'head'))
- tiles_grad: bfloat16 [6, 4096, 768], P(None, ('seq', 'head'))
- ln1_gain_grad: float32 [768], replicated
- ln1_bias_grad: float32 [768], replicated
- w_qkv_grad: float32 [768, 3, 768], P('seq', None, 'head')
- qv_bias_grad: float32 [2, 768], P(None, 'head')
- w_out_grad: float32 [768, 768], P('head', 'seq')
- out_bias_grad: float32 [768], replicated
- ln2_gain_grad: float32 [768], replicated
- ln2_bias_grad: float32 [768], replicated
- w_fc1_grad: float32 [768, 3072], P('seq', 'head')
- fc1_bias_grad: float32 [3072], P('head')
- w_fc2_grad: float32 [3072, 768], P('head', 'seq')
- fc2_bias_grad: float32 [768], replicated
The draws below stay inside these ranges and needn't reach their ends.
Inputs may be any that keep to these rules, and one draw needn't show every extreme that they name: `lengths`: one slide, drawn from the seed, uses all 4096 tiles; each other slide uses 4096 // 4 or more. `padding_mask`: the first 16 tiles of every slide are marked 1.
All inputs are finite; a program needn't handle non-finite values.
Results may differ from the reference program's by a relative error of at most 0.02.
Values may be sent and summed in bfloat16 or wider, within the bound.
No kernel may reach another device: no remote copies, remote signals or barrier semaphores. Data moves between devices by JAX's collectives and lax.ppermute only.
A program may use at most 384 MiB of HBM per device.

```python
import math
import jax
import jax.numpy as jnp
from jax import lax

D = 768
HEADS = 16
FF = 3072
SLIDES = 6
SEG = 1024
SEG2 = 5792
RATIO = 16
LEN = 4096


def draw_lengths(key, part):
    key = jax.random.fold_in(key, 11)
    pick_key, len_key = jax.random.split(key)
    full_slide = jax.random.randint(pick_key, (), 0, SLIDES)
    drawn = jax.random.randint(len_key, (SLIDES,), LEN // 4, LEN + 1)
    return jnp.where(jnp.arange(SLIDES) == full_slide, LEN, drawn).astype(jnp.int32)


def draw_padding_mask(key, part):
    key = jax.random.fold_in(key, 23)
    coin = jax.random.randint(key, (SLIDES, LEN), 0, 20)
    keep = (coin < 17) | (jnp.arange(LEN)[None, :] < RATIO)
    return keep.astype(jnp.int32)


def set_ends(entries, own_key, least, largest):
    longest = entries.shape.index(max(entries.shape))
    spots = []
    for shift in (0, 1):
        where = [jax.random.randint(jax.random.fold_in(own_key, axis), (), 0, length) for axis, length in enumerate(entries.shape)]
        where[longest] = (where[longest] + shift) % entries.shape[longest]
        spots.append(tuple(where))
    return entries.at[spots[0]].set(least).at[spots[1]].set(largest)


def block_levels(rng, extent, cuts, low, largest):
    level, own = 1.0, jax.random.fold_in(rng, 6)
    for position, blocks in cuts:
        draws = jnp.exp(jax.random.uniform(jax.random.fold_in(own, position), (blocks,), jnp.float32, low / len(cuts), largest / len(cuts)))
        level = level * jnp.repeat(draws, extent[position] // blocks).reshape([-1 if axis == position else 1 for axis in range(len(extent))])
    return level


def centred(own_key, shape, scale, most, cuts=(), held_as=jnp.bfloat16):
    array = jax.random.normal(own_key, shape, jnp.float32) * scale
    if len(cuts) > 0:
        array = block_levels(own_key, shape, cuts, -0.22, 0.18) * array
    return jnp.clip(array, min=-most, max=most).astype(held_as)


def setup_inputs(seed: int = 0) -> dict:
    splits = jax.random.split(jax.random.key(seed), 18)
    tiles = centred(splits[0], (SLIDES, LEN, D), 1.0, 6.0, ((1, 32),))
    coords = set_ends(jax.random.randint(splits[1], (SLIDES, LEN, 2), 0, 256), jax.random.fold_in(splits[1], 1), 0, 255).astype(jnp.int32)
    lengths = draw_lengths(jax.random.fold_in(splits[17], 71), 0)
    padding_mask = draw_padding_mask(jax.random.fold_in(splits[17], 71), 0)
    ln1_gain = jnp.clip(1.0 + 0.18 * jax.random.normal(splits[4], (D,), jnp.float32), 0.1, 1.9)
    ln1_bias = centred(splits[5], (D,), 0.3, 4.0, (), jnp.float32)
    query_key_value_weight = centred(splits[6], (D, 3, D), D ** -0.5, 0.21875, ((2, 4),))
    qv_bias = centred(splits[7], (2, D), 0.5, 6.0, ((1, 4),), jnp.float32)
    attention_output_weight = centred(splits[8], (D, D), 2 ** -0.5, 4.0, ((0, 4),))
    attention_output_bias = centred(splits[9], (D,), 0.3, 4.0, (), jnp.float32)
    ln2_gain = jnp.clip(1.0 + 0.18 * jax.random.normal(splits[10], (D,), jnp.float32), 0.1, 1.9)
    ln2_bias = centred(splits[11], (D,), 0.3, 4.0, (), jnp.float32)
    mlp_entry_matrix = centred(splits[12], (D, FF), D ** -0.5, 0.21875, ((1, 4),))
    mlp_entry_offset = centred(splits[13], (FF,), 0.5, 6.0, ((0, 4),), jnp.float32)
    feed_output_weight = centred(splits[14], (FF, D), FF ** -0.5, 0.109375, ((0, 4),))
    feed_output_bias = centred(splits[15], (D,), 0.3, 4.0, (), jnp.float32)
    cotangent = centred(splits[16], (SLIDES, LEN, D), 1.0, 6.0, ((1, 32),))
    return {"tiles": tiles, "coords": coords, "lengths": lengths, "padding_mask": padding_mask, "ln1_gain": ln1_gain, "ln1_bias": ln1_bias, "query_key_value_weight": query_key_value_weight, "qv_bias": qv_bias, "attention_output_weight": attention_output_weight, "attention_output_bias": attention_output_bias, "ln2_gain": ln2_gain, "ln2_bias": ln2_bias, "mlp_entry_matrix": mlp_entry_matrix, "mlp_entry_offset": mlp_entry_offset, "feed_output_weight": feed_output_weight, "feed_output_bias": feed_output_bias, "cotangent": cotangent}


@jax.custom_vjp
def low(v):
    return lax.optimization_barrier(v.astype(jnp.bfloat16)).astype(jnp.float32)

@jax.custom_vjp
def compiled_reverse_pass(v):
    return v

def low_keep(v):
    return (low(v), None)

def low_pass(kept, grad):
    return (grad,)

def back_keep(v):
    return (v, None)

def back_low(kept, grad):
    return (low(grad),)
low.defvjp(low_keep, low_pass)
compiled_reverse_pass.defvjp(back_keep, back_low)
TOP_MATMUL_MODE = lax.Precision.HIGHEST
NEG = -10000.0
FLOOR = -1e+30
EPS = 1e-05

def layer_norm(value, gain, shift):
    mean = lax.optimization_barrier(jnp.mean(value, axis=-1, keepdims=True))
    centered = value - mean
    var = lax.optimization_barrier(jnp.mean(centered * centered, axis=-1, keepdims=True))
    return centered * lax.rsqrt(var + EPS) * gain + shift

def position_table(coords, width):
    quarter = width // 4
    freq = jnp.exp(-jnp.log(10000.0) * jnp.arange(quarter, dtype=jnp.float32) / quarter)
    col_angle = coords[..., 0:1].astype(jnp.float32) * freq
    row_angle = coords[..., 1:2].astype(jnp.float32) * freq
    return jnp.concatenate([jnp.sin(col_angle), jnp.cos(col_angle), jnp.sin(row_angle), jnp.cos(row_angle)], axis=-1)

def attend(query, keys, values, bias, pair):
    scale = 1.0 / math.sqrt(D // HEADS)
    scores = jnp.einsum('qhe,khe->hqk', query, keys, precision=TOP_MATMUL_MODE) * scale + jnp.transpose(bias)[:, None, :] + pair
    scores = compiled_reverse_pass(scores)
    total = jax.nn.logsumexp(scores, axis=-1)
    probs = low(jnp.exp(scores - total[..., None]))
    result = jnp.einsum('hqk,khe->qhe', probs, values, precision=TOP_MATMUL_MODE)
    return (result, jnp.transpose(total)[..., None])

def far_branch(query, keys, values, valid, dilation, reach):
    head_dim = D // HEADS
    head_ids = jnp.arange(HEADS, dtype=jnp.int32)
    offsets = head_ids % dilation
    count = LEN // dilation

    def strided(value):
        return value.reshape((count, dilation) + value.shape[1:])[:, offsets, head_ids]
    key_bias = jnp.where(valid.reshape(count, dilation)[:, offsets], 0.0, NEG)
    places = dilation * jnp.arange(count, dtype=jnp.int32)
    block = math.gcd(count, 512)
    far_keys = strided(keys)
    far_values = strided(values)

    def per_block(args):
        q_block, p_block = args
        pair = jnp.where((p_block // reach)[:, None] == (places // reach)[None, :], 0.0, NEG)
        return attend(q_block, far_keys, far_values, key_bias, pair)
    out, total = lax.map(jax.checkpoint(per_block), (strided(query).reshape(count // block, block, HEADS, head_dim), places.reshape(count // block, block)))
    out = compiled_reverse_pass(out.reshape(count, HEADS, head_dim))
    total = total.reshape(count, HEADS, 1)

    def spread(value):
        full = jnp.zeros((count, dilation) + value.shape[1:], jnp.float32).at[:, offsets, head_ids].set(value)
        return full.reshape((LEN,) + value.shape[1:])
    chosen = jnp.arange(dilation, dtype=jnp.int32)[:, None] == offsets[None, :]
    selected = jnp.tile(chosen, (count, 1))[..., None]
    return (spread(out), jnp.where(selected, spread(total), FLOOR))

def slide_attention(query_key_value, valid):
    head_dim = D // HEADS
    bias = jnp.where(valid, 0.0, NEG)
    query, keys, values = (query_key_value[:, 0], query_key_value[:, 1], query_key_value[:, 2])
    count = LEN // SEG

    def segment(args):
        q_seg, k_seg, v_seg, b_seg = args
        return attend(q_seg, k_seg, v_seg, jnp.broadcast_to(b_seg[:, None], (SEG, HEADS)), 0.0)
    near_out, near_total = lax.map(jax.checkpoint(segment), (query.reshape(count, SEG, HEADS, head_dim), keys.reshape(count, SEG, HEADS, head_dim), values.reshape(count, SEG, HEADS, head_dim), bias.reshape(count, SEG)))
    near_out = compiled_reverse_pass(near_out.reshape(LEN, HEADS, head_dim))
    near_total = near_total.reshape(LEN, HEADS, 1)
    outs_all = [near_out]
    totals_all = [near_total]
    for dilation, reach in zip((RATIO // 8, RATIO // 4, RATIO // 2, RATIO), (SEG2, LEN, LEN, LEN)):
        far_out, far_total = far_branch(query, keys, values, valid, dilation, reach)
        outs_all.append(far_out)
        totals_all.append(far_total)
    stacked = jnp.stack(totals_all)
    highest = lax.optimization_barrier(jnp.max(stacked, axis=0))
    raised = jnp.exp(stacked - highest)
    weights = raised / lax.optimization_barrier(jnp.sum(raised, axis=0))
    combined_output = weights[0] * outs_all[0]
    for index in range(1, len(outs_all)):
        combined_output = combined_output + weights[index] * outs_all[index]
    return combined_output.reshape(LEN, D)

def forward(base, ln1_gain, ln1_bias, query_key_value_weight, qv_bias, attention_output_weight, attention_output_bias, ln2_gain, ln2_bias, mlp_entry_matrix, mlp_entry_offset, feed_output_weight, feed_output_bias, valid):
    first_normalized = low(layer_norm(base, ln1_gain, ln1_bias))
    triple_bias = jnp.stack([qv_bias[0], jnp.zeros_like(qv_bias[0]), qv_bias[1]])
    query_key_value = jnp.einsum('ymk,kpb->ympb', first_normalized, query_key_value_weight, precision=TOP_MATMUL_MODE) + triple_bias
    query_key_value = low(compiled_reverse_pass(query_key_value))
    query_key_value = query_key_value.reshape(SLIDES, LEN, 3, HEADS, D // HEADS)
    combined_output = lax.map(lambda pair: slide_attention(pair[0], pair[1]), (query_key_value, valid))
    combined_output = low(combined_output)
    attention_output = compiled_reverse_pass(jnp.einsum('mua,ah->muh', combined_output, attention_output_weight, precision=TOP_MATMUL_MODE) + attention_output_bias)
    mid = base + attention_output
    later_layernormed = low(layer_norm(mid, ln2_gain, ln2_bias))
    before_nonlinearity = compiled_reverse_pass(jnp.einsum('awq,qd->awd', later_layernormed, mlp_entry_matrix, precision=TOP_MATMUL_MODE) + mlp_entry_offset)
    hidden_activation = low(jax.nn.gelu(before_nonlinearity, approximate=False))
    feedforward_output = compiled_reverse_pass(jnp.einsum('nrv,vk->nrk', hidden_activation, feed_output_weight, precision=TOP_MATMUL_MODE) + feed_output_bias)
    return mid + feedforward_output

def reference(tiles, coords, lengths, padding_mask, ln1_gain, ln1_bias, query_key_value_weight, qv_bias, attention_output_weight, attention_output_bias, ln2_gain, ln2_bias, mlp_entry_matrix, mlp_entry_offset, feed_output_weight, feed_output_bias, cotangent):
    base = tiles.astype(jnp.float32) + position_table(coords, D)
    positions = jnp.arange(LEN, dtype=jnp.int32)
    valid = (positions[None, :] < lengths[:, None]) & (padding_mask == 1)
    params = tuple((p.astype(jnp.float32) for p in (ln1_gain, ln1_bias, query_key_value_weight, qv_bias, attention_output_weight, attention_output_bias, ln2_gain, ln2_bias, mlp_entry_matrix, mlp_entry_offset, feed_output_weight, feed_output_bias)))
    result, pull = jax.vjp(lambda *values: forward(*values, valid), base, *params)
    grads = pull(cotangent.astype(jnp.float32))
    return (result.astype(jnp.bfloat16), grads[0].astype(jnp.bfloat16), grads[1], grads[2], grads[3], grads[4], grads[5], grads[6], grads[7], grads[8], grads[9], grads[10], grads[11], grads[12])
```

```python
from functools import partial
import math

import jax
import jax.numpy as jnp
import ml_dtypes
import numpy as np
from jax import lax
from jax.experimental import pallas as pl
from jax.experimental.pallas import tpu as pltpu
from jax.sharding import PartitionSpec as P

HEADS = 16
FF = 3072
SEG2 = 5792
RATIO = 16


NEG = -10000.0
FLOOR = -1e30
EPS = 1e-05


def partner(x, axis, stride):
    return lax.ppermute(x, axis, [(i, i ^ 1 << stride) for i in range(lax.axis_size(axis))])


def layer_norm(value, gain, shift):
    mean = jnp.mean(value, axis=-1, keepdims=True)
    centered = value - mean
    var = jnp.mean(centered * centered, axis=-1, keepdims=True)
    return centered * lax.rsqrt(var + EPS) * gain + shift


def position_table(coords, width):
    quarter = width // 4
    freq = jnp.exp(-jnp.log(10000.0) * jnp.arange(quarter, dtype=jnp.float32) / quarter)
    col_angle = coords[..., 0:1].astype(jnp.float32) * freq
    row_angle = coords[..., 1:2].astype(jnp.float32) * freq
    return jnp.concatenate(
        [jnp.sin(col_angle), jnp.cos(col_angle), jnp.sin(row_angle), jnp.cos(row_angle)], axis=-1
    )


def mask_shape(value, chosen):
    return (1, 1, chosen.shape[0]) + (1,) * (value.ndim - 4) + (chosen.shape[1], 1)


def pick(value, chosen):
    rate = chosen.shape[0]
    split = value.reshape((value.shape[0], value.shape[1] // rate, rate) + value.shape[2:])
    return jnp.sum(
        jnp.where(chosen.reshape(mask_shape(value, chosen)), split, jnp.zeros((), value.dtype)),
        axis=2,
    )


def spread(value, chosen):
    rate = chosen.shape[0]
    full = jnp.where(
        chosen.reshape(mask_shape(value, chosen)),
        jnp.expand_dims(value, 2),
        jnp.zeros((), value.dtype),
    )
    return full.reshape((value.shape[0], value.shape[1] * rate) + value.shape[2:])


def scores_of(query, keys, bias, pair, scale):
    raw = jnp.einsum("qhe,khe->hqk", query, keys, preferred_element_type=jnp.float32)
    return raw * scale + jnp.transpose(bias)[:, None, :] + pair


def attend_forward(query, keys, values, bias, pair, scale):
    scores = scores_of(query, keys, bias, pair, scale)
    total = jax.nn.logsumexp(scores, axis=-1)
    probs = jnp.exp(scores - total[..., None]).astype(jnp.bfloat16)
    result = jnp.einsum("hqk,khe->qhe", probs, values, preferred_element_type=jnp.float32)
    return (result, jnp.transpose(total)[..., None])


def attend_backward(query, keys, values, bias, pair, total, grad_out, grad_total, scale):
    scores = scores_of(query, keys, bias, pair, scale)
    probs = jnp.exp(scores - jnp.transpose(total[..., 0])[..., None])
    grad_probs = jnp.einsum("qhe,khe->hqk", grad_out, values, preferred_element_type=jnp.float32)
    delta = jnp.sum(probs * grad_probs, axis=-1) - jnp.transpose(grad_total[..., 0])
    grad_scores = (probs * (grad_probs - delta[..., None])).astype(jnp.bfloat16)
    grad_query = (
        jnp.einsum("hqk,khe->qhe", grad_scores, keys, preferred_element_type=jnp.float32) * scale
    )
    grad_keys = (
        jnp.einsum("hqk,qhe->khe", grad_scores, query, preferred_element_type=jnp.float32) * scale
    )
    grad_values = jnp.einsum(
        "hqk,qhe->khe", probs.astype(jnp.bfloat16), grad_out, preferred_element_type=jnp.float32
    )
    return (grad_query, grad_keys, grad_values)


def forward_slide(args, pair, scale):
    q_one, kv_one, bias_one = args
    return attend_forward(q_one, kv_one[:, 0], kv_one[:, 1], bias_one, pair, scale)


def backward_slide(args, pair, scale):
    q_one, kv_one, bias_one, total_one, grad_one, grad_total_one = args
    return attend_backward(
        q_one,
        kv_one[:, 0],
        kv_one[:, 1],
        bias_one,
        pair,
        total_one,
        grad_one,
        grad_total_one,
        scale,
    )


def on_device(
    tiles,
    coords,
    lengths,
    padding_mask,
    ln1_gain,
    ln1_bias,
    query_key_value_weight,
    qv_bias,
    attention_output_weight,
    attention_output_bias,
    ln2_gain,
    ln2_bias,
    mlp_entry_matrix,
    mlp_entry_offset,
    feed_output_weight,
    feed_output_bias,
    cotangent,
):
    slides, rows, width = tiles.shape
    head_count = lax.axis_size("head")
    local_width = query_key_value_weight.shape[2]
    local_heads = local_width * HEADS // width
    head_dim = width // HEADS
    hidden_local = mlp_entry_matrix.shape[1]
    scale = 1.0 / math.sqrt(head_dim)
    seg_rows = rows * head_count
    total_len = padding_mask.shape[1]
    seq_index = lax.axis_index("seq")
    head_index = lax.axis_index("head")
    dilations = (RATIO // 8, RATIO // 4, RATIO // 2, RATIO)
    reaches = (SEG2, total_len, total_len, total_len)
    positions = jnp.arange(total_len, dtype=jnp.int32)
    valid = (positions[None, :] < lengths[:, None]) & (padding_mask == 1)
    own_valid = lax.dynamic_slice_in_dim(valid, seq_index * seg_rows, seg_rows, 1)
    mate_valid = lax.dynamic_slice_in_dim(valid, (seq_index ^ 1) * seg_rows, seg_rows, 1)
    near_valid = jnp.concatenate([own_valid, mate_valid], axis=1)
    near_bias = jnp.broadcast_to(
        jnp.where(near_valid, 0.0, NEG)[..., None], (slides, 2 * seg_rows, local_heads)
    )
    global_heads = head_index * local_heads + jnp.arange(local_heads, dtype=jnp.int32)
    chosens = []
    far_biases = []
    selects = []
    pair_masks = []
    for dilation, reach in zip(dilations, reaches):
        chosen = (
            jnp.arange(dilation, dtype=jnp.int32)[:, None] == (global_heads % dilation)[None, :]
        )
        chosens.append(chosen)
        far_valid = jnp.any(
            valid.reshape(slides, total_len // dilation, dilation)[..., None] & chosen[None, None],
            axis=2,
        )
        far_biases.append(jnp.where(far_valid, 0.0, NEG))
        selects.append(
            (
                (jnp.arange(seg_rows, dtype=jnp.int32) % dilation)[:, None]
                == (global_heads % dilation)[None, :]
            )[None, :, :, None]
        )
        query_places = seq_index * seg_rows + dilation * jnp.arange(
            seg_rows // dilation, dtype=jnp.int32
        )
        key_places = dilation * jnp.arange(total_len // dilation, dtype=jnp.int32)
        pair_masks.append(
            jnp.where((query_places // reach)[:, None] == (key_places // reach)[None, :], 0.0, NEG)
        )
    base = tiles.astype(jnp.float32) + position_table(coords, width)
    first_normalized = layer_norm(base, ln1_gain, ln1_bias).astype(jnp.bfloat16)
    initial_tokens, cotangent_rows = (
        lax.all_gather(first_normalized, "head", axis=1, tiled=True),
        lax.all_gather(cotangent, "head", axis=1, tiled=True),
    )
    packed_projection_matrix = query_key_value_weight.reshape(width, 3 * local_width)
    triple_bias = jnp.concatenate([qv_bias[0], jnp.zeros_like(qv_bias[0]), qv_bias[1]])
    query_key_value = (
        jnp.einsum(
            "hmq,qn->hmn",
            initial_tokens,
            packed_projection_matrix,
            preferred_element_type=jnp.float32,
        )
        + triple_bias
    ).astype(jnp.bfloat16)
    query_key_value = query_key_value.reshape(slides, seg_rows, 3, local_heads, head_dim)
    query = query_key_value[:, :, 0]
    key_value = query_key_value[:, :, 1:3]
    mate_kv = partner(key_value, "seq", 0)
    near_kv = jnp.concatenate([key_value, mate_kv], axis=1)

    def collect(piece):
        return tuple((pick(piece, chosens[index]) for index in range(4)))

    far_kvs = collect(lax.all_gather(key_value, "seq", axis=1, tiled=True))
    far_queries = [pick(query, chosen) for chosen in chosens]
    near_out, near_total = lax.map(
        partial(forward_slide, pair=0.0, scale=scale), (query, near_kv, near_bias)
    )
    far_results = []
    for index in range(4):
        far_results.append(
            lax.map(
                partial(forward_slide, pair=pair_masks[index], scale=scale),
                (far_queries[index], far_kvs[index], far_biases[index]),
            )
        )
    outs_full = [near_out] + [spread(far_results[index][0], chosens[index]) for index in range(4)]
    totals_full = [near_total] + [
        jnp.where(selects[index], spread(far_results[index][1], chosens[index]), FLOOR)
        for index in range(4)
    ]
    stacked = jnp.stack(totals_full)
    highest = jnp.max(stacked, axis=0)
    raised = jnp.exp(stacked - highest)
    weights = raised / jnp.sum(raised, axis=0)
    combined_output = weights[0] * outs_full[0]
    for index in range(1, 5):
        combined_output = combined_output + weights[index] * outs_full[index]
    combined_lowered = combined_output.reshape(slides, seg_rows, local_width).astype(jnp.bfloat16)
    attention_piece = jnp.einsum(
        "mua,ah->muh", combined_lowered, attention_output_weight, preferred_element_type=jnp.float32
    )
    attn_rows = lax.psum_scatter(
        attention_piece.astype(jnp.bfloat16), "head", scatter_dimension=1, tiled=True
    ).astype(jnp.float32)
    mid = base + (attn_rows + attention_output_bias)
    later_layernormed = layer_norm(mid, ln2_gain, ln2_bias).astype(jnp.bfloat16)
    later_tokens = lax.all_gather(later_layernormed, "head", axis=1, tiled=True)
    before_nonlinearity = (
        jnp.einsum(
            "awq,qd->awd", later_tokens, mlp_entry_matrix, preferred_element_type=jnp.float32
        )
        + mlp_entry_offset
    )
    hidden_activation = jax.nn.gelu(before_nonlinearity, approximate=False).astype(jnp.bfloat16)
    feedforward_piece = jnp.einsum(
        "nrv,vk->nrk", hidden_activation, feed_output_weight, preferred_element_type=jnp.float32
    )
    mlp_rows_sum = lax.psum_scatter(
        feedforward_piece.astype(jnp.bfloat16), "head", scatter_dimension=1, tiled=True
    ).astype(jnp.float32)
    output = mid + (mlp_rows_sum + feed_output_bias)
    cot_float = cotangent.astype(jnp.float32)
    grad_fc2_bias = jnp.sum(cot_float, axis=(0, 1))
    hidden_gradient = jnp.einsum(
        "tvq,cq->tvc", cotangent_rows, feed_output_weight, preferred_element_type=jnp.float32
    )
    feed_output_weight_gradient = jnp.einsum(
        "gar,gai->ri", hidden_activation, cotangent_rows, preferred_element_type=jnp.float32
    )
    gelu_pull = jax.vjp(lambda v: jax.nn.gelu(v, approximate=False), before_nonlinearity)[1]
    preactivation_gradient = gelu_pull(hidden_gradient)[0].astype(jnp.bfloat16)
    feed_input_weight_gradient = jnp.einsum(
        "vxr,vxm->rm", later_tokens, preactivation_gradient, preferred_element_type=jnp.float32
    )
    grad_fc1_bias = jnp.sum(preactivation_gradient.astype(jnp.float32), axis=(0, 1))
    second_backward = jnp.einsum(
        "ivo,go->ivg", preactivation_gradient, mlp_entry_matrix, preferred_element_type=jnp.float32
    )
    back2_rows = lax.psum_scatter(
        second_backward.astype(jnp.bfloat16), "head", scatter_dimension=1, tiled=True
    ).astype(jnp.float32)
    norm2_pull = jax.vjp(layer_norm, mid, ln2_gain, ln2_bias)[1]
    grad_mid_norm, grad_ln2_gain, grad_ln2_bias = norm2_pull(back2_rows)
    grad_mid = cot_float + grad_mid_norm
    grad_attn = grad_mid.astype(jnp.bfloat16)
    grad_out_bias = jnp.sum(grad_attn.astype(jnp.float32), axis=(0, 1))
    attention_rows_gradient = lax.all_gather(grad_attn, "head", axis=1, tiled=True)
    grad_w_out = jnp.einsum(
        "fub,fui->bi", combined_lowered, attention_rows_gradient, preferred_element_type=jnp.float32
    )
    grad_merged = jnp.einsum(
        "tpq,jq->tpj",
        attention_rows_gradient,
        attention_output_weight,
        preferred_element_type=jnp.float32,
    )
    grad_merged = grad_merged.reshape(slides, seg_rows, local_heads, head_dim)
    grad_parts = [weights[index] * grad_merged for index in range(5)]
    gaps = [
        weights[index]
        * jnp.sum(grad_merged * (outs_full[index] - combined_output), axis=-1, keepdims=True)
        for index in range(5)
    ]
    grad_near = grad_parts[0].astype(jnp.bfloat16)
    near_dq, near_dk, near_dv = lax.map(
        partial(backward_slide, pair=0.0, scale=scale),
        (query, near_kv, near_bias, near_total, grad_near, gaps[0]),
    )
    own_grad = jnp.stack([near_dk[:, :seg_rows], near_dv[:, :seg_rows]], axis=2)
    mate_grad = jnp.stack([near_dk[:, seg_rows:], near_dv[:, seg_rows:]], axis=2)
    returned = partner(mate_grad.astype(jnp.bfloat16), "seq", 0).astype(mate_grad.dtype)
    far_grads = []
    grad_query = near_dq
    for index in range(4):
        grad_far = pick(grad_parts[index + 1], chosens[index]).astype(jnp.bfloat16)
        grad_far_total = pick(gaps[index + 1], chosens[index])
        far_dq, far_dk, far_dv = lax.map(
            partial(backward_slide, pair=pair_masks[index], scale=scale),
            (
                far_queries[index],
                far_kvs[index],
                far_biases[index],
                far_results[index][1],
                grad_far,
                grad_far_total,
            ),
        )
        far_grads.append(jnp.stack([far_dk, far_dv], axis=2))
        grad_query = grad_query + spread(far_dq, chosens[index])
    far_back = (
        lax.psum_scatter(
            far_grads[0].astype(jnp.bfloat16), "seq", scatter_dimension=1, tiled=True
        ).astype(jnp.float32),
        lax.psum_scatter(
            far_grads[1].astype(jnp.bfloat16), "seq", scatter_dimension=1, tiled=True
        ).astype(jnp.float32),
        lax.psum_scatter(
            far_grads[2].astype(jnp.bfloat16), "seq", scatter_dimension=1, tiled=True
        ).astype(jnp.float32),
        lax.psum_scatter(
            far_grads[3].astype(jnp.bfloat16), "seq", scatter_dimension=1, tiled=True
        ).astype(jnp.float32),
    )
    grad_kv = own_grad + returned
    for index in range(4):
        grad_kv = grad_kv + spread(far_back[index], chosens[index])
    query_key_value_gradient = jnp.concatenate([grad_query[:, :, None], grad_kv], axis=2).astype(
        jnp.bfloat16
    )
    query_key_value_gradient = query_key_value_gradient.reshape(slides, seg_rows, 3 * local_width)
    grad_w_qkv = jnp.einsum(
        "ymt,yma->ta", initial_tokens, query_key_value_gradient, preferred_element_type=jnp.float32
    ).reshape(width, 3, local_width)
    bias_sums = jnp.sum(query_key_value_gradient.astype(jnp.float32), axis=(0, 1)).reshape(
        3, local_width
    )
    grad_qv = jnp.stack([bias_sums[0], bias_sums[2]])
    first_backward = jnp.einsum(
        "kgw,aw->kga",
        query_key_value_gradient,
        packed_projection_matrix,
        preferred_element_type=jnp.float32,
    )
    back1_rows = lax.psum_scatter(
        first_backward.astype(jnp.bfloat16), "head", scatter_dimension=1, tiled=True
    ).astype(jnp.float32)
    norm1_pull = jax.vjp(layer_norm, base, ln1_gain, ln1_bias)[1]
    grad_base_norm, grad_ln1_gain, grad_ln1_bias = norm1_pull(back1_rows)
    tiles_grad = (grad_mid + grad_base_norm).astype(jnp.bfloat16)
    w_qkv_grad, w_out_grad, w_fc1_grad, w_fc2_grad = (
        lax.psum_scatter(
            grad_w_qkv.astype(jnp.bfloat16), "seq", scatter_dimension=0, tiled=True
        ).astype(jnp.float32),
        lax.psum_scatter(
            grad_w_out.astype(jnp.bfloat16), "seq", scatter_dimension=1, tiled=True
        ).astype(jnp.float32),
        lax.psum_scatter(
            feed_input_weight_gradient.astype(jnp.bfloat16), "seq", scatter_dimension=0, tiled=True
        ).astype(jnp.float32),
        lax.psum_scatter(
            feed_output_weight_gradient.astype(jnp.bfloat16), "seq", scatter_dimension=1, tiled=True
        ).astype(jnp.float32),
    )
    shared = jnp.stack(
        [grad_ln1_gain, grad_ln1_bias, grad_out_bias, grad_ln2_gain, grad_ln2_bias, grad_fc2_bias]
    )
    qv_full = lax.dynamic_update_slice_in_dim(
        jnp.zeros((2, width), jnp.float32), grad_qv, head_index * local_width, 1
    )
    fc1_full = lax.dynamic_update_slice_in_dim(
        jnp.zeros((FF,), jnp.float32), grad_fc1_bias, head_index * hidden_local, 0
    )
    shared_sum, qv_sum, fc1_sum = lax.psum((shared, qv_full, fc1_full), ("seq", "head"))
    qv_bias_grad = lax.dynamic_slice_in_dim(qv_sum, head_index * local_width, local_width, 1)
    fc1_bias_grad = lax.dynamic_slice_in_dim(fc1_sum, head_index * hidden_local, hidden_local, 0)
    return (
        output.astype(jnp.bfloat16),
        tiles_grad,
        shared_sum[0],
        shared_sum[1],
        w_qkv_grad,
        qv_bias_grad,
        w_out_grad,
        shared_sum[2],
        shared_sum[3],
        shared_sum[4],
        w_fc1_grad,
        fc1_bias_grad,
        w_fc2_grad,
        shared_sum[5],
    )


HEAD_DIM = 48
TRIPLE = 144
META = 32
AUG = 128
OUT_ROWS = 64
ACC_ROWS = 56
SLOT_ORDER = (0, 2, 1, 3)
LOG2E = math.log2(math.e)
COST = 2.5
FIRST_COLUMNS = 1024
BF = jnp.bfloat16
F32 = jnp.float32


def dot(a, b):
    return lax.dot_general(a, b, (((1,), (0,)), ((), ())), preferred_element_type=F32)


def dot_nt(a, b):
    return lax.dot_general(a, b, (((1,), (1,)), ((), ())), preferred_element_type=F32)


def split3(value):
    high = value.astype(BF)
    rest = value - high.astype(F32)
    middle = rest.astype(BF)
    low = (rest - middle.astype(F32)).astype(BF)
    return high, middle, low


def split3_constant(value):
    pieces = []
    rest = np.float32(value)
    for _ in range(3):
        piece = np.float32(rest.astype(ml_dtypes.bfloat16))
        pieces.append(float(piece))
        rest = np.float32(rest - piece)
    return pieces


def joined(rows):
    wide = rows.astype(F32)
    return wide[0:1] + wide[1:2] + wide[2:3]


def rows_of(shape, first, pieces):
    row = lax.broadcasted_iota(jnp.int32, shape, 0)
    out = jnp.zeros(shape, F32)
    for index, piece in enumerate(pieces):
        out = jnp.where(row == first + index, piece, out)
    return out


def rows_between(shape, first, count):
    row = lax.broadcasted_iota(jnp.int32, shape, 0)
    return jnp.where((row >= first) & (row < first + count), 1.0, 0.0)


def query_rows(query, meta, factor):
    wide = query.astype(F32) * factor
    high = wide.astype(BF)
    low = (wide - high.astype(F32)).astype(BF)
    return jnp.concatenate([high, low, meta], 0)


def key_rows(keys, meta):
    return jnp.concatenate([keys, keys, meta], 0)


def ones_below(value, count):
    width = value.shape[-1]
    return jnp.concatenate([value, rows_between((16, width), 0, count).astype(BF)], 0)


def plain64(value):
    return jnp.concatenate([value, jnp.zeros((16, value.shape[-1]), value.dtype)], 0)


def padded_turn(value):
    height, width = value.shape
    missing = -height % 128
    full = jnp.concatenate([value, jnp.zeros((missing, width), value.dtype)], 0)
    return full.T


def turned_out(value):
    height = value.shape[0]
    return jnp.concatenate([value, jnp.zeros((height, 64), F32)], 1).T[0:HEAD_DIM]


def bias_rows(valid):
    shape = (META, valid.shape[-1])
    return rows_of(shape, 0, [(1.0 - valid) * part for part in split3_constant(NEG * LOG2E)])


def near_key_meta(valid):
    shape = (META, valid.shape[-1])
    return (bias_rows(valid) + rows_between(shape, 15, 3)).astype(BF)


def far_levels(place, width, half):
    head = 4 * (2 * place[2] + place[3]) + place[0]
    lane = lax.broadcasted_iota(jnp.int32, (1, width), 1)
    spot = (2 * (lane & (half - 1)) + (place[0] & 1)) & 15
    return jnp.where(
        spot == (head & 15),
        4,
        jnp.where((spot & 7) == (head & 7), 3, jnp.where((spot & 3) == (head & 3), 2, 1)),
    )


def far_tables(level):
    pieces = {0: [], 1: []}
    for extra in (0, 1):
        for part in range(3):
            for kind in range(1, 5):
                row = jnp.zeros(level.shape, F32)
                for there in range(1, 5):
                    amount = split3_constant(math.log2(min(kind, there) + extra))[part]
                    row = jnp.where(level == there, amount, row)
                pieces[extra].append(row)
    shape = (META, level.shape[-1])
    return rows_of(shape, 3, pieces[0]) + rows_between(shape, 15, 3) + rows_of(shape, 18, pieces[1])


def far_queries(level):
    shape = (META, level.shape[-1])
    chosen = [jnp.where(level == kind, 1.0, 0.0) for kind in range(1, 5)] * 3
    ones = rows_between(shape, 0, 3)
    return (ones + rows_of(shape, 18, chosen)).astype(BF), (ones + rows_of(shape, 3, chosen)).astype(BF)


def softmax_out(keys, values, queries, stage):
    top = None
    for index, key in enumerate(keys):
        scores = dot(key(), queries[index])
        stage[index] = scores
        peak = jnp.max(scores, axis=0, keepdims=True)
        top = peak if top is None else jnp.maximum(top, peak)
    acc = None
    for index, value in enumerate(values):
        probs = jnp.exp2(stage[index] - top).astype(BF)
        part = dot(value(), probs)
        acc = part if acc is None else acc + part
    total = acc[HEAD_DIM : HEAD_DIM + 1]
    return acc[0:HEAD_DIM] * (1.0 / total), top + jnp.log2(total)


def moments(value):
    mean = jnp.mean(value, axis=-1, keepdims=True)
    centered = value - mean
    var = jnp.mean(centered * centered, axis=-1, keepdims=True)
    rate = lax.rsqrt(var + EPS)
    return centered * rate, rate


def norm_back(xhat, rate, gain, upstream):
    a = upstream * gain
    return rate * (
        a - jnp.mean(a, axis=-1, keepdims=True) - xhat * jnp.mean(a * xhat, axis=-1, keepdims=True)
    )


def parity_order(rows, back):
    first = lax.broadcasted_iota(jnp.int32, (rows, rows), 1 if back else 0)
    second = lax.broadcasted_iota(jnp.int32, (rows, rows), 0 if back else 1)
    half = rows // 2
    source = jnp.where(first < half, 2 * first, 2 * (first - half) + 1)
    return (source == second).astype(F32).astype(BF)


def entry_kernel(
    place, tiles_a, tiles_b, coords_a, coords_b, cot_a, cot_b, table, base, cot_out, own, other
):
    rows = tiles_a.shape[1]
    half = rows // 2
    order = parity_order(rows, False)
    lane = lax.broadcasted_iota(jnp.int32, (rows, 256), 1).astype(F32)
    sides = ((tiles_a, coords_a, cot_a, own), (tiles_b, coords_b, cot_b, other))
    for side, (tiles, coords, cot, out) in enumerate(sides):
        spots = dot(order, coords[0].astype(F32).astype(BF))
        parts = []
        for axis in range(2):
            hot = (spots[:, axis : axis + 1] == lane).astype(F32).astype(BF)
            parts.append(dot(hot, table[0]) + dot(hot, table[1]) + dot(hot, table[2]))
        value = dot(order, tiles[0]) + jnp.concatenate(parts, 1)
        base[side, 0] = value
        xhat = moments(value)[0].astype(BF)
        out[0, 0] = xhat[:half]
        out[0, 1] = xhat[half:]
        cot_out[side, 0] = dot(order, cot[0]).astype(BF)


def join_kernel(place, first, second, out):
    here = first.shape[2]
    out[:, :, :here] = first[...]
    out[:, :, here:] = second[...]


def widen_kernel(place, first, second, stay, send):
    half = first.shape[2] // 2
    stay[...] = jnp.concatenate([first[:, :, :half], second[:, :, :half]], -1)
    send[...] = jnp.concatenate([first[:, :, half:], second[:, :, half:]], -1)


def narrow_kernel(place, first, second, stay, send):
    here = first.shape[2]
    columns = first.shape[-1] // 2
    for ref, part in ((first, slice(0, here)), (second, slice(here, 2 * here))):
        stay[:, :, part] = ref[..., :columns]
        send[:, :, part] = ref[..., columns:]


def fold_kernel(place, first, second, stay, send):
    half = first.shape[2] // 2
    total = (first[...].astype(F32) + second[...].astype(F32)).astype(BF)
    stay[...] = total[:, :, :half]
    send[...] = total[:, :, half:]


def z_fold_kernel(place, first, second, stay, send, total, *, bit):
    half = first.shape[0] // 2
    total[...] = (first[...].astype(F32) + second[...].astype(F32)).astype(BF)
    side = place[0] // 2 if bit else place[0] % 2
    stay[...] = total[pl.ds(pl.multiple_of(side * half, 32), half)]
    send[...] = total[pl.ds(pl.multiple_of((1 - side) * half, 32), half)]


def weights_out_kernel(place, first, second, fc1, fc2, out):
    total = first[...].astype(F32) + second[...].astype(F32)
    width = fc1.shape[1]
    rows = total.shape[0]
    fc1[...] = total[:, :width]
    out[...] = padded_turn(total[:, width:FIRST_COLUMNS])[: out.shape[0], :rows]
    fc2[...] = padded_turn(total[:, FIRST_COLUMNS:])[:, :rows]


def qkv_out_kernel(place, first, second, out):
    total = first[...].astype(F32) + second[...].astype(F32)
    for head in range(4):
        for part in range(3):
            at = (head * 3 + part) * HEAD_DIM
            out[:, part, head * HEAD_DIM : (head + 1) * HEAD_DIM] = total[:, at : at + HEAD_DIM]


def small_start_kernel(place, sums_a, sums_b, fc1_a, fc1_b, ln_sum, bias_sum, stay, send, last):
    width = sums_a.shape[1]
    common = [sums_a[index : index + 1] + sums_b[index : index + 1] for index in range(4)]
    common += [ln_sum[0:1], ln_sum[1:2]]
    slots = [fc1_a[slot, 0:1] + fc1_b[slot, 0:1] for slot in range(4)]
    stay[...] = rows_of((8, width), 0, common + slots[0:2])
    send[...] = rows_of((8, width), 0, common + slots[2:4])
    missing = width - bias_sum.shape[1]
    last[...] = jnp.concatenate([bias_sum[...], jnp.zeros((8, missing), F32)], 1)


def small_middle_kernel(place, first, second, stay, send):
    total = first[...] + second[...]
    row = lax.broadcasted_iota(jnp.int32, total.shape, 0)
    stay[...] = jnp.where(row == 7, 0.0, total)
    send[...] = jnp.where(row == 6, total[7:8], jnp.where(row == 7, 0.0, total))


def small_last_kernel(place, first, second, last, out):
    total = first[...] + second[...]
    row = lax.broadcasted_iota(jnp.int32, total.shape, 0)
    out[...] = jnp.where(row == 7, last[...], total)


def add_kernel(place, first, second, out):
    out[...] = first[...] + second[...]


def normed_of(xhat, gains):
    return (xhat.astype(F32) * gains[0:1] + gains[1:2]).astype(BF)


def qkv_kernel(place, first, second, weight, bias, gains, near, s0, s1, s2, s3):
    width = first.shape[2]
    for parity in range(2):
        for part, ref in enumerate((first, second)):
            made = dot_nt(weight[...], normed_of(ref[0, parity], gains)) + bias[...]
            made = made.astype(BF)
            for head in range(4):
                near[0, head, parity, :, part * width : (part + 1) * width] = made[
                    head * TRIPLE : (head + 1) * TRIPLE
                ]
    for slot, ref in enumerate((s0, s1, s2, s3)):
        head = place[0] ^ slot
        ref[0] = near[0, head, head & 1]


def near_forward_kernel(place, qkv, valid, out, key_aug, value_aug, stage, *, slide, factor):
    width = qkv.shape[-1]
    own = lax.rem(pl.program_id(0), 2)
    queries = []
    ones = rows_between((META, width), 0, 3).astype(BF)
    for role in range(2):
        parity = own if role == 0 else 1 - own
        block = qkv[0, 0, parity]
        there = valid[place[1] * 3 + slide, pl.ds(place[0] * 2 + parity, 1)]
        key_aug[role] = key_rows(block[48:96], near_key_meta(there)).T
        value_aug[role] = ones_below(block[96:144], 1)
        queries.append(query_rows(block[0:48], ones, factor))
    for role, used in ((0, (1,)), (1, (0, 1))):
        result, total = softmax_out(
            [lambda r=r: key_aug[r] for r in used],
            [lambda r=r: value_aug[r] for r in used],
            [queries[role]] * len(used),
            stage,
        )
        out[0, role] = jnp.concatenate([result, rows_of((8, width), 0, [total])], 0)


def far_forward_kernel(
    place, b0, b1, b2, b3, valid, o0, o1, o2, o3, key_aug, value_aug, q_same, q_other, stage, out,
    *, first_slide, half, factor,
):
    width = b0.shape[-1]
    slide = first_slide + pl.program_id(0)
    level = far_levels(place, width, half)
    tail = far_tables(level)
    same, other = far_queries(level)
    for slot, block in enumerate((b0, b1, b2, b3)):
        row = (place[0] ^ slot) * 2 + (place[0] & 1)
        there = valid[place[1] * 3 + slide, pl.ds(row, 1)]
        key_aug[slot] = key_rows(block[0, 48:96], (tail + bias_rows(there)).astype(BF)).T
        value_aug[slot] = ones_below(block[0, 96:144], 1)
        q_same[slot] = query_rows(block[0, 0:48], same, factor)
        q_other[slot] = query_rows(block[0, 0:48], other, factor)

    def step(slot, carry):
        places = [lax.rem(slot + shift, 4) for shift in range(4)]
        result, total = softmax_out(
            [lambda p=p: key_aug[p] for p in places],
            [lambda p=p: value_aug[p] for p in places],
            [q_same[slot], q_other[slot], q_other[slot], q_other[slot]],
            stage,
        )
        ending = rows_of((16, width), 0, [part.astype(F32) for part in split3(total)])
        out[slot] = jnp.concatenate([result, ending], 0).astype(BF)
        return carry

    lax.fori_loop(0, 4, step, 0)
    for slot, ref in enumerate((o0, o1, o2, o3)):
        ref[0] = out[slot]


def merge_kernel(place, *refs):
    count = refs[-2].shape[0]
    nears = refs[:count]
    f0, f1, f2, f3, kept, stay, send, far = refs[count:]
    width = kept.shape[-1]
    for slide, near in enumerate(nears):
        for slot, ref in enumerate((f0, f1, f2, f3)):
            far[place[0] ^ slot] = ref[slide]
        by_parity = [[], []]
        for head in range(4):
            own = head & 1
            there = far[head]
            far_total = joined(there[48:51])
            near_total = near[head, 0, 48:49]
            top = jnp.maximum(far_total, near_total)
            total = top + jnp.log2(jnp.exp2(far_total - top) + jnp.exp2(near_total - top))
            both = there[0:48].astype(F32) * jnp.exp2(far_total - total) + near[
                head, 0, 0:48
            ] * jnp.exp2(near_total - total)
            kept[slide, head, own] = jnp.concatenate([both, rows_of((8, width), 0, [total])], 0)
            kept[slide, head, 1 - own] = near[head, 1]
            by_parity[own].append(both)
            by_parity[1 - own].append(near[head, 1, 0:48])
        for parity in range(2):
            turned = padded_turn(jnp.concatenate(by_parity[parity], 0))[:, 0:192].astype(BF)
            for block in range(4):
                rows = slice(block * width // 8, (block + 1) * width // 8)
                stay[slide, parity, block] = turned[rows]
                rows = slice((block + 4) * width // 8, (block + 5) * width // 8)
                send[slide, parity, block] = turned[rows]


def gradient_rows_kernel(place, first, second, kept, *refs):
    near, s0, s1, s2, s3 = refs[-5:]
    half = first.shape[2]
    width = kept.shape[-1]
    for parity in range(2):
        turned = jnp.concatenate(
            [
                jnp.concatenate([ref[0, parity], jnp.zeros((half, 64), BF)], 1).T
                for ref in (first, second)
            ],
            1,
        )
        for head in range(4):
            part = turned[head * 48 : (head + 1) * 48]
            inner = jnp.sum(part.astype(F32) * kept[0, head, parity, 0:48], axis=0, keepdims=True)
            total = kept[0, head, parity, 48:49]
            rows = [piece.astype(F32) for piece in split3(total) + split3(inner)]
            ending = rows_of((16, width), 0, rows).astype(BF)
            near[0, head, parity] = jnp.concatenate([part, ending], 0)
    for slot, ref in enumerate((s0, s1, s2, s3)):
        head = place[0] ^ slot
        ref[0] = near[0, head, head & 1]


def negated_total(grad_block, base):
    tail = grad_block[48:64].astype(F32)
    row = lax.broadcasted_iota(jnp.int32, base.shape, 0)
    out = base.astype(F32)
    for index in range(3):
        out = jnp.where(row == 15 + index, -tail[index : index + 1], out)
    return out.astype(BF)


def gradient_aug(grad_block):
    width = grad_block.shape[-1]
    tail = grad_block[48:64].astype(F32)
    rows = rows_of((16, width), 0, [-tail[index : index + 1] for index in (3, 4, 5)])
    return jnp.concatenate([grad_block[0:48], rows.astype(BF)], 0)


def pair_block(key_aug, value_aug, queries, grads):
    probs = jnp.exp2(dot(key_aug, queries))
    slopes = (probs * dot(value_aug, grads)).astype(BF)
    return probs.astype(BF), slopes


def near_backward_kernel(
    place, qkv, valid, grad, out, key_aug, key_t, value_aug, q_aug, g_aug, q_nat, g_nat,
    *, slide, factor, scale,
):
    width = qkv.shape[-1]
    own = lax.rem(pl.program_id(0), 2)
    ones = rows_between((META, width), 0, 3)
    for role in range(2):
        parity = own if role == 0 else 1 - own
        block = qkv[0, 0, parity]
        given = grad[0, 0, parity]
        there = valid[place[1] * 3 + slide, pl.ds(place[0] * 2 + parity, 1)]
        key_aug[role] = key_rows(block[48:96], near_key_meta(there)).T
        key_t[role] = plain64(block[48:96])
        value_aug[role] = padded_turn(ones_below(block[96:144], 3))[:, 0:64]
        q_aug[role] = query_rows(block[0:48], negated_total(given, ones), factor)
        g_aug[role] = gradient_aug(given)
        q_nat[role] = padded_turn(plain64(block[0:48]))[:, 0:64]
        g_nat[role] = padded_turn(plain64(given[0:48]))[:, 0:64]
    dq = [None, None]
    for key_role, users in ((0, (1,)), (1, (0, 1))):
        dk = None
        dv = None
        for role in users:
            probs, slopes = pair_block(
                key_aug[key_role], value_aug[key_role], q_aug[role], g_aug[role]
            )
            add_v = dot(probs, g_nat[role])
            add_k = dot(slopes, q_nat[role])
            add_q = dot(key_t[key_role], slopes)
            dv = add_v if dv is None else dv + add_v
            dk = add_k if dk is None else dk + add_k
            dq[role] = add_q if dq[role] is None else dq[role] + add_q
        parity = own if key_role == 0 else 1 - own
        out[0, parity, 48:96] = (turned_out(dk) * scale).astype(BF)
        out[0, parity, 96:144] = turned_out(dv).astype(BF)
    for role in range(2):
        parity = own if role == 0 else 1 - own
        out[0, parity, 0:48] = (dq[role][0:48] * scale).astype(BF)


def far_backward_kernel(
    place, b0, b1, b2, b3, g0, g1, g2, g3, valid, o0, o1, o2, o3,
    key_aug, key_t, value_aug, q_same, q_other, g_aug, q_nat, g_nat, dq, out,
    *, first_slide, half, factor, scale,
):
    width = b0.shape[-1]
    slide = first_slide + pl.program_id(0)
    level = far_levels(place, width, half)
    tail = far_tables(level)
    same, other = far_queries(level)
    for slot, (block, given) in enumerate(((b0, g0), (b1, g1), (b2, g2), (b3, g3))):
        grad = given[0]
        row = (place[0] ^ slot) * 2 + (place[0] & 1)
        there = valid[place[1] * 3 + slide, pl.ds(row, 1)]
        key_aug[slot] = key_rows(block[0, 48:96], (tail + bias_rows(there)).astype(BF)).T
        key_t[slot] = plain64(block[0, 48:96])
        value_aug[slot] = padded_turn(ones_below(block[0, 96:144], 3))[:, 0:64]
        q_same[slot] = query_rows(block[0, 0:48], negated_total(grad, same), factor)
        q_other[slot] = query_rows(block[0, 0:48], negated_total(grad, other), factor)
        g_aug[slot] = gradient_aug(grad)
        q_nat[slot] = padded_turn(plain64(block[0, 0:48]))[:, 0:64]
        g_nat[slot] = padded_turn(plain64(grad[0:48]))[:, 0:64]
    dq[...] = jnp.zeros_like(dq)

    def step(slot, carry):
        dk = None
        dv = None
        for shift in range(4):
            there = lax.rem(slot + shift, 4)
            queries = q_same[there] if shift == 0 else q_other[there]
            probs, slopes = pair_block(key_aug[slot], value_aug[slot], queries, g_aug[there])
            add_v = dot(probs, g_nat[there])
            add_k = dot(slopes, q_nat[there])
            dv = add_v if dv is None else dv + add_v
            dk = add_k if dk is None else dk + add_k
            dq[there] += dot(key_t[slot], slopes)
        out[slot, 48:96] = (turned_out(dk) * scale).astype(BF)
        out[slot, 96:144] = turned_out(dv).astype(BF)
        return carry

    lax.fori_loop(0, 4, step, 0)
    for slot, ref in enumerate((o0, o1, o2, o3)):
        ref[0] = out[slot]
        ref[0, 0:48] = (dq[slot, 0:48] * scale).astype(BF)


def qkv_backward_kernel(place, *refs, count, begins, ends):
    refs = list(refs)
    nears = [refs.pop(0) for _ in range(count)]
    f0, f1, f2, f3, first, second, weight, gains = [refs.pop(0) for _ in range(8)]
    before = [] if begins else [refs.pop(0) for _ in range(3)]
    wgrads = [refs.pop(0) for _ in range(2 if ends else 1)]
    bias_sum, ln_sum, stay, send, far = refs[:5]
    acc = refs[5] if ends else wgrads[0]
    if begins:
        for ref in (acc, bias_sum, ln_sum):
            ref[...] = jnp.zeros_like(ref)
    else:
        for ref, old in zip((acc, bias_sum, ln_sum), before):
            ref[...] = old[...]
    half = first.shape[2]
    piece_rows = half // 4
    gain_row = jnp.zeros((1, gains.shape[1]), F32)
    bias_row = jnp.zeros((1, gains.shape[1]), F32)
    ones = jnp.ones((8, 2 * half), BF)
    for slide, near in enumerate(nears):
        for slot, ref in enumerate((f0, f1, f2, f3)):
            far[place[0] ^ slot] = ref[slide]
        for parity in range(2):
            pieces = []
            for head in range(4):
                piece = near[head, parity]
                if head & 1 == parity:
                    piece = (piece.astype(F32) + far[head].astype(F32)).astype(BF)
                pieces.append(piece)
            total = jnp.concatenate(pieces, 0)
            bias_sum[...] += dot_nt(ones, total)
            turned = padded_turn(total)[:, 0 : total.shape[0]]
            for part, ref, out in ((0, first, stay), (1, second, send)):
                xhat = ref[slide, parity]
                here = slice(part * half, (part + 1) * half)
                acc[...] += dot(total[:, here], normed_of(xhat, gains))
                back = dot(turned[here], weight[...])
                low = back.astype(BF)
                for block in range(4):
                    out[slide, parity, block] = low[block * piece_rows : (block + 1) * piece_rows]
                gain_row = gain_row + jnp.sum(back * xhat.astype(F32), axis=0, keepdims=True)
                bias_row = bias_row + jnp.sum(back, axis=0, keepdims=True)
    ln_sum[...] += rows_of(ln_sum.shape, 0, [gain_row, bias_row])
    if ends:
        missing = wgrads[0].shape[1] - acc.shape[0]
        full = jnp.concatenate([acc[...], jnp.zeros((missing, acc.shape[1]), F32)], 0)
        turned = full.T.astype(BF)
        rows = turned.shape[0] // 8
        for index in range(8):
            part = turned[index * rows : (index + 1) * rows]
            where = slice(index // 2 * rows, (index // 2 + 1) * rows)

            @pl.when(place[1] == index % 2)
            def _():
                wgrads[0][where] = part

            @pl.when(place[1] != index % 2)
            def _():
                wgrads[1][where] = part


def exit_kernel(place, first, second, base, grad_mid, out_rows, gains, *refs):
    tiles_grad, output = refs[-2:]
    rows = base.shape[2]
    half = rows // 2
    xhat, rate = moments(base[0, 0])
    side = pl.program_id(0)
    upstream = jnp.concatenate(
        [jnp.where(side == 0, first[0, part], second[0, part]) for part in range(2)], 0
    ).astype(F32)
    grad = grad_mid[0, 0] + norm_back(xhat, rate, gains[0:1], upstream)
    undo = parity_order(rows, True)
    tiles_grad[0] = dot(undo, grad.astype(BF)).astype(BF)
    output[0] = dot(undo, out_rows[0, 0]).astype(BF)


def mlp_kernel(
    place, base, own, other, cot, w1, w2, wo0, wo1, wo2, wo3, offset, small,
    output, grad_mid, grad_own, grad_other, hidden_out, g_pre_out, normed_t, cot_t, attn_t,
    merged_out, sums, fc1_sum,
    w_out, mid, merged, normed, ff, back,
):
    step = pl.program_id(0)
    rows, width = mid.shape
    part = 256
    half = part // 4

    def cot_at(first):
        slide = first // part
        return jnp.concatenate([cot[0, slide], cot[1, slide]], 0)

    @pl.when(step == 0)
    def _():
        for index, ref in enumerate((wo0, wo1, wo2, wo3)):
            w_out[index * 192 : (index + 1) * 192] = ref[0]
        for first in range(0, rows, part):
            here = pl.ds(first, part)
            slide = first // part
            for side, ref in enumerate((own, other)):
                for parity in range(2):
                    at = first + (2 * side + parity) * half
                    merged[at : at + half] = ref[slide, parity]
            value = jnp.concatenate([base[0, slide], base[1, slide]], 0)
            value = value + (dot(merged[here], w_out[...]) + small[0:1])
            mid[here] = value
            xhat, _ = moments(value)
            low = (xhat * small[1:2] + small[2:3]).astype(BF)
            normed[here] = low
            normed_t[:, first : first + part] = low.T
            cot_t[:, first : first + part] = cot_at(first).T
        for index, slot in enumerate(SLOT_ORDER):
            merged_out[slot] = merged[:, index * 192 : (index + 1) * 192]

    shift = joined(offset[0, 0:3])
    fc1 = jnp.zeros((1, width), F32)
    for first in range(0, rows, part):
        here = pl.ds(first, part)
        pre = dot(normed[here], w1[0]) + shift
        cdf = 0.5 * (1.0 + lax.erf(pre * math.sqrt(0.5)))
        hidden = (pre * cdf).astype(BF)
        slope = cdf + pre * (jnp.exp(-0.5 * pre * pre) * (1.0 / math.sqrt(2.0 * math.pi)))
        g_pre = (dot_nt(cot_at(first), w2[0]) * slope).astype(BF)
        hidden_out[0, here] = hidden
        g_pre_out[0, here] = g_pre
        add_ff = dot(hidden, w2[0])
        add_back = dot_nt(g_pre, w1[0])

        @pl.when(step == 0)
        def _():
            ff[here] = add_ff
            back[here] = add_back

        @pl.when(step != 0)
        def _():
            ff[here] += add_ff
            back[here] += add_back

        fc1 = fc1 + jnp.sum(g_pre.astype(F32), axis=0, keepdims=True)
    fc1_sum[0] = jnp.broadcast_to(fc1, (8, width))

    @pl.when(step == pl.num_programs(0) - 1)
    def _():
        totals = [jnp.zeros((1, width), F32)] * 4
        for first in range(0, rows, part):
            here = pl.ds(first, part)
            slide = first // part
            value = mid[here]
            result = (value + (ff[here] + small[3:4])).astype(BF)
            xhat, rate = moments(value)
            upstream = back[here]
            cot_wide = cot_at(first).astype(F32)
            grad = cot_wide + norm_back(xhat, rate, small[1:2], upstream)
            low = grad.astype(BF)
            back_rows = dot_nt(low, w_out[...]).astype(BF)
            for side, ref in enumerate((grad_own, grad_other)):
                output[side, slide] = result[2 * side * half : 2 * (side + 1) * half]
                grad_mid[side, slide] = grad[2 * side * half : 2 * (side + 1) * half]
                for parity in range(2):
                    at = (2 * side + parity) * half
                    ref[slide, parity, 0] = back_rows[at : at + half]
            attn_t[:, first : first + part] = low.T
            wide = low.astype(F32)
            for index, piece in enumerate((wide, upstream * xhat, upstream, cot_wide)):
                totals[index] = totals[index] + jnp.sum(piece, axis=0, keepdims=True)
        sums[...] = rows_of((8, width), 0, totals)


def weight_grad_kernel(place, *refs, partner):
    groups = [refs[0:6], refs[6:12]]
    outs = refs[12 + 2 * partner :]
    width = refs[0].shape[0]
    piece = width // 8
    slot = pl.program_id(0)

    def rows(index):
        return slice(index // 2 * piece, (index // 2 + 1) * piece)

    def over(index, other):
        return sum(dot(group[index][...], group[other][0]) for group in groups)

    second = over(1, 4)
    for index in range(8):
        side = (index % 2) ^ place[1]
        part = second[index * piece : (index + 1) * piece]
        if not partner:
            outs[1][0, side, rows(index)] = part.astype(BF)
            continue
        part = (part + refs[13][0, side, rows(index)].astype(F32)).astype(BF)
        for here, ref in enumerate(outs[2:]):

            @pl.when(slot == here)
            def _():
                ref[side, rows(index)] = part

    rest = over(2, 5)
    missing = FIRST_COLUMNS - width - rest.shape[1]
    rest = jnp.concatenate([rest, jnp.zeros((width, missing), F32)], 1)
    for first, value in ((0, over(0, 3)), (width, rest)):
        columns = slice(first, first + value.shape[1])
        for index in range(8):
            part = value[index * piece : (index + 1) * piece]
            if not partner:
                outs[0][(index % 2) ^ place[1], 0, rows(index), columns] = part.astype(BF)
                continue
            for side, ref in enumerate(outs[:2]):

                @pl.when((index % 2) ^ place[1] == side)
                def _():
                    there = part + refs[12][side, 0, rows(index), columns].astype(F32)
                    ref[0, rows(index), columns] = there.astype(BF)


def side_fold_kernel(place, first, second, stay, send):
    total = (first[...].astype(F32) + second[...].astype(F32)).astype(BF)
    stay[...] = total[0]
    send[...] = total[1]


def z_fold_both_kernel(place, first, second, third, fourth, stay, send, total):
    columns = first.shape[1]
    half = first.shape[0] // 2
    total[:, :columns] = (first[...].astype(F32) + second[...].astype(F32)).astype(BF)
    total[:, columns:] = (third[...].astype(F32) + fourth[...].astype(F32)).astype(BF)
    side = place[0] // 2
    stay[...] = total[pl.ds(pl.multiple_of(side * half, 32), half)]
    send[...] = total[pl.ds(pl.multiple_of((1 - side) * half, 32), half)]


def hold_kernel(place, w1, w2, wo, offset, out):
    width = w1.shape[1]
    out[0:width] = w1[...]
    out[width : 2 * width] = w2[...]
    out[2 * width : 2 * width + wo.shape[0]] = wo[...]
    rows = [part.astype(F32) for part in split3(offset[...])]
    out[2 * width + wo.shape[0] :] = rows_of((16, width), 0, rows).astype(BF)


def whole(shape):
    return pl.BlockSpec(tuple(shape), lambda *_: (0,) * len(shape))


def shaped(shape, dtype):
    return jax.ShapeDtypeStruct(tuple(shape), dtype)


def run(name, body, place, ins, outs, grid=(1,), scratch=(), tokens=(), aliases=None, mib=48, us=5):
    arrays = [pair[0] for pair in ins]
    in_specs = [whole(a.shape) if s is None else s for a, s in ins]
    in_specs += [pl.BlockSpec(memory_space=pl.ANY)] * len(tokens)
    out_specs = [whole(o.shape) if s is None else s for o, s in outs]
    given, extra = len(ins), len(tokens)

    def kernel(place_ref, *refs):
        body(place_ref, *refs[:given], *refs[given + extra :])

    return pl.pallas_call(
        kernel,
        grid_spec=pltpu.PrefetchScalarGridSpec(
            num_scalar_prefetch=1,
            grid=grid,
            in_specs=in_specs,
            out_specs=out_specs,
            scratch_shapes=list(scratch),
        ),
        out_shape=[o for o, _ in outs],
        input_output_aliases={k + 1: v for k, v in (aliases or {}).items()},
        compiler_params=pltpu.CompilerParams(vmem_limit_bytes=mib * 1024 * 1024),
        cost_estimate=pl.CostEstimate(
            flops=int(COST * us * 1.1e9), transcendentals=0, bytes_accessed=int(COST * us * 3.6e6)
        ),
        name=name,
    )(place, *arrays, *tokens)


def swap(value, axis, bit):
    return lax.ppermute(value, axis, [(i, i ^ bit) for i in range(lax.axis_size(axis))])


def paired(body, given):
    def kernel(place, *refs):
        near, away = refs[given : given + 2]
        slots = (near.at[0], near.at[1], away.at[0], away.at[1])
        body(place, *refs[:given], *slots, *refs[given + 2 :])

    return kernel


def pair_kernel(place, near, away, out):
    out[0] = near[1]
    out[1] = away[1]


def nested(
    tiles,
    coords,
    lengths,
    padding_mask,
    ln1_gain,
    ln1_bias,
    query_key_value_weight,
    qv_bias,
    attention_output_weight,
    attention_output_bias,
    ln2_gain,
    ln2_bias,
    mlp_entry_matrix,
    mlp_entry_offset,
    feed_output_weight,
    feed_output_bias,
    cotangent,
):
    slides, rows, width = tiles.shape
    group = slides // 2
    half = rows // 2
    lanes = 8 * half
    mine = lanes // 2
    local = query_key_value_weight.shape[2]
    scale = 1.0 / math.sqrt(HEAD_DIM)
    factor = scale * LOG2E
    seq_index = lax.axis_index("seq")
    head_index = lax.axis_index("head")
    z, y = seq_index // 2, seq_index % 2
    x, core = head_index // 2, head_index % 2
    place = jnp.stack([z, y, x, core]).astype(jnp.int32)
    parts = ((0, 1), (1, group - 1))
    token = []

    def step(name, body, ins, outs, **options):
        made = run(name, body, place, ins, outs, tokens=list(token), **options)
        token[:] = [made[-1]]
        return made

    def vm(*shape, dtype=BF):
        return pltpu.VMEM(shape, dtype)

    def bf(*shape):
        return shaped(shape, BF)

    def f32(*shape):
        return shaped(shape, F32)

    def plain(*arrays):
        return [(array, None) for array in arrays]

    def lead_block(*shape):
        return pl.BlockSpec((1,) + shape, lambda k, p: (k,) + (0,) * len(shape))

    def over_z(pieces):
        return [(pieces[0], None)] + [(swap(pieces[k], "seq", 2 * k), None) for k in (1, 2, 3)]

    def over_z_first(pair):
        return pair[0], swap(pair[1], "seq", 4)

    def over_z_second(pair):
        near, away = pair
        send = step("pair", pair_kernel, plain(near, away), [(shaped(near.shape, BF), None)], us=0.5)[0]
        got = swap(send, "seq", 2)
        return [(near, 0), (got, 0), (away, 0), (got, 1)]

    def by_slide(slots):
        out = []
        for array, index in slots:
            shape = array.shape[-2:]
            if index is None:
                out.append((array, lead_block(*shape)))
            else:
                out.append((array, pl.BlockSpec((None, 1) + shape, lambda k, p, i=index: (i, k, 0, 0))))
        return out

    def all_slides(slots):
        out = []
        for array, index in slots:
            if index is None:
                out.append((array, None))
            else:
                shape = array.shape[1:]
                out.append((array, pl.BlockSpec((None,) + shape, lambda k, p, i=index: (i, 0, 0, 0))))
        return out

    total_len = padding_mask.shape[1]
    positions = jnp.arange(total_len, dtype=jnp.int32)
    valid = (positions[None, :] < lengths[:, None]) & (padding_mask == 1)
    valid = valid.astype(BF).reshape(slides * 4, total_len // 4)
    spot = jnp.arange(total_len // 4, dtype=jnp.int32)
    lane = spot % lanes
    chip = lane // half
    there = (
        (y ^ (chip & 1)) * lanes
        + (x ^ ((chip >> 1) & 1)) * (lanes // 2)
        + (core ^ (chip >> 2)) * rows
        + 2 * (lane % half)
        + spot // lanes
    )
    taken = (spot[:, None] == there[None, :]).astype(BF)
    valid = jnp.einsum("rp,pl->rl", valid, taken, preferred_element_type=F32)
    valid = valid.reshape(slides, 8, lanes)

    weight = query_key_value_weight.reshape(width, 3, 4, HEAD_DIM).transpose(2, 1, 3, 0)
    weight = weight.reshape(3 * local, width)
    triple = jnp.stack([qv_bias[0], jnp.zeros_like(qv_bias[0]), qv_bias[1]])
    triple = triple.reshape(3, 4, HEAD_DIM).transpose(1, 0, 2).reshape(3 * local, 1)
    gains = jnp.concatenate([jnp.stack([ln1_gain, ln1_bias]), jnp.zeros((6, width), F32)], 0)
    small = jnp.concatenate(
        [
            jnp.stack([attention_output_bias, ln2_gain, ln2_bias, feed_output_bias]),
            jnp.zeros((4, width), F32),
        ],
        0,
    )
    quarter = width // 4
    freq = jnp.exp(-jnp.log(10000.0) * jnp.arange(quarter, dtype=F32) / quarter)
    angle = jnp.arange(256, dtype=F32)[:, None] * freq
    table = jnp.stack(split3(jnp.concatenate([jnp.sin(angle), jnp.cos(angle)], axis=-1)))

    bases, cots, blocks = [], [], []
    pending = []
    for first, count in parts:

        def at_side(side, depth, first=first):
            return pl.BlockSpec(
                (1, rows, depth), lambda k, p: ((p[1] ^ side) * group + first + k, 0, 0)
            )

        both = pl.BlockSpec((2, 1, rows, width), lambda k, p: (0, k, 0, 0))
        piece = pl.BlockSpec((1, 2, half, width), lambda k, p: (k, 0, 0, 0))
        pair = (2, count, rows, width)
        ins = []
        for array, depth in ((tiles, width), (coords, 2), (cotangent, width)):
            ins += [(array, at_side(0, depth)), (array, at_side(1, depth))]
        base, cot, own, other = step(
            "entry",
            entry_kernel,
            ins + plain(table),
            [
                (f32(*pair), both),
                (bf(*pair), both),
                (bf(count, 2, half, width), piece),
                (bf(count, 2, half, width), piece),
            ],
            grid=(count,),
            us=2.2 * count,
        )
        bases.append(base)
        cots.append(cot)
        shape = (count, 2, 1, half, width)
        pending.append((own.reshape(shape), swap(other, "seq", 1).reshape(shape)))

    def join(first, second):
        shape = first.shape[:2] + (2 * first.shape[2],) + first.shape[3:]
        return step("join", join_kernel, plain(first, second), [(shaped(shape, BF), None)], us=1)[0]

    pending = [join(*pair) for pair in pending]
    pending = [(block, swap(block, "head", 2)) for block in pending]

    qkvs, far_blocks = [None, None], [None, None]
    near_outs, near_grads = [None] * group, [None] * group

    def project(g):
        first, count = parts[g]
        outs = step(
            "qkv",
            qkv_kernel,
            [(blocks[g][0], lead_block(2, mine, width)), (blocks[g][1], lead_block(2, mine, width))]
            + plain(weight, triple, gains),
            [(bf(count, 4, 2, TRIPLE, lanes), lead_block(4, 2, TRIPLE, lanes))]
            + [(bf(count, TRIPLE, lanes), lead_block(TRIPLE, lanes))] * 4,
            grid=(count,),
            us=2.2 * count,
        )
        qkvs[g] = outs[0]
        far_blocks[g] = over_z(outs[1:])

    def spread_columns(g):
        block = join(*pending[g])
        shape = (parts[g][1], 2, mine, width)
        blocks.append((block.reshape(shape), swap(block, "head", 1).reshape(shape)))

    def head_block(k, height):
        return pl.BlockSpec((1, 1, 2, height, lanes), lambda i, p: (k, i, 0, 0, 0))

    def each_head(height):
        return pl.BlockSpec((1, 2, height, lanes), lambda i, p: (i, 0, 0, 0))

    def near_forward(g, k):
        slide = parts[g][0] + k
        near_outs[slide] = step(
            "near_forward",
            partial(near_forward_kernel, slide=slide, factor=factor),
            [(qkvs[g], head_block(k, TRIPLE)), (valid, None)],
            [(f32(4, 2, ACC_ROWS, lanes), each_head(ACC_ROWS))],
            grid=(4,),
            scratch=[vm(2, lanes, AUG), vm(2, OUT_ROWS, lanes), vm(2, lanes, lanes, dtype=F32)],
            us=6.6,
        )[0]

    far_outs, kept, merged = [None, None], [None, None], [None, None]

    def far_kernel(name, body, g, ins, height, scratch, two_steps, us, **options):
        first, count = parts[g]
        body = partial(body, first_slide=first, half=half, factor=factor, **options)
        if two_steps:
            body = paired(body, len(ins))
            block = pl.BlockSpec((2, 1, height, lanes), lambda k, p: (0, k, 0, 0))
            outs = [(bf(2, count, height, lanes), block)] * 2
        else:
            outs = [(bf(count, height, lanes), lead_block(height, lanes))] * 4
        outs = step(name, body, ins, outs, grid=(count,), scratch=scratch, us=us * count)
        return over_z_first(outs) if two_steps else over_z(outs)

    def far_forward(g, two_steps):
        far_outs[g] = far_kernel(
            "far_forward",
            far_forward_kernel,
            g,
            by_slide(far_blocks[g]) + plain(valid),
            OUT_ROWS,
            [
                vm(4, lanes, AUG),
                vm(4, OUT_ROWS, lanes),
                vm(4, AUG, lanes),
                vm(4, AUG, lanes),
                vm(4, lanes, lanes, dtype=F32),
                vm(4, OUT_ROWS, lanes),
            ],
            two_steps,
            8,
        )

    def merge(g):
        first, count = parts[g]
        turned = bf(count, 2, 4, half, local)
        kept[g], stay, send = step(
            "merge",
            merge_kernel,
            plain(*near_outs[first : first + count]) + all_slides(far_outs[g]),
            [(f32(count, 4, 2, ACC_ROWS, lanes), None), (turned, None), (turned, None)],
            scratch=[vm(4, OUT_ROWS, lanes)],
            us=count,
        )
        merged[g] = (stay, swap(send, "head", 1))

    def widen(g, axis, bit):
        pieces = [(a, None) for a in merged[g]]
        count, _, blocks_here, _, columns = merged[g][0].shape
        shape = bf(count, 2, blocks_here // 2, half, 2 * columns)
        stay, send = step("widen", widen_kernel, pieces, [(shape, None)] * 2, us=1)
        merged[g] = (stay, swap(send, axis, bit))

    spread_columns(0)
    project(0)
    near_forward(0, 0)
    spread_columns(1)
    packed = step(
        "hold",
        hold_kernel,
        plain(
            mlp_entry_matrix,
            feed_output_weight,
            attention_output_weight,
            mlp_entry_offset[None],
        ),
        [(bf(2 * width + local + 16, width), None)],
        us=2,
    )[0]
    packed = lax.all_gather(packed, "head")
    project(1)
    far_forward(0, True)
    near_forward(1, 0)
    far_outs[0] = over_z_second(far_outs[0])
    near_forward(1, 1)
    merge(0)
    far_forward(1, False)
    widen(0, "head", 2)

    def last_widen(g):
        first, second = merged[g]
        count = first.shape[0]
        shape = bf(count, 2, 1, half, width)
        stay, send = step("widen", widen_kernel, plain(first, second), [(shape, None)] * 2, us=1)
        shape = (count, 2, half, width)
        merged[g] = (stay.reshape(shape), swap(send, "seq", 1).reshape(shape))

    last_widen(0)
    merge(1)
    widen(1, "head", 2)

    def head_of(i, p):
        return (p[2] ^ (i % 2)) * 2 + (p[3] ^ (i // 2))

    def weight_spec(height, index, slot=None):
        if slot is None:
            return pl.BlockSpec((1, height, width), lambda i, p: (head_of(i, p), index, 0))
        return pl.BlockSpec((1, height, width), lambda i, p: (head_of(slot, p), index, 0))

    def slot_block(*shape):
        return pl.BlockSpec((1,) + shape, lambda i, p: (i,) + (0,) * len(shape))

    owned, given, grads = [None, None], [None, None], [None, None]

    def feed_forward(g):
        count = parts[g][1]
        here = 2 * count * rows
        pair = (2, count, rows, width)
        turned = bf(width, here)
        piece = bf(count, 2, 1, half, width)
        outs = step(
            "mlp",
            mlp_kernel,
            plain(bases[g], *merged[g], cots[g])
            + [(packed, weight_spec(width, 0)), (packed, weight_spec(width, 1))]
            + [(packed, weight_spec(local, 2 * width // local, slot)) for slot in SLOT_ORDER]
            + [(packed, weight_spec(16, (2 * width + local) // 16)), (small, None)],
            [
                (bf(*pair), None),
                (f32(*pair), None),
                (piece, None),
                (piece, None),
                (bf(4, here, width), slot_block(here, width)),
                (bf(4, here, width), slot_block(here, width)),
                (turned, None),
                (turned, None),
                (turned, None),
                (bf(4, here, local), None),
                (f32(8, width), None),
                (f32(4, 8, width), slot_block(8, width)),
            ],
            grid=(4,),
            scratch=[
                vm(width, width),
                vm(here, width, dtype=F32),
                vm(here, width),
                vm(here, width),
                vm(here, width, dtype=F32),
                vm(here, width, dtype=F32),
            ],
            mib=60,
            us=5 + 10 * count,
        )
        output, grad_mid, own, other, hidden, g_pre, normed_t, cot_t, attn_t, slots, sums, fc1 = outs
        owned[g] = (output, grad_mid, sums, fc1)
        grads[g] = (normed_t, cot_t, attn_t, g_pre, hidden, slots)
        given[g] = (own, swap(other, "seq", 1))

    def narrow(g, axis, bit):
        first, second = given[g]
        count, _, blocks_here, _, columns = first.shape
        shape = bf(count, 2, 2 * blocks_here, half, columns // 2)
        stay, send = step("narrow", narrow_kernel, plain(first, second), [(shape, None)] * 2, us=1)
        given[g] = (stay, swap(send, axis, bit))

    feed_forward(0)
    last_widen(1)
    feed_forward(1)

    tall = width // 2
    sent = [
        (bf(2, 2, tall, FIRST_COLUMNS), pl.BlockSpec((2, 1, tall, FIRST_COLUMNS), lambda i, p: (0, i, 0, 0))),
        (bf(2, 2, tall, width), pl.BlockSpec((1, 2, tall, width), lambda i, p: (i, 0, 0, 0))),
    ]
    kept_w = [(bf(2, tall, FIRST_COLUMNS), slot_block(tall, FIRST_COLUMNS))] * 2
    kept_w += [(bf(2, tall, width), None)] * 2

    def weight_grads(first, partner):
        def at(*shape):
            return pl.BlockSpec((1,) + shape, lambda i, p: (i + first, 0, 0))

        ins = []
        for (_, count), (normed_t, cot_t, attn_t, g_pre, hidden, slots) in zip(parts, grads):
            here = 2 * count * rows
            ins += plain(normed_t, cot_t, attn_t)
            ins += [(g_pre, at(here, width)), (hidden, at(here, width)), (slots, at(here, local))]
        return step(
            "weight_grads",
            partial(weight_grad_kernel, partner=len(partner) // 2),
            ins + [(value, spec) for value, (_, spec) in zip(partner, sent)],
            kept_w if partner else sent,
            grid=(2,),
            mib=56,
            us=12,
        )

    def split_fold(pair, axis, bit):
        shape = pair[0].shape[1:]
        stay, send = step(
            "split_fold", side_fold_kernel, plain(*pair), [(shaped(shape, BF), None)] * 2, us=2
        )
        return stay, swap(send, axis, bit)

    grad_rows, far_grads, far_backs = [None, None], [None, None], [None, None]
    backs, sums_so_far = [None, None], []

    def rows_of_gradients(g):
        first, count = parts[g]
        pieces = [value.reshape(count, 2, mine, local) for value in given[g]]
        slot = pl.BlockSpec((1, OUT_ROWS, lanes), lambda k, p: (first + k, 0, 0))
        any_spec = pl.BlockSpec(memory_space=pl.ANY)
        before = [(array, any_spec) for array in far_grads[0] or []]
        outs = step(
            "gradient_rows",
            gradient_rows_kernel,
            [(value, lead_block(2, mine, local)) for value in pieces]
            + [(kept[g], lead_block(4, 2, ACC_ROWS, lanes))]
            + before,
            [(bf(count, 4, 2, OUT_ROWS, lanes), lead_block(4, 2, OUT_ROWS, lanes))]
            + [(bf(group, OUT_ROWS, lanes), slot)] * 4,
            grid=(count,),
            aliases={3 + k: 1 + k for k in range(4)} if before else None,
            us=count,
        )
        grad_rows[g] = outs[0]
        far_grads[0] = outs[1:] if first == 0 else over_z(outs[1:])

    def near_backward(g, k):
        slide = parts[g][0] + k
        near_grads[slide] = step(
            "near_backward",
            partial(near_backward_kernel, slide=slide, factor=factor, scale=scale),
            [(qkvs[g], head_block(k, TRIPLE)), (valid, None), (grad_rows[g], head_block(k, OUT_ROWS))],
            [(bf(4, 2, TRIPLE, lanes), each_head(TRIPLE))],
            grid=(4,),
            scratch=[
                vm(2, lanes, AUG),
                vm(2, OUT_ROWS, lanes),
                vm(2, lanes, OUT_ROWS),
                vm(2, AUG, lanes),
                vm(2, OUT_ROWS, lanes),
                vm(2, lanes, OUT_ROWS),
                vm(2, lanes, OUT_ROWS),
            ],
            us=9.7,
        )[0]

    def far_backward(g, two_steps):
        first = parts[g][0]
        grads_here = [
            (array, pl.BlockSpec((1, OUT_ROWS, lanes), lambda k, p: (first + k, 0, 0)))
            for array, _ in far_grads[0]
        ]
        far_backs[g] = far_kernel(
            "far_backward",
            far_backward_kernel,
            g,
            by_slide(far_blocks[g]) + grads_here + plain(valid),
            TRIPLE,
            [
                vm(4, lanes, AUG),
                vm(4, OUT_ROWS, lanes),
                vm(4, lanes, OUT_ROWS),
                vm(4, AUG, lanes),
                vm(4, AUG, lanes),
                vm(4, OUT_ROWS, lanes),
                vm(4, lanes, OUT_ROWS),
                vm(4, lanes, OUT_ROWS),
                vm(4, OUT_ROWS, lanes, dtype=F32),
                vm(4, TRIPLE, lanes),
            ],
            two_steps,
            12,
            scale=scale,
        )

    def project_back(g, ends):
        first, count = parts[g]
        begins = not ends
        if ends:
            wgrads = [(bf(width // 2, 3 * local + 64), None)] * 2
        else:
            wgrads = [(f32(3 * local, width), None)]
        back = bf(count, 2, 4, half, width)
        outs = step(
            "qkv_backward",
            partial(qkv_backward_kernel, count=count, begins=begins, ends=ends),
            plain(*near_grads[first : first + count])
            + all_slides(far_backs[g])
            + plain(*blocks[g], weight, gains, *sums_so_far),
            wgrads + [(f32(8, 3 * local), None), (f32(8, width), None), (back, None), (back, None)],
            scratch=[vm(4, TRIPLE, lanes)] + ([vm(3 * local, width, dtype=F32)] if ends else []),
            us=2 + 4 * count,
        )
        sums_so_far[:] = outs[:-2]
        backs[g] = (outs[-2], swap(outs[-1], "head", 1))

    def fold_back(g, axis, bit):
        first, second = backs[g]
        count, _, blocks_here, _, _ = first.shape
        shape = bf(count, 2, blocks_here // 2, half, width)
        stay, send = step("fold", fold_kernel, plain(first, second), [(shape, None)] * 2, us=1)
        backs[g] = (stay, swap(send, axis, bit))

    results = []

    def leave(g):
        first, count = parts[g]
        output, grad_mid = owned[g][:2]
        pieces = [value.reshape(count, 2, half, width) for value in backs[g]]
        piece = pl.BlockSpec((1, 2, half, width), lambda s, k, p: (k, 0, 0, 0))
        row = pl.BlockSpec((1, 1, rows, width), lambda s, k, p: (s, k, 0, 0))
        out = pl.BlockSpec((1, rows, width), lambda s, k, p: ((p[1] ^ s) * group + first + k, 0, 0))
        any_spec = pl.BlockSpec(memory_space=pl.ANY)
        results[:] = step(
            "leave",
            exit_kernel,
            [(value, piece) for value in pieces]
            + [(bases[g], row), (grad_mid, row), (output, row), (gains, None)]
            + [(value, any_spec) for value in results],
            [(bf(*tiles.shape), out)] * 2,
            grid=(2, count),
            aliases={6: 0, 7: 1} if results else None,
            us=1 + 1.3 * count,
        )

    def z_fold(pair, bit):
        first, second = pair
        shape = bf(first.shape[0] // 2, first.shape[1])
        stay, send = step(
            "z_fold",
            partial(z_fold_kernel, bit=bit),
            plain(first, second),
            [(shape, None)] * 2,
            scratch=[vm(*first.shape)],
            us=1,
        )
        return stay, swap(send, "seq", 4 if bit else 2)

    def small_step(name, body, pair, extra=()):
        return step(name, body, plain(*pair, *extra), [(f32(8, width), None)], us=0.5)[0]

    narrow(0, "head", 2)
    sent_w = weight_grads(2, [])
    narrow(0, "head", 1)
    narrow(1, "head", 2)
    rows_of_gradients(0)
    near_backward(0, 0)
    narrow(1, "head", 1)
    outs = weight_grads(0, [swap(value, "head", 1) for value in sent_w])
    first_w = (outs[0], swap(outs[1], "seq", 1))
    second_w = (outs[2], swap(outs[3], "head", 2))
    rows_of_gradients(1)
    near_backward(1, 0)
    far_backward(1, False)
    second_w = split_fold(second_w, "seq", 1)
    first_w = split_fold(first_w, "head", 2)
    far_backward(0, True)
    near_backward(1, 1)
    far_backs[0] = over_z_second(far_backs[0])
    stay, send = step(
        "z_fold_both",
        z_fold_both_kernel,
        plain(*first_w, *second_w),
        [(bf(tall // 2, FIRST_COLUMNS + width), None)] * 2,
        scratch=[vm(tall, FIRST_COLUMNS + width)],
        us=2,
    )
    folded = (stay, swap(send, "seq", 4))
    project_back(1, False)
    fold_back(1, "head", 2)
    project_back(0, True)
    stay, send, bias_sum, ln_sum = sums_so_far
    grad_in = (stay, swap(send, "seq", 1))
    stay, send, last = step(
        "small_start",
        small_start_kernel,
        plain(*[owned[g][2] for g in range(2)], *[owned[g][3] for g in range(2)], ln_sum, bias_sum),
        [(f32(8, width), None)] * 3,
        us=0.5,
    )
    common = (stay, swap(send, "head", 1))
    fold_back(0, "head", 2)
    stay, send = step("small_middle", small_middle_kernel, plain(*common), [(f32(8, width), None)] * 2, us=0.5)
    common = (stay, swap(send, "head", 2))
    fold_back(1, "seq", 1)
    grad_in = z_fold(grad_in, True)
    common = small_step("small_last", small_last_kernel, common, [last])
    common = (common, swap(common, "seq", 1))
    fold_back(0, "seq", 1)
    folded = z_fold(folded, False)
    common = small_step("add", add_kernel, common)
    common = (common, swap(common, "seq", 4))
    leave(1)
    grad_in = z_fold(grad_in, False)
    common = small_step("add", add_kernel, common)
    common = (common, swap(common, "seq", 2))
    leave(0)
    w_fc1_grad, w_fc2_grad, w_out_grad = step(
        "weights_out",
        weights_out_kernel,
        plain(*folded),
        [
            (f32(width // 8, width), None),
            (f32(width, width // 8), None),
            (f32(local, width // 8), None),
        ],
        us=1.5,
    )
    w_qkv_grad = step(
        "qkv_out", qkv_out_kernel, plain(*grad_in), [(f32(width // 8, 3, local), None)], us=1.5
    )[0]
    common = small_step("add", add_kernel, common)
    per_head = common[7, : 3 * local].reshape(4, 3, HEAD_DIM).transpose(1, 0, 2).reshape(3, local)
    tiles_grad, output = results
    return (
        output,
        tiles_grad,
        common[4],
        common[5],
        w_qkv_grad,
        jnp.stack([per_head[0], per_head[2]]),
        w_out_grad,
        common[0],
        common[1],
        common[2],
        w_fc1_grad,
        common[6],
        w_fc2_grad,
        common[3],
    )


def nests(mesh, tiles, padding_mask):
    sizes = (mesh.shape["seq"], mesh.shape["head"], tiles.shape[0])
    return sizes == (8, 4, 6) and padding_mask.shape[1] <= SEG2


def solution(mesh):
    def program(*args):
        one_span = nests(mesh, args[0], args[3])
        return spread_out(mesh, nested if one_span else on_device)(*args)

    return program


def spread_out(mesh, body):
    placed = (
        P(None, ("seq", "head"), None),
        P(None, ("seq", "head"), None),
        P(),
        P(),
        P(),
        P(),
        P(None, None, "head"),
        P(None, "head"),
        P("head", None),
        P(),
        P(),
        P(),
        P(None, "head"),
        P("head"),
        P("head", None),
        P(),
        P(None, ("seq", "head"), None),
    )
    return jax.shard_map(
        body,
        mesh=mesh,
        in_specs=placed,
        out_specs=(
            P(None, ("seq", "head"), None),
            P(None, ("seq", "head"), None),
            P(),
            P(),
            P("seq", None, "head"),
            P(None, "head"),
            P("head", "seq"),
            P(),
            P(),
            P(),
            P("seq", "head"),
            P("head"),
            P("head", "seq"),
            P(),
        ),
        check_vma=False,
    )
```

```python
from functools import partial
import math

import jax
import jax.numpy as jnp
import ml_dtypes
import numpy as np
from jax import lax
from jax.experimental import pallas as pl
from jax.experimental.pallas import tpu as pltpu
from jax.sharding import PartitionSpec as P

HEADS = 16
FF = 3072
SEG2 = 5792
RATIO = 16


NEG = -10000.0
FLOOR = -1e30
EPS = 1e-05


def partner(x, axis, stride):
    return lax.ppermute(x, axis, [(i, i ^ 1 << stride) for i in range(lax.axis_size(axis))])


def layer_norm(value, gain, shift):
    mean = jnp.mean(value, axis=-1, keepdims=True)
    centered = value - mean
    var = jnp.mean(centered * centered, axis=-1, keepdims=True)
    return centered * lax.rsqrt(var + EPS) * gain + shift


def position_table(coords, width):
    quarter = width // 4
    freq = jnp.exp(-jnp.log(10000.0) * jnp.arange(quarter, dtype=jnp.float32) / quarter)
    col_angle = coords[..., 0:1].astype(jnp.float32) * freq
    row_angle = coords[..., 1:2].astype(jnp.float32) * freq
    return jnp.concatenate(
        [jnp.sin(col_angle), jnp.cos(col_angle), jnp.sin(row_angle), jnp.cos(row_angle)], axis=-1
    )


def mask_shape(value, chosen):
    return (1, 1, chosen.shape[0]) + (1,) * (value.ndim - 4) + (chosen.shape[1], 1)


def pick(value, chosen):
    rate = chosen.shape[0]
    split = value.reshape((value.shape[0], value.shape[1] // rate, rate) + value.shape[2:])
    return jnp.sum(
        jnp.where(chosen.reshape(mask_shape(value, chosen)), split, jnp.zeros((), value.dtype)),
        axis=2,
    )


def spread(value, chosen):
    rate = chosen.shape[0]
    full = jnp.where(
        chosen.reshape(mask_shape(value, chosen)),
        jnp.expand_dims(value, 2),
        jnp.zeros((), value.dtype),
    )
    return full.reshape((value.shape[0], value.shape[1] * rate) + value.shape[2:])


def scores_of(query, keys, bias, pair, scale):
    raw = jnp.einsum("qhe,khe->hqk", query, keys, preferred_element_type=jnp.float32)
    return raw * scale + jnp.transpose(bias)[:, None, :] + pair


def attend_forward(query, keys, values, bias, pair, scale):
    scores = scores_of(query, keys, bias, pair, scale)
    total = jax.nn.logsumexp(scores, axis=-1)
    probs = jnp.exp(scores - total[..., None]).astype(jnp.bfloat16)
    result = jnp.einsum("hqk,khe->qhe", probs, values, preferred_element_type=jnp.float32)
    return (result, jnp.transpose(total)[..., None])


def attend_backward(query, keys, values, bias, pair, total, grad_out, grad_total, scale):
    scores = scores_of(query, keys, bias, pair, scale)
    probs = jnp.exp(scores - jnp.transpose(total[..., 0])[..., None])
    grad_probs = jnp.einsum("qhe,khe->hqk", grad_out, values, preferred_element_type=jnp.float32)
    delta = jnp.sum(probs * grad_probs, axis=-1) - jnp.transpose(grad_total[..., 0])
    grad_scores = (probs * (grad_probs - delta[..., None])).astype(jnp.bfloat16)
    grad_query = (
        jnp.einsum("hqk,khe->qhe", grad_scores, keys, preferred_element_type=jnp.float32) * scale
    )
    grad_keys = (
        jnp.einsum("hqk,qhe->khe", grad_scores, query, preferred_element_type=jnp.float32) * scale
    )
    grad_values = jnp.einsum(
        "hqk,qhe->khe", probs.astype(jnp.bfloat16), grad_out, preferred_element_type=jnp.float32
    )
    return (grad_query, grad_keys, grad_values)


def forward_slide(args, pair, scale):
    q_one, kv_one, bias_one = args
    return attend_forward(q_one, kv_one[:, 0], kv_one[:, 1], bias_one, pair, scale)


def backward_slide(args, pair, scale):
    q_one, kv_one, bias_one, total_one, grad_one, grad_total_one = args
    return attend_backward(
        q_one,
        kv_one[:, 0],
        kv_one[:, 1],
        bias_one,
        pair,
        total_one,
        grad_one,
        grad_total_one,
        scale,
    )


def on_device(
    tiles,
    coords,
    lengths,
    padding_mask,
    ln1_gain,
    ln1_bias,
    query_key_value_weight,
    qv_bias,
    attention_output_weight,
    attention_output_bias,
    ln2_gain,
    ln2_bias,
    mlp_entry_matrix,
    mlp_entry_offset,
    feed_output_weight,
    feed_output_bias,
    cotangent,
):
    slides, rows, width = tiles.shape
    head_count = lax.axis_size("head")
    local_width = query_key_value_weight.shape[2]
    local_heads = local_width * HEADS // width
    head_dim = width // HEADS
    hidden_local = mlp_entry_matrix.shape[1]
    scale = 1.0 / math.sqrt(head_dim)
    seg_rows = rows * head_count
    total_len = padding_mask.shape[1]
    seq_index = lax.axis_index("seq")
    head_index = lax.axis_index("head")
    dilations = (RATIO // 8, RATIO // 4, RATIO // 2, RATIO)
    reaches = (SEG2, total_len, total_len, total_len)
    positions = jnp.arange(total_len, dtype=jnp.int32)
    valid = (positions[None, :] < lengths[:, None]) & (padding_mask == 1)
    own_valid = lax.dynamic_slice_in_dim(valid, seq_index * seg_rows, seg_rows, 1)
    mate_valid = lax.dynamic_slice_in_dim(valid, (seq_index ^ 1) * seg_rows, seg_rows, 1)
    near_valid = jnp.concatenate([own_valid, mate_valid], axis=1)
    near_bias = jnp.broadcast_to(
        jnp.where(near_valid, 0.0, NEG)[..., None], (slides, 2 * seg_rows, local_heads)
    )
    global_heads = head_index * local_heads + jnp.arange(local_heads, dtype=jnp.int32)
    chosens = []
    far_biases = []
    selects = []
    pair_masks = []
    for dilation, reach in zip(dilations, reaches):
        chosen = (
            jnp.arange(dilation, dtype=jnp.int32)[:, None] == (global_heads % dilation)[None, :]
        )
        chosens.append(chosen)
        far_valid = jnp.any(
            valid.reshape(slides, total_len // dilation, dilation)[..., None] & chosen[None, None],
            axis=2,
        )
        far_biases.append(jnp.where(far_valid, 0.0, NEG))
        selects.append(
            (
                (jnp.arange(seg_rows, dtype=jnp.int32) % dilation)[:, None]
                == (global_heads % dilation)[None, :]
            )[None, :, :, None]
        )
        query_places = seq_index * seg_rows + dilation * jnp.arange(
            seg_rows // dilation, dtype=jnp.int32
        )
        key_places = dilation * jnp.arange(total_len // dilation, dtype=jnp.int32)
        pair_masks.append(
            jnp.where((query_places // reach)[:, None] == (key_places // reach)[None, :], 0.0, NEG)
        )
    base = tiles.astype(jnp.float32) + position_table(coords, width)
    first_normalized = layer_norm(base, ln1_gain, ln1_bias).astype(jnp.bfloat16)
    initial_tokens, cotangent_rows = (
        lax.all_gather(first_normalized, "head", axis=1, tiled=True),
        lax.all_gather(cotangent, "head", axis=1, tiled=True),
    )
    packed_projection_matrix = query_key_value_weight.reshape(width, 3 * local_width)
    triple_bias = jnp.concatenate([qv_bias[0], jnp.zeros_like(qv_bias[0]), qv_bias[1]])
    query_key_value = (
        jnp.einsum(
            "hmq,qn->hmn",
            initial_tokens,
            packed_projection_matrix,
            preferred_element_type=jnp.float32,
        )
        + triple_bias
    ).astype(jnp.bfloat16)
    query_key_value = query_key_value.reshape(slides, seg_rows, 3, local_heads, head_dim)
    query = query_key_value[:, :, 0]
    key_value = query_key_value[:, :, 1:3]
    mate_kv = partner(key_value, "seq", 0)
    near_kv = jnp.concatenate([key_value, mate_kv], axis=1)

    def collect(piece):
        return tuple((pick(piece, chosens[index]) for index in range(4)))

    far_kvs = collect(lax.all_gather(key_value, "seq", axis=1, tiled=True))
    far_queries = [pick(query, chosen) for chosen in chosens]
    near_out, near_total = lax.map(
        partial(forward_slide, pair=0.0, scale=scale), (query, near_kv, near_bias)
    )
    far_results = []
    for index in range(4):
        far_results.append(
            lax.map(
                partial(forward_slide, pair=pair_masks[index], scale=scale),
                (far_queries[index], far_kvs[index], far_biases[index]),
            )
        )
    outs_full = [near_out] + [spread(far_results[index][0], chosens[index]) for index in range(4)]
    totals_full = [near_total] + [
        jnp.where(selects[index], spread(far_results[index][1], chosens[index]), FLOOR)
        for index in range(4)
    ]
    stacked = jnp.stack(totals_full)
    highest = jnp.max(stacked, axis=0)
    raised = jnp.exp(stacked - highest)
    weights = raised / jnp.sum(raised, axis=0)
    combined_output = weights[0] * outs_full[0]
    for index in range(1, 5):
        combined_output = combined_output + weights[index] * outs_full[index]
    combined_lowered = combined_output.reshape(slides, seg_rows, local_width).astype(jnp.bfloat16)
    attention_piece = jnp.einsum(
        "mua,ah->muh", combined_lowered, attention_output_weight, preferred_element_type=jnp.float32
    )
    attn_rows = lax.psum_scatter(
        attention_piece.astype(jnp.bfloat16), "head", scatter_dimension=1, tiled=True
    ).astype(jnp.float32)
    mid = base + (attn_rows + attention_output_bias)
    later_layernormed = layer_norm(mid, ln2_gain, ln2_bias).astype(jnp.bfloat16)
    later_tokens = lax.all_gather(later_layernormed, "head", axis=1, tiled=True)
    before_nonlinearity = (
        jnp.einsum(
            "awq,qd->awd", later_tokens, mlp_entry_matrix, preferred_element_type=jnp.float32
        )
        + mlp_entry_offset
    )
    hidden_activation = jax.nn.gelu(before_nonlinearity, approximate=False).astype(jnp.bfloat16)
    feedforward_piece = jnp.einsum(
        "nrv,vk->nrk", hidden_activation, feed_output_weight, preferred_element_type=jnp.float32
    )
    mlp_rows_sum = lax.psum_scatter(
        feedforward_piece.astype(jnp.bfloat16), "head", scatter_dimension=1, tiled=True
    ).astype(jnp.float32)
    output = mid + (mlp_rows_sum + feed_output_bias)
    cot_float = cotangent.astype(jnp.float32)
    grad_fc2_bias = jnp.sum(cot_float, axis=(0, 1))
    hidden_gradient = jnp.einsum(
        "tvq,cq->tvc", cotangent_rows, feed_output_weight, preferred_element_type=jnp.float32
    )
    feed_output_weight_gradient = jnp.einsum(
        "gar,gai->ri", hidden_activation, cotangent_rows, preferred_element_type=jnp.float32
    )
    gelu_pull = jax.vjp(lambda v: jax.nn.gelu(v, approximate=False), before_nonlinearity)[1]
    preactivation_gradient = gelu_pull(hidden_gradient)[0].astype(jnp.bfloat16)
    feed_input_weight_gradient = jnp.einsum(
        "vxr,vxm->rm", later_tokens, preactivation_gradient, preferred_element_type=jnp.float32
    )
    grad_fc1_bias = jnp.sum(preactivation_gradient.astype(jnp.float32), axis=(0, 1))
    second_backward = jnp.einsum(
        "ivo,go->ivg", preactivation_gradient, mlp_entry_matrix, preferred_element_type=jnp.float32
    )
    back2_rows = lax.psum_scatter(
        second_backward.astype(jnp.bfloat16), "head", scatter_dimension=1, tiled=True
    ).astype(jnp.float32)
    norm2_pull = jax.vjp(layer_norm, mid, ln2_gain, ln2_bias)[1]
    grad_mid_norm, grad_ln2_gain, grad_ln2_bias = norm2_pull(back2_rows)
    grad_mid = cot_float + grad_mid_norm
    grad_attn = grad_mid.astype(jnp.bfloat16)
    grad_out_bias = jnp.sum(grad_attn.astype(jnp.float32), axis=(0, 1))
    attention_rows_gradient = lax.all_gather(grad_attn, "head", axis=1, tiled=True)
    grad_w_out = jnp.einsum(
        "fub,fui->bi", combined_lowered, attention_rows_gradient, preferred_element_type=jnp.float32
    )
    grad_merged = jnp.einsum(
        "tpq,jq->tpj",
        attention_rows_gradient,
        attention_output_weight,
        preferred_element_type=jnp.float32,
    )
    grad_merged = grad_merged.reshape(slides, seg_rows, local_heads, head_dim)
    grad_parts = [weights[index] * grad_merged for index in range(5)]
    gaps = [
        weights[index]
        * jnp.sum(grad_merged * (outs_full[index] - combined_output), axis=-1, keepdims=True)
        for index in range(5)
    ]
    grad_near = grad_parts[0].astype(jnp.bfloat16)
    near_dq, near_dk, near_dv = lax.map(
        partial(backward_slide, pair=0.0, scale=scale),
        (query, near_kv, near_bias, near_total, grad_near, gaps[0]),
    )
    own_grad = jnp.stack([near_dk[:, :seg_rows], near_dv[:, :seg_rows]], axis=2)
    mate_grad = jnp.stack([near_dk[:, seg_rows:], near_dv[:, seg_rows:]], axis=2)
    returned = partner(mate_grad.astype(jnp.bfloat16), "seq", 0).astype(mate_grad.dtype)
    far_grads = []
    grad_query = near_dq
    for index in range(4):
        grad_far = pick(grad_parts[index + 1], chosens[index]).astype(jnp.bfloat16)
        grad_far_total = pick(gaps[index + 1], chosens[index])
        far_dq, far_dk, far_dv = lax.map(
            partial(backward_slide, pair=pair_masks[index], scale=scale),
            (
                far_queries[index],
                far_kvs[index],
                far_biases[index],
                far_results[index][1],
                grad_far,
                grad_far_total,
            ),
        )
        far_grads.append(jnp.stack([far_dk, far_dv], axis=2))
        grad_query = grad_query + spread(far_dq, chosens[index])
    far_back = (
        lax.psum_scatter(
            far_grads[0].astype(jnp.bfloat16), "seq", scatter_dimension=1, tiled=True
        ).astype(jnp.float32),
        lax.psum_scatter(
            far_grads[1].astype(jnp.bfloat16), "seq", scatter_dimension=1, tiled=True
        ).astype(jnp.float32),
        lax.psum_scatter(
            far_grads[2].astype(jnp.bfloat16), "seq", scatter_dimension=1, tiled=True
        ).astype(jnp.float32),
        lax.psum_scatter(
            far_grads[3].astype(jnp.bfloat16), "seq", scatter_dimension=1, tiled=True
        ).astype(jnp.float32),
    )
    grad_kv = own_grad + returned
    for index in range(4):
        grad_kv = grad_kv + spread(far_back[index], chosens[index])
    query_key_value_gradient = jnp.concatenate([grad_query[:, :, None], grad_kv], axis=2).astype(
        jnp.bfloat16
    )
    query_key_value_gradient = query_key_value_gradient.reshape(slides, seg_rows, 3 * local_width)
    grad_w_qkv = jnp.einsum(
        "ymt,yma->ta", initial_tokens, query_key_value_gradient, preferred_element_type=jnp.float32
    ).reshape(width, 3, local_width)
    bias_sums = jnp.sum(query_key_value_gradient.astype(jnp.float32), axis=(0, 1)).reshape(
        3, local_width
    )
    grad_qv = jnp.stack([bias_sums[0], bias_sums[2]])
    first_backward = jnp.einsum(
        "kgw,aw->kga",
        query_key_value_gradient,
        packed_projection_matrix,
        preferred_element_type=jnp.float32,
    )
    back1_rows = lax.psum_scatter(
        first_backward.astype(jnp.bfloat16), "head", scatter_dimension=1, tiled=True
    ).astype(jnp.float32)
    norm1_pull = jax.vjp(layer_norm, base, ln1_gain, ln1_bias)[1]
    grad_base_norm, grad_ln1_gain, grad_ln1_bias = norm1_pull(back1_rows)
    tiles_grad = (grad_mid + grad_base_norm).astype(jnp.bfloat16)
    w_qkv_grad, w_out_grad, w_fc1_grad, w_fc2_grad = (
        lax.psum_scatter(
            grad_w_qkv.astype(jnp.bfloat16), "seq", scatter_dimension=0, tiled=True
        ).astype(jnp.float32),
        lax.psum_scatter(
            grad_w_out.astype(jnp.bfloat16), "seq", scatter_dimension=1, tiled=True
        ).astype(jnp.float32),
        lax.psum_scatter(
            feed_input_weight_gradient.astype(jnp.bfloat16), "seq", scatter_dimension=0, tiled=True
        ).astype(jnp.float32),
        lax.psum_scatter(
            feed_output_weight_gradient.astype(jnp.bfloat16), "seq", scatter_dimension=1, tiled=True
        ).astype(jnp.float32),
    )
    shared = jnp.stack(
        [grad_ln1_gain, grad_ln1_bias, grad_out_bias, grad_ln2_gain, grad_ln2_bias, grad_fc2_bias]
    )
    qv_full = lax.dynamic_update_slice_in_dim(
        jnp.zeros((2, width), jnp.float32), grad_qv, head_index * local_width, 1
    )
    fc1_full = lax.dynamic_update_slice_in_dim(
        jnp.zeros((FF,), jnp.float32), grad_fc1_bias, head_index * hidden_local, 0
    )
    shared_sum, qv_sum, fc1_sum = lax.psum((shared, qv_full, fc1_full), ("seq", "head"))
    qv_bias_grad = lax.dynamic_slice_in_dim(qv_sum, head_index * local_width, local_width, 1)
    fc1_bias_grad = lax.dynamic_slice_in_dim(fc1_sum, head_index * hidden_local, hidden_local, 0)
    return (
        output.astype(jnp.bfloat16),
        tiles_grad,
        shared_sum[0],
        shared_sum[1],
        w_qkv_grad,
        qv_bias_grad,
        w_out_grad,
        shared_sum[2],
        shared_sum[3],
        shared_sum[4],
        w_fc1_grad,
        fc1_bias_grad,
        w_fc2_grad,
        shared_sum[5],
    )


HEAD_DIM = 48
TRIPLE = 144
META = 32
AUG = 128
OUT_ROWS = 64
ACC_ROWS = 56
SLOT_ORDER = (0, 2, 1, 3)
LOG2E = math.log2(math.e)
COST = 2.5
NEAR_US = 6.6
WG_US = 12
NB_US = 0.2
FA_US = 3
SMALL_US = 0.5
FIRST_COLUMNS = 1024
BF = jnp.bfloat16
F32 = jnp.float32


def dot(a, b):
    return lax.dot_general(a, b, (((1,), (0,)), ((), ())), preferred_element_type=F32)


def dot_nt(a, b):
    return lax.dot_general(a, b, (((1,), (1,)), ((), ())), preferred_element_type=F32)


def split3(value):
    high = value.astype(BF)
    rest = value - high.astype(F32)
    middle = rest.astype(BF)
    low = (rest - middle.astype(F32)).astype(BF)
    return high, middle, low


def split3_constant(value):
    pieces = []
    rest = np.float32(value)
    for _ in range(3):
        piece = np.float32(rest.astype(ml_dtypes.bfloat16))
        pieces.append(float(piece))
        rest = np.float32(rest - piece)
    return pieces


def joined(rows):
    wide = rows.astype(F32)
    return wide[0:1] + wide[1:2] + wide[2:3]


def rows_of(shape, first, pieces):
    row = lax.broadcasted_iota(jnp.int32, shape, 0)
    out = jnp.zeros(shape, F32)
    for index, piece in enumerate(pieces):
        out = jnp.where(row == first + index, piece, out)
    return out


def rows_between(shape, first, count):
    row = lax.broadcasted_iota(jnp.int32, shape, 0)
    return jnp.where((row >= first) & (row < first + count), 1.0, 0.0)


def query_rows(query, meta, factor):
    wide = query.astype(F32) * factor
    high = wide.astype(BF)
    low = (wide - high.astype(F32)).astype(BF)
    return jnp.concatenate([high, low, meta], 0)


def key_rows(keys, meta):
    return jnp.concatenate([keys, keys, meta], 0)


def ones_below(value, count):
    width = value.shape[-1]
    return jnp.concatenate([value, rows_between((16, width), 0, count).astype(BF)], 0)


def plain64(value):
    return jnp.concatenate([value, jnp.zeros((16, value.shape[-1]), value.dtype)], 0)


def padded_turn(value):
    height, width = value.shape
    missing = -height % 128
    full = jnp.concatenate([value, jnp.zeros((missing, width), value.dtype)], 0)
    return full.T


def turned_out(value):
    height = value.shape[0]
    return jnp.concatenate([value, jnp.zeros((height, 64), F32)], 1).T[0:HEAD_DIM]


def bias_rows(valid):
    shape = (META, valid.shape[-1])
    return rows_of(shape, 0, [(1.0 - valid) * part for part in split3_constant(NEG * LOG2E)])


def near_key_meta(valid):
    shape = (META, valid.shape[-1])
    return (bias_rows(valid) + rows_between(shape, 15, 3)).astype(BF)


def far_levels(place, width, half):
    head = 4 * (2 * place[2] + place[3]) + place[0]
    lane = lax.broadcasted_iota(jnp.int32, (1, width), 1)
    spot = (2 * (lane & (half - 1)) + (place[0] & 1)) & 15
    return jnp.where(
        spot == (head & 15),
        4,
        jnp.where((spot & 7) == (head & 7), 3, jnp.where((spot & 3) == (head & 3), 2, 1)),
    )


def far_tables(level):
    pieces = {0: [], 1: []}
    for extra in (0, 1):
        for part in range(3):
            for kind in range(1, 5):
                row = jnp.zeros(level.shape, F32)
                for there in range(1, 5):
                    amount = split3_constant(math.log2(min(kind, there) + extra))[part]
                    row = jnp.where(level == there, amount, row)
                pieces[extra].append(row)
    shape = (META, level.shape[-1])
    return rows_of(shape, 3, pieces[0]) + rows_between(shape, 15, 3) + rows_of(shape, 18, pieces[1])


def far_queries(level):
    shape = (META, level.shape[-1])
    chosen = [jnp.where(level == kind, 1.0, 0.0) for kind in range(1, 5)] * 3
    ones = rows_between(shape, 0, 3)
    return (ones + rows_of(shape, 18, chosen)).astype(BF), (ones + rows_of(shape, 3, chosen)).astype(BF)


def softmax_out(keys, values, queries, stage):
    top = None
    for index, key in enumerate(keys):
        scores = dot(key(), queries[index])
        stage[index] = scores
        peak = jnp.max(scores, axis=0, keepdims=True)
        top = peak if top is None else jnp.maximum(top, peak)
    acc = None
    for index, value in enumerate(values):
        probs = jnp.exp2(stage[index] - top).astype(BF)
        part = dot(value(), probs)
        acc = part if acc is None else acc + part
    total = acc[HEAD_DIM : HEAD_DIM + 1]
    return acc[0:HEAD_DIM] * (1.0 / total), top + jnp.log2(total)


def moments(value):
    mean = jnp.mean(value, axis=-1, keepdims=True)
    centered = value - mean
    var = jnp.mean(centered * centered, axis=-1, keepdims=True)
    rate = lax.rsqrt(var + EPS)
    return centered * rate, rate


def norm_back(xhat, rate, gain, upstream):
    a = upstream * gain
    return rate * (
        a - jnp.mean(a, axis=-1, keepdims=True) - xhat * jnp.mean(a * xhat, axis=-1, keepdims=True)
    )


def parity_order(rows, back):
    first = lax.broadcasted_iota(jnp.int32, (rows, rows), 1 if back else 0)
    second = lax.broadcasted_iota(jnp.int32, (rows, rows), 0 if back else 1)
    half = rows // 2
    source = jnp.where(first < half, 2 * first, 2 * (first - half) + 1)
    return (source == second).astype(F32).astype(BF)


def entry_kernel(
    place, tiles_a, tiles_b, coords_a, coords_b, cot_a, cot_b, table, base, cot_out, own, other
):
    rows = tiles_a.shape[1]
    half = rows // 2
    order = parity_order(rows, False)
    lane = lax.broadcasted_iota(jnp.int32, (rows, 256), 1).astype(F32)
    sides = ((tiles_a, coords_a, cot_a, own), (tiles_b, coords_b, cot_b, other))
    for side, (tiles, coords, cot, out) in enumerate(sides):
        spots = dot(order, coords[0].astype(F32).astype(BF))
        parts = []
        for axis in range(2):
            hot = (spots[:, axis : axis + 1] == lane).astype(F32).astype(BF)
            parts.append(dot(hot, table[0]) + dot(hot, table[1]) + dot(hot, table[2]))
        value = dot(order, tiles[0]) + jnp.concatenate(parts, 1)
        base[side, 0] = value
        xhat = moments(value)[0].astype(BF)
        out[0, 0] = xhat[:half]
        out[0, 1] = xhat[half:]
        cot_out[side, 0] = dot(order, cot[0]).astype(BF)


def join_kernel(place, first, second, out):
    here = first.shape[2]
    out[:, :, :here] = first[...]
    out[:, :, here:] = second[...]


def widen_kernel(place, first, second, stay, send):
    half = first.shape[2] // 2
    stay[...] = jnp.concatenate([first[:, :, :half], second[:, :, :half]], -1)
    send[...] = jnp.concatenate([first[:, :, half:], second[:, :, half:]], -1)


def narrow_kernel(place, first, second, stay, send):
    here = first.shape[2]
    columns = first.shape[-1] // 2
    for ref, part in ((first, slice(0, here)), (second, slice(here, 2 * here))):
        stay[:, :, part] = ref[..., :columns]
        send[:, :, part] = ref[..., columns:]


def fold_kernel(place, first, second, stay, send):
    half = first.shape[2] // 2
    total = (first[...].astype(F32) + second[...].astype(F32)).astype(BF)
    stay[...] = total[:, :, :half]
    send[...] = total[:, :, half:]


def z_halves(place, total, stay, send, nearest):
    piece = total.shape[0] // (4 if nearest else 2)
    side = place[0] % 2 if nearest else place[0] // 2
    for lead in range(2 if nearest else 1):
        rows = slice(lead * piece, (lead + 1) * piece)
        for ref, here in ((stay, side), (send, 1 - side)):
            at = pl.multiple_of((2 * lead + here) * piece, 32)
            ref[rows] = total[pl.ds(at, piece)]


def z_fold_kernel(place, first, second, stay, send, total, *, nearest):
    total[...] = (first[...].astype(F32) + second[...].astype(F32)).astype(BF)
    z_halves(place, total, stay, send, nearest)


def weights_out_kernel(place, first, second, fc1, fc2, out):
    total = first[...].astype(F32) + second[...].astype(F32)
    width = fc1.shape[1]
    rows = total.shape[0]
    fc1[...] = total[:, :width]
    out[...] = padded_turn(total[:, width:FIRST_COLUMNS])[: out.shape[0], :rows]
    fc2[...] = padded_turn(total[:, FIRST_COLUMNS:])[:, :rows]


def qkv_out_kernel(place, first, second, out):
    total = first[...].astype(F32) + second[...].astype(F32)
    for head in range(4):
        for part in range(3):
            at = (head * 3 + part) * HEAD_DIM
            out[:, part, head * HEAD_DIM : (head + 1) * HEAD_DIM] = total[:, at : at + HEAD_DIM]


def small_start_kernel(place, sums_a, sums_b, fc1_a, fc1_b, ln_sum, bias_sum, stay, send):
    width = sums_a.shape[1]
    common = [sums_a[index : index + 1] + sums_b[index : index + 1] for index in range(4)]
    common += [ln_sum[0:1], ln_sum[1:2]]
    slots = [fc1_a[slot, 0:1] + fc1_b[slot, 0:1] for slot in range(4)]
    missing = width - bias_sum.shape[1]
    last = jnp.concatenate([bias_sum[0:1], jnp.zeros((1, missing), F32)], 1)
    stay[...] = rows_of((16, width), 0, common + slots[0:2] + [last])
    send[...] = rows_of((8, width), 0, common + slots[2:4])


def small_first_kernel(place, first, second, out):
    out[0:8] = first[0:8] + second[...]
    out[8:16] = first[8:16]


def small_middle_kernel(place, first, second, stay, send):
    total = first[...] + second[...]
    row = lax.broadcasted_iota(jnp.int32, stay.shape, 0)
    stay[...] = jnp.where(row == 7, total[8:9], total[0:8])
    send[...] = jnp.where(row == 6, total[7:8], jnp.where(row == 7, 0.0, total[0:8]))


def add_kernel(place, first, second, out):
    out[...] = first[...] + second[...]


def normed_of(xhat, gains):
    return (xhat.astype(F32) * gains[0:1] + gains[1:2]).astype(BF)


def qkv_kernel(place, first, second, weight, bias, gains, near, s0, s1, s2, s3):
    width = first.shape[2]
    for parity in range(2):
        for part, ref in enumerate((first, second)):
            made = dot_nt(weight[...], normed_of(ref[0, parity], gains)) + bias[...]
            made = made.astype(BF)
            for head in range(4):
                near[0, head, parity, :, part * width : (part + 1) * width] = made[
                    head * TRIPLE : (head + 1) * TRIPLE
                ]
    for slot, ref in enumerate((s0, s1, s2, s3)):
        head = place[0] ^ slot
        ref[0] = near[0, head, head & 1]


def near_forward_kernel(place, qkv, valid, out, key_aug, value_aug, stage, *, slide, factor):
    width = qkv.shape[-1]
    own = lax.rem(pl.program_id(0), 2)
    queries = []
    ones = rows_between((META, width), 0, 3).astype(BF)
    for role in range(2):
        parity = own if role == 0 else 1 - own
        block = qkv[0, 0, parity]
        there = valid[place[1] * 3 + slide, pl.ds(place[0] * 2 + parity, 1)]
        key_aug[role] = key_rows(block[48:96], near_key_meta(there)).T
        value_aug[role] = ones_below(block[96:144], 1)
        queries.append(query_rows(block[0:48], ones, factor))
    for role, used in ((0, (1,)), (1, (0, 1))):
        result, total = softmax_out(
            [lambda r=r: key_aug[r] for r in used],
            [lambda r=r: value_aug[r] for r in used],
            [queries[role]] * len(used),
            stage,
        )
        out[0, role] = jnp.concatenate([result, rows_of((8, width), 0, [total])], 0)


def far_forward_kernel(
    place, b0, b1, b2, b3, valid, o0, o1, o2, o3, key_aug, value_aug, q_same, q_other, stage, out,
    *, first_slide, half, factor,
):
    width = b0.shape[-1]
    slide = first_slide + pl.program_id(0)
    level = far_levels(place, width, half)
    tail = far_tables(level)
    same, other = far_queries(level)
    for slot, block in enumerate((b0, b1, b2, b3)):
        row = (place[0] ^ slot) * 2 + (place[0] & 1)
        there = valid[place[1] * 3 + slide, pl.ds(row, 1)]
        key_aug[slot] = key_rows(block[0, 48:96], (tail + bias_rows(there)).astype(BF)).T
        value_aug[slot] = ones_below(block[0, 96:144], 1)
        q_same[slot] = query_rows(block[0, 0:48], same, factor)
        q_other[slot] = query_rows(block[0, 0:48], other, factor)

    def step(slot, carry):
        places = [lax.rem(slot + shift, 4) for shift in range(4)]
        result, total = softmax_out(
            [lambda p=p: key_aug[p] for p in places],
            [lambda p=p: value_aug[p] for p in places],
            [q_same[slot], q_other[slot], q_other[slot], q_other[slot]],
            stage,
        )
        ending = rows_of((16, width), 0, [part.astype(F32) for part in split3(total)])
        out[slot] = jnp.concatenate([result, ending], 0).astype(BF)
        return carry

    lax.fori_loop(0, 4, step, 0)
    for slot, ref in enumerate((o0, o1, o2, o3)):
        ref[0] = out[slot]


def merge_kernel(place, *refs):
    count = refs[-2].shape[0]
    nears = refs[:count]
    f0, f1, f2, f3, kept, stay, send, far = refs[count:]
    width = kept.shape[-1]
    for slide, near in enumerate(nears):
        for slot, ref in enumerate((f0, f1, f2, f3)):
            far[place[0] ^ slot] = ref[slide]
        by_parity = [[], []]
        for head in range(4):
            own = head & 1
            there = far[head]
            far_total = joined(there[48:51])
            near_total = near[head, 0, 48:49]
            top = jnp.maximum(far_total, near_total)
            total = top + jnp.log2(jnp.exp2(far_total - top) + jnp.exp2(near_total - top))
            both = there[0:48].astype(F32) * jnp.exp2(far_total - total) + near[
                head, 0, 0:48
            ] * jnp.exp2(near_total - total)
            kept[slide, head, own] = jnp.concatenate([both, rows_of((8, width), 0, [total])], 0)
            kept[slide, head, 1 - own] = near[head, 1]
            by_parity[own].append(both)
            by_parity[1 - own].append(near[head, 1, 0:48])
        for parity in range(2):
            turned = padded_turn(jnp.concatenate(by_parity[parity], 0))[:, 0:192].astype(BF)
            for block in range(4):
                rows = slice(block * width // 8, (block + 1) * width // 8)
                stay[slide, parity, block] = turned[rows]
                rows = slice((block + 4) * width // 8, (block + 5) * width // 8)
                send[slide, parity, block] = turned[rows]


def gradient_rows_kernel(place, first, second, kept, *refs):
    near, s0, s1, s2, s3 = refs[-5:]
    half = first.shape[2]
    width = kept.shape[-1]
    for parity in range(2):
        turned = jnp.concatenate(
            [
                jnp.concatenate([ref[0, parity], jnp.zeros((half, 64), BF)], 1).T
                for ref in (first, second)
            ],
            1,
        )
        for head in range(4):
            part = turned[head * 48 : (head + 1) * 48]
            inner = jnp.sum(part.astype(F32) * kept[0, head, parity, 0:48], axis=0, keepdims=True)
            total = kept[0, head, parity, 48:49]
            rows = [piece.astype(F32) for piece in split3(total) + split3(inner)]
            ending = rows_of((16, width), 0, rows).astype(BF)
            near[0, head, parity] = jnp.concatenate([part, ending], 0)
    for slot, ref in enumerate((s0, s1, s2, s3)):
        head = place[0] ^ slot
        ref[0] = near[0, head, head & 1]


def negated_total(grad_block, base):
    tail = grad_block[48:64].astype(F32)
    row = lax.broadcasted_iota(jnp.int32, base.shape, 0)
    out = base.astype(F32)
    for index in range(3):
        out = jnp.where(row == 15 + index, -tail[index : index + 1], out)
    return out.astype(BF)


def gradient_aug(grad_block):
    width = grad_block.shape[-1]
    tail = grad_block[48:64].astype(F32)
    rows = rows_of((16, width), 0, [-tail[index : index + 1] for index in (3, 4, 5)])
    return jnp.concatenate([grad_block[0:48], rows.astype(BF)], 0)


def pair_block(key_aug, value_aug, queries, grads):
    probs = jnp.exp2(dot(key_aug, queries))
    slopes = (probs * dot(value_aug, grads)).astype(BF)
    return probs.astype(BF), slopes


def near_backward_kernel(
    place, qkv, valid, grad, out, key_aug, key_t, value_aug, q_aug, g_aug, q_nat, g_nat,
    *, slide, factor, scale,
):
    width = qkv.shape[-1]
    own = lax.rem(pl.program_id(0), 2)
    ones = rows_between((META, width), 0, 3)
    for role in range(2):
        parity = own if role == 0 else 1 - own
        block = qkv[0, 0, parity]
        given = grad[0, 0, parity]
        there = valid[place[1] * 3 + slide, pl.ds(place[0] * 2 + parity, 1)]
        key_aug[role] = key_rows(block[48:96], near_key_meta(there)).T
        key_t[role] = plain64(block[48:96])
        value_aug[role] = padded_turn(ones_below(block[96:144], 3))[:, 0:64]
        q_aug[role] = query_rows(block[0:48], negated_total(given, ones), factor)
        g_aug[role] = gradient_aug(given)
        q_nat[role] = padded_turn(plain64(block[0:48]))[:, 0:64]
        g_nat[role] = padded_turn(plain64(given[0:48]))[:, 0:64]
    dq = [None, None]
    for key_role, users in ((0, (1,)), (1, (0, 1))):
        dk = None
        dv = None
        for role in users:
            probs, slopes = pair_block(
                key_aug[key_role], value_aug[key_role], q_aug[role], g_aug[role]
            )
            add_v = dot(probs, g_nat[role])
            add_k = dot(slopes, q_nat[role])
            add_q = dot(key_t[key_role], slopes)
            dv = add_v if dv is None else dv + add_v
            dk = add_k if dk is None else dk + add_k
            dq[role] = add_q if dq[role] is None else dq[role] + add_q
        parity = own if key_role == 0 else 1 - own
        out[0, parity, 48:96] = (turned_out(dk) * scale).astype(BF)
        out[0, parity, 96:144] = turned_out(dv).astype(BF)
    for role in range(2):
        parity = own if role == 0 else 1 - own
        out[0, parity, 0:48] = (dq[role][0:48] * scale).astype(BF)


def far_backward_kernel(
    place, b0, b1, b2, b3, g0, g1, g2, g3, valid, o0, o1, o2, o3,
    key_aug, key_t, value_aug, q_same, q_other, g_aug, q_nat, g_nat, dq, out,
    *, first_slide, half, factor, scale,
):
    width = b0.shape[-1]
    slide = first_slide + pl.program_id(0)
    level = far_levels(place, width, half)
    tail = far_tables(level)
    same, other = far_queries(level)
    for slot, (block, given) in enumerate(((b0, g0), (b1, g1), (b2, g2), (b3, g3))):
        grad = given[0]
        row = (place[0] ^ slot) * 2 + (place[0] & 1)
        there = valid[place[1] * 3 + slide, pl.ds(row, 1)]
        key_aug[slot] = key_rows(block[0, 48:96], (tail + bias_rows(there)).astype(BF)).T
        key_t[slot] = plain64(block[0, 48:96])
        value_aug[slot] = padded_turn(ones_below(block[0, 96:144], 3))[:, 0:64]
        q_same[slot] = query_rows(block[0, 0:48], negated_total(grad, same), factor)
        q_other[slot] = query_rows(block[0, 0:48], negated_total(grad, other), factor)
        g_aug[slot] = gradient_aug(grad)
        q_nat[slot] = padded_turn(plain64(block[0, 0:48]))[:, 0:64]
        g_nat[slot] = padded_turn(plain64(grad[0:48]))[:, 0:64]
    dq[...] = jnp.zeros_like(dq)

    def step(slot, carry):
        dk = None
        dv = None
        for shift in range(4):
            there = lax.rem(slot + shift, 4)
            queries = q_same[there] if shift == 0 else q_other[there]
            probs, slopes = pair_block(key_aug[slot], value_aug[slot], queries, g_aug[there])
            add_v = dot(probs, g_nat[there])
            add_k = dot(slopes, q_nat[there])
            dv = add_v if dv is None else dv + add_v
            dk = add_k if dk is None else dk + add_k
            dq[there] += dot(key_t[slot], slopes)
        out[slot, 48:96] = (turned_out(dk) * scale).astype(BF)
        out[slot, 96:144] = turned_out(dv).astype(BF)
        return carry

    lax.fori_loop(0, 4, step, 0)
    for slot, ref in enumerate((o0, o1, o2, o3)):
        ref[0] = out[slot]
        ref[0, 0:48] = (dq[slot, 0:48] * scale).astype(BF)


def qkv_backward_kernel(place, *refs, count, begins, ends):
    refs = list(refs)
    nears = [refs.pop(0) for _ in range(count)]
    fars = [[refs.pop(0) for _ in range(4)] for _ in range(count)]
    first, second, weight, gains = [refs.pop(0) for _ in range(4)]
    before = [] if begins else [refs.pop(0) for _ in range(3)]
    wgrads = [refs.pop(0) for _ in range(2 if ends else 1)]
    bias_sum, ln_sum, stay, send, far = refs[:5]
    acc = refs[5] if ends else wgrads[0]
    if begins:
        for ref in (acc, bias_sum, ln_sum):
            ref[...] = jnp.zeros_like(ref)
    else:
        for ref, old in zip((acc, bias_sum, ln_sum), before):
            ref[...] = old[...]
    half = first.shape[2]
    piece_rows = half // 4
    gain_row = jnp.zeros((1, gains.shape[1]), F32)
    bias_row = jnp.zeros((1, gains.shape[1]), F32)
    ones = jnp.ones((8, 2 * half), BF)
    for slide, near in enumerate(nears):
        for slot, ref in enumerate(fars[slide]):
            far[place[0] ^ slot] = ref[0]
        for parity in range(2):
            pieces = []
            for head in range(4):
                piece = near[head, parity]
                if head & 1 == parity:
                    piece = (piece.astype(F32) + far[head].astype(F32)).astype(BF)
                pieces.append(piece)
            total = jnp.concatenate(pieces, 0)
            bias_sum[...] += dot_nt(ones, total)
            turned = padded_turn(total)[:, 0 : total.shape[0]]
            for part, ref, out in ((0, first, stay), (1, second, send)):
                xhat = ref[slide, parity]
                here = slice(part * half, (part + 1) * half)
                acc[...] += dot(total[:, here], normed_of(xhat, gains))
                back = dot(turned[here], weight[...])
                low = back.astype(BF)
                for block in range(4):
                    out[slide, parity, block] = low[block * piece_rows : (block + 1) * piece_rows]
                gain_row = gain_row + jnp.sum(back * xhat.astype(F32), axis=0, keepdims=True)
                bias_row = bias_row + jnp.sum(back, axis=0, keepdims=True)
    ln_sum[...] += rows_of(ln_sum.shape, 0, [gain_row, bias_row])
    if ends:
        missing = wgrads[0].shape[1] - acc.shape[0]
        full = jnp.concatenate([acc[...], jnp.zeros((missing, acc.shape[1]), F32)], 0)
        turned = full.T.astype(BF)
        rows = turned.shape[0] // 8
        for index in range(8):
            part = turned[index * rows : (index + 1) * rows]
            where = slice(index // 2 * rows, (index // 2 + 1) * rows)

            @pl.when(place[1] == index % 2)
            def _():
                wgrads[0][where] = part

            @pl.when(place[1] != index % 2)
            def _():
                wgrads[1][where] = part


def exit_kernel(place, first, second, base, grad_mid, out_rows, gains, *refs):
    tiles_grad, output = refs[-2:]
    rows = base.shape[2]
    half = rows // 2
    xhat, rate = moments(base[0, 0])
    side = pl.program_id(0)
    upstream = jnp.concatenate(
        [jnp.where(side == 0, first[0, part], second[0, part]) for part in range(2)], 0
    ).astype(F32)
    grad = grad_mid[0, 0] + norm_back(xhat, rate, gains[0:1], upstream)
    undo = parity_order(rows, True)
    tiles_grad[0] = dot(undo, grad.astype(BF)).astype(BF)
    output[0] = dot(undo, out_rows[0, 0]).astype(BF)


def mlp_kernel(
    place, base, own, other, cot, w1, w2, wo0, wo1, wo2, wo3, offset, small,
    output, grad_mid, grad_own, grad_other, hidden_out, g_pre_out, normed_t, cot_t, attn_t,
    merged_out, sums, fc1_sum,
    w_out, mid, merged, normed, ff, back,
):
    step = pl.program_id(0)
    rows, width = mid.shape
    part = 256
    half = part // 4

    def cot_at(first):
        slide = first // part
        return jnp.concatenate([cot[0, slide], cot[1, slide]], 0)

    @pl.when(step == 0)
    def _():
        for index, ref in enumerate((wo0, wo1, wo2, wo3)):
            w_out[index * 192 : (index + 1) * 192] = ref[0]
        for first in range(0, rows, part):
            here = pl.ds(first, part)
            slide = first // part
            for side, ref in enumerate((own, other)):
                for parity in range(2):
                    at = first + (2 * side + parity) * half
                    merged[at : at + half] = ref[slide, parity]
            value = jnp.concatenate([base[0, slide], base[1, slide]], 0)
            value = value + (dot(merged[here], w_out[...]) + small[0:1])
            mid[here] = value
            xhat, _ = moments(value)
            low = (xhat * small[1:2] + small[2:3]).astype(BF)
            normed[here] = low
            normed_t[:, first : first + part] = low.T
            cot_t[:, first : first + part] = cot_at(first).T
        for index, slot in enumerate(SLOT_ORDER):
            merged_out[slot] = merged[:, index * 192 : (index + 1) * 192]

    shift = joined(offset[0, 0:3])
    fc1 = jnp.zeros((1, width), F32)
    for first in range(0, rows, part):
        here = pl.ds(first, part)
        pre = dot(normed[here], w1[0]) + shift
        cdf = 0.5 * (1.0 + lax.erf(pre * math.sqrt(0.5)))
        hidden = (pre * cdf).astype(BF)
        slope = cdf + pre * (jnp.exp(-0.5 * pre * pre) * (1.0 / math.sqrt(2.0 * math.pi)))
        g_pre = (dot_nt(cot_at(first), w2[0]) * slope).astype(BF)
        hidden_out[0, here] = hidden
        g_pre_out[0, here] = g_pre
        add_ff = dot(hidden, w2[0])
        add_back = dot_nt(g_pre, w1[0])

        @pl.when(step == 0)
        def _():
            ff[here] = add_ff
            back[here] = add_back

        @pl.when(step != 0)
        def _():
            ff[here] += add_ff
            back[here] += add_back

        fc1 = fc1 + jnp.sum(g_pre.astype(F32), axis=0, keepdims=True)
    fc1_sum[0] = jnp.broadcast_to(fc1, (8, width))

    @pl.when(step == pl.num_programs(0) - 1)
    def _():
        totals = [jnp.zeros((1, width), F32)] * 4
        for first in range(0, rows, part):
            here = pl.ds(first, part)
            slide = first // part
            value = mid[here]
            result = (value + (ff[here] + small[3:4])).astype(BF)
            xhat, rate = moments(value)
            upstream = back[here]
            cot_wide = cot_at(first).astype(F32)
            grad = cot_wide + norm_back(xhat, rate, small[1:2], upstream)
            low = grad.astype(BF)
            back_rows = dot_nt(low, w_out[...]).astype(BF)
            for side, ref in enumerate((grad_own, grad_other)):
                output[side, slide] = result[2 * side * half : 2 * (side + 1) * half]
                grad_mid[side, slide] = grad[2 * side * half : 2 * (side + 1) * half]
                for parity in range(2):
                    at = (2 * side + parity) * half
                    ref[slide, parity, 0] = back_rows[at : at + half]
            attn_t[:, first : first + part] = low.T
            wide = low.astype(F32)
            for index, piece in enumerate((wide, upstream * xhat, upstream, cot_wide)):
                totals[index] = totals[index] + jnp.sum(piece, axis=0, keepdims=True)
        sums[...] = rows_of((8, width), 0, totals)


def weight_grad_kernel(place, *refs, partner):
    groups = [refs[0:6], refs[6:12]]
    outs = refs[12 + 2 * partner :]
    width = refs[0].shape[0]
    piece = width // 8
    slot = pl.program_id(0)

    def rows(index):
        return slice(index // 2 * piece, (index // 2 + 1) * piece)

    def over(index, other):
        return sum(dot(group[index][...], group[other][0]) for group in groups)

    second = over(1, 4)
    for index in range(8):
        side = (index % 2) ^ place[1]
        part = second[index * piece : (index + 1) * piece]
        if not partner:
            outs[1][0, side, rows(index)] = part.astype(BF)
            continue
        part = (part + refs[13][0, side, rows(index)].astype(F32)).astype(BF)
        for here, ref in enumerate(outs[2:]):

            @pl.when(slot == here)
            def _():
                ref[side, rows(index)] = part

    rest = over(2, 5)
    missing = FIRST_COLUMNS - width - rest.shape[1]
    rest = jnp.concatenate([rest, jnp.zeros((width, missing), F32)], 1)
    for first, value in ((0, over(0, 3)), (width, rest)):
        columns = slice(first, first + value.shape[1])
        for index in range(8):
            part = value[index * piece : (index + 1) * piece]
            if not partner:
                outs[0][(index % 2) ^ place[1], 0, rows(index), columns] = part.astype(BF)
                continue
            for side, ref in enumerate(outs[:2]):

                @pl.when((index % 2) ^ place[1] == side)
                def _():
                    there = part + refs[12][side, 0, rows(index), columns].astype(F32)
                    ref[0, rows(index), columns] = there.astype(BF)


def side_fold_kernel(place, first, second, stay, send):
    total = (first[...].astype(F32) + second[...].astype(F32)).astype(BF)
    stay[...] = total[0]
    send[...] = total[1]


def z_fold_both_kernel(place, first, second, third, fourth, stay, send, total):
    columns = first.shape[1]
    total[:, :columns] = (first[...].astype(F32) + second[...].astype(F32)).astype(BF)
    total[:, columns:] = (third[...].astype(F32) + fourth[...].astype(F32)).astype(BF)
    z_halves(place, total, stay, send, True)


def hold_kernel(place, w1, w2, wo, offset, out):
    width = w1.shape[1]
    out[0:width] = w1[...]
    out[width : 2 * width] = w2[...]
    out[2 * width : 2 * width + wo.shape[0]] = wo[...]
    rows = [part.astype(F32) for part in split3(offset[...])]
    out[2 * width + wo.shape[0] :] = rows_of((16, width), 0, rows).astype(BF)


def whole(shape):
    return pl.BlockSpec(tuple(shape), lambda *_: (0,) * len(shape))


def shaped(shape, dtype):
    return jax.ShapeDtypeStruct(tuple(shape), dtype)


def run(name, body, place, ins, outs, grid=(1,), scratch=(), tokens=(), aliases=None, mib=48, us=5):
    arrays = [pair[0] for pair in ins]
    in_specs = [whole(a.shape) if s is None else s for a, s in ins]
    in_specs += [pl.BlockSpec(memory_space=pl.ANY)] * len(tokens)
    out_specs = [whole(o.shape) if s is None else s for o, s in outs]
    given, extra = len(ins), len(tokens)

    def kernel(place_ref, *refs):
        body(place_ref, *refs[:given], *refs[given + extra :])

    return pl.pallas_call(
        kernel,
        grid_spec=pltpu.PrefetchScalarGridSpec(
            num_scalar_prefetch=1,
            grid=grid,
            in_specs=in_specs,
            out_specs=out_specs,
            scratch_shapes=list(scratch),
        ),
        out_shape=[o for o, _ in outs],
        input_output_aliases={k + 1: v for k, v in (aliases or {}).items()},
        compiler_params=pltpu.CompilerParams(vmem_limit_bytes=mib * 1024 * 1024),
        cost_estimate=pl.CostEstimate(
            flops=int(COST * us * 1.1e9), transcendentals=0, bytes_accessed=int(COST * us * 3.6e6)
        ),
        name=name,
    )(place, *arrays, *tokens)


def swap(value, axis, bit):
    return lax.ppermute(value, axis, [(i, i ^ bit) for i in range(lax.axis_size(axis))])


def paired(body, given):
    def kernel(place, *refs):
        near, away = refs[given : given + 2]
        slots = (near.at[0], near.at[1], away.at[0], away.at[1])
        body(place, *refs[:given], *slots, *refs[given + 2 :])

    return kernel


def pair_kernel(place, near, away, out):
    out[0] = near[1]
    out[1] = away[1]


def nested(
    tiles,
    coords,
    lengths,
    padding_mask,
    ln1_gain,
    ln1_bias,
    query_key_value_weight,
    qv_bias,
    attention_output_weight,
    attention_output_bias,
    ln2_gain,
    ln2_bias,
    mlp_entry_matrix,
    mlp_entry_offset,
    feed_output_weight,
    feed_output_bias,
    cotangent,
):
    slides, rows, width = tiles.shape
    group = slides // 2
    half = rows // 2
    lanes = 8 * half
    mine = lanes // 2
    local = query_key_value_weight.shape[2]
    scale = 1.0 / math.sqrt(HEAD_DIM)
    factor = scale * LOG2E
    seq_index = lax.axis_index("seq")
    head_index = lax.axis_index("head")
    z, y = seq_index // 2, seq_index % 2
    x, core = head_index // 2, head_index % 2
    place = jnp.stack([z, y, x, core]).astype(jnp.int32)
    parts = ((0, 1), (1, group - 1))
    token = []

    def step(name, body, ins, outs, **options):
        made = run(name, body, place, ins, outs, tokens=list(token), **options)
        token[:] = [made[-1]]
        return made

    def vm(*shape, dtype=BF):
        return pltpu.VMEM(shape, dtype)

    def bf(*shape):
        return shaped(shape, BF)

    def f32(*shape):
        return shaped(shape, F32)

    def plain(*arrays):
        return [(array, None) for array in arrays]

    def lead_block(*shape):
        return pl.BlockSpec((1,) + shape, lambda k, p: (k,) + (0,) * len(shape))

    def over_z(pieces):
        return [(pieces[0], None)] + [(swap(pieces[k], "seq", 2 * k), None) for k in (1, 2, 3)]

    def over_z_first(pair):
        return pair[0], swap(pair[1], "seq", 4)

    def over_z_second(pair):
        near, away = pair
        send = step("pair", pair_kernel, plain(near, away), [(shaped(near.shape, BF), None)], us=SMALL_US)[0]
        got = swap(send, "seq", 2)
        return [(near, 0), (got, 0), (away, 0), (got, 1)]

    def by_slide(slots):
        out = []
        for array, index in slots:
            shape = array.shape[-2:]
            if index is None:
                out.append((array, lead_block(*shape)))
            else:
                out.append((array, pl.BlockSpec((None, 1) + shape, lambda k, p, i=index: (i, k, 0, 0))))
        return out

    def all_slides(slots):
        out = []
        for array, index in slots:
            if index is None:
                out.append((array, None))
            else:
                shape = array.shape[1:]
                out.append((array, pl.BlockSpec((None,) + shape, lambda k, p, i=index: (i, 0, 0, 0))))
        return out

    total_len = padding_mask.shape[1]
    positions = jnp.arange(total_len, dtype=jnp.int32)
    valid = (positions[None, :] < lengths[:, None]) & (padding_mask == 1)
    valid = valid.astype(BF).reshape(slides * 4, total_len // 4)
    spot = jnp.arange(total_len // 4, dtype=jnp.int32)
    lane = spot % lanes
    chip = lane // half
    there = (
        (y ^ (chip & 1)) * lanes
        + (x ^ ((chip >> 1) & 1)) * (lanes // 2)
        + (core ^ (chip >> 2)) * rows
        + 2 * (lane % half)
        + spot // lanes
    )
    taken = (spot[:, None] == there[None, :]).astype(BF)
    valid = jnp.einsum("rp,pl->rl", valid, taken, preferred_element_type=F32)
    valid = valid.reshape(slides, 8, lanes)

    weight = query_key_value_weight.reshape(width, 3, 4, HEAD_DIM).transpose(2, 1, 3, 0)
    weight = weight.reshape(3 * local, width)
    triple = jnp.stack([qv_bias[0], jnp.zeros_like(qv_bias[0]), qv_bias[1]])
    triple = triple.reshape(3, 4, HEAD_DIM).transpose(1, 0, 2).reshape(3 * local, 1)
    gains = jnp.concatenate([jnp.stack([ln1_gain, ln1_bias]), jnp.zeros((6, width), F32)], 0)
    small = jnp.concatenate(
        [
            jnp.stack([attention_output_bias, ln2_gain, ln2_bias, feed_output_bias]),
            jnp.zeros((4, width), F32),
        ],
        0,
    )
    quarter = width // 4
    freq = jnp.exp(-jnp.log(10000.0) * jnp.arange(quarter, dtype=F32) / quarter)
    angle = jnp.arange(256, dtype=F32)[:, None] * freq
    table = jnp.stack(split3(jnp.concatenate([jnp.sin(angle), jnp.cos(angle)], axis=-1)))

    bases, cots, blocks = [], [], []
    pending = []
    for first, count in parts:

        def at_side(side, depth, first=first):
            return pl.BlockSpec(
                (1, rows, depth), lambda k, p: ((p[1] ^ side) * group + first + k, 0, 0)
            )

        both = pl.BlockSpec((2, 1, rows, width), lambda k, p: (0, k, 0, 0))
        piece = pl.BlockSpec((1, 2, half, width), lambda k, p: (k, 0, 0, 0))
        pair = (2, count, rows, width)
        ins = []
        for array, depth in ((tiles, width), (coords, 2), (cotangent, width)):
            ins += [(array, at_side(0, depth)), (array, at_side(1, depth))]
        base, cot, own, other = step(
            "entry",
            entry_kernel,
            ins + plain(table),
            [
                (f32(*pair), both),
                (bf(*pair), both),
                (bf(count, 2, half, width), piece),
                (bf(count, 2, half, width), piece),
            ],
            grid=(count,),
            us=2.2 * count,
        )
        bases.append(base)
        cots.append(cot)
        shape = (count, 2, 1, half, width)
        pending.append((own.reshape(shape), swap(other, "seq", 1).reshape(shape)))

    def join(first, second):
        shape = first.shape[:2] + (2 * first.shape[2],) + first.shape[3:]
        return step("join", join_kernel, plain(first, second), [(shaped(shape, BF), None)], us=1)[0]

    pending = [join(*pair) for pair in pending]
    pending = [(block, swap(block, "head", 2)) for block in pending]

    qkvs, far_blocks = [None, None], [None, None]
    near_outs, near_grads = [None] * group, [None] * group

    def project(g):
        first, count = parts[g]
        outs = step(
            "qkv",
            qkv_kernel,
            [(blocks[g][0], lead_block(2, mine, width)), (blocks[g][1], lead_block(2, mine, width))]
            + plain(weight, triple, gains),
            [(bf(count, 4, 2, TRIPLE, lanes), lead_block(4, 2, TRIPLE, lanes))]
            + [(bf(count, TRIPLE, lanes), lead_block(TRIPLE, lanes))] * 4,
            grid=(count,),
            us=2.2 * count,
        )
        qkvs[g] = outs[0]
        far_blocks[g] = over_z(outs[1:])

    def spread_columns(g):
        block = join(*pending[g])
        shape = (parts[g][1], 2, mine, width)
        blocks.append((block.reshape(shape), swap(block, "head", 1).reshape(shape)))

    def head_block(k, height):
        return pl.BlockSpec((1, 1, 2, height, lanes), lambda i, p: (k, i, 0, 0, 0))

    def each_head(height):
        return pl.BlockSpec((1, 2, height, lanes), lambda i, p: (i, 0, 0, 0))

    def near_forward(g, k):
        slide = parts[g][0] + k
        near_outs[slide] = step(
            "near_forward",
            partial(near_forward_kernel, slide=slide, factor=factor),
            [(qkvs[g], head_block(k, TRIPLE)), (valid, None)],
            [(f32(4, 2, ACC_ROWS, lanes), each_head(ACC_ROWS))],
            grid=(4,),
            scratch=[vm(2, lanes, AUG), vm(2, OUT_ROWS, lanes), vm(2, lanes, lanes, dtype=F32)],
            us=NEAR_US,
        )[0]

    far_outs, kept, merged = [None, None], [None, None], [None, None]

    def far_kernel(name, body, g, ins, height, scratch, two_steps, us, **options):
        first, count = parts[g]
        body = partial(body, first_slide=first, half=half, factor=factor, **options)
        if two_steps:
            body = paired(body, len(ins))
            block = pl.BlockSpec((2, 1, height, lanes), lambda k, p: (0, k, 0, 0))
            outs = [(bf(2, count, height, lanes), block)] * 2
        else:
            outs = [(bf(count, height, lanes), lead_block(height, lanes))] * 4
        outs = step(name, body, ins, outs, grid=(count,), scratch=scratch, us=us * count)
        return over_z_first(outs) if two_steps else over_z(outs)

    def far_forward(g, two_steps):
        far_outs[g] = far_kernel(
            "far_forward",
            far_forward_kernel,
            g,
            by_slide(far_blocks[g]) + plain(valid),
            OUT_ROWS,
            [
                vm(4, lanes, AUG),
                vm(4, OUT_ROWS, lanes),
                vm(4, AUG, lanes),
                vm(4, AUG, lanes),
                vm(4, lanes, lanes, dtype=F32),
                vm(4, OUT_ROWS, lanes),
            ],
            two_steps,
            8,
        )

    def merge(g):
        first, count = parts[g]
        turned = bf(count, 2, 4, half, local)
        kept[g], stay, send = step(
            "merge",
            merge_kernel,
            plain(*near_outs[first : first + count]) + all_slides(far_outs[g]),
            [(f32(count, 4, 2, ACC_ROWS, lanes), None), (turned, None), (turned, None)],
            scratch=[vm(4, OUT_ROWS, lanes)],
            us=count,
        )
        merged[g] = (stay, swap(send, "head", 1))

    def widen(g, axis, bit):
        pieces = [(a, None) for a in merged[g]]
        count, _, blocks_here, _, columns = merged[g][0].shape
        shape = bf(count, 2, blocks_here // 2, half, 2 * columns)
        stay, send = step("widen", widen_kernel, pieces, [(shape, None)] * 2, us=1)
        merged[g] = (stay, swap(send, axis, bit))

    spread_columns(0)
    project(0)
    near_forward(0, 0)
    far_forward(0, True)
    spread_columns(1)
    packed = step(
        "hold",
        hold_kernel,
        plain(
            mlp_entry_matrix,
            feed_output_weight,
            attention_output_weight,
            mlp_entry_offset[None],
        ),
        [(bf(2 * width + local + 16, width), None)],
        us=2,
    )[0]
    packed = lax.all_gather(packed, "head")
    project(1)
    near_forward(1, 0)
    far_outs[0] = over_z_second(far_outs[0])
    near_forward(1, 1)
    merge(0)
    far_forward(1, False)
    widen(0, "head", 2)

    def last_widen(g):
        first, second = merged[g]
        count = first.shape[0]
        shape = bf(count, 2, 1, half, width)
        stay, send = step("widen", widen_kernel, plain(first, second), [(shape, None)] * 2, us=1)
        shape = (count, 2, half, width)
        merged[g] = (stay.reshape(shape), swap(send, "seq", 1).reshape(shape))

    last_widen(0)
    merge(1)
    widen(1, "head", 2)
    last_widen(1)

    def head_of(i, p):
        return (p[2] ^ (i % 2)) * 2 + (p[3] ^ (i // 2))

    def weight_spec(height, index, slot=None):
        if slot is None:
            return pl.BlockSpec((1, height, width), lambda i, p: (head_of(i, p), index, 0))
        return pl.BlockSpec((1, height, width), lambda i, p: (head_of(slot, p), index, 0))

    def slot_block(*shape):
        return pl.BlockSpec((1,) + shape, lambda i, p: (i,) + (0,) * len(shape))

    owned, given, grads = [None, None], [None, None], [None, None]

    def feed_forward(g):
        count = parts[g][1]
        here = 2 * count * rows
        pair = (2, count, rows, width)
        turned = bf(width, here)
        piece = bf(count, 2, 1, half, width)
        outs = step(
            "mlp",
            mlp_kernel,
            plain(bases[g], *merged[g], cots[g])
            + [(packed, weight_spec(width, 0)), (packed, weight_spec(width, 1))]
            + [(packed, weight_spec(local, 2 * width // local, slot)) for slot in SLOT_ORDER]
            + [(packed, weight_spec(16, (2 * width + local) // 16)), (small, None)],
            [
                (bf(*pair), None),
                (f32(*pair), None),
                (piece, None),
                (piece, None),
                (bf(4, here, width), slot_block(here, width)),
                (bf(4, here, width), slot_block(here, width)),
                (turned, None),
                (turned, None),
                (turned, None),
                (bf(4, here, local), None),
                (f32(8, width), None),
                (f32(4, 8, width), slot_block(8, width)),
            ],
            grid=(4,),
            scratch=[
                vm(width, width),
                vm(here, width, dtype=F32),
                vm(here, width),
                vm(here, width),
                vm(here, width, dtype=F32),
                vm(here, width, dtype=F32),
            ],
            mib=60,
            us=5 + 10 * count,
        )
        output, grad_mid, own, other, hidden, g_pre, normed_t, cot_t, attn_t, slots, sums, fc1 = outs
        owned[g] = (output, grad_mid, sums, fc1)
        grads[g] = (normed_t, cot_t, attn_t, g_pre, hidden, slots)
        given[g] = (own, swap(other, "seq", 1))

    def narrow(g, axis, bit):
        first, second = given[g]
        count, _, blocks_here, _, columns = first.shape
        shape = bf(count, 2, 2 * blocks_here, half, columns // 2)
        stay, send = step("narrow", narrow_kernel, plain(first, second), [(shape, None)] * 2, us=1)
        given[g] = (stay, swap(send, axis, bit))

    feed_forward(0)
    feed_forward(1)

    tall = width // 2
    sent = [
        (bf(2, 2, tall, FIRST_COLUMNS), pl.BlockSpec((2, 1, tall, FIRST_COLUMNS), lambda i, p: (0, i, 0, 0))),
        (bf(2, 2, tall, width), pl.BlockSpec((1, 2, tall, width), lambda i, p: (i, 0, 0, 0))),
    ]
    kept_w = [(bf(2, tall, FIRST_COLUMNS), slot_block(tall, FIRST_COLUMNS))] * 2
    kept_w += [(bf(2, tall, width), None)] * 2

    def weight_grads(first, partner):
        def at(*shape):
            return pl.BlockSpec((1,) + shape, lambda i, p: (i + first, 0, 0))

        ins = []
        for (_, count), (normed_t, cot_t, attn_t, g_pre, hidden, slots) in zip(parts, grads):
            here = 2 * count * rows
            ins += plain(normed_t, cot_t, attn_t)
            ins += [(g_pre, at(here, width)), (hidden, at(here, width)), (slots, at(here, local))]
        return step(
            "weight_grads",
            partial(weight_grad_kernel, partner=len(partner) // 2),
            ins + [(value, spec) for value, (_, spec) in zip(partner, sent)],
            kept_w if partner else sent,
            grid=(2,),
            mib=56,
            us=WG_US,
        )

    def split_fold(pair, axis, bit):
        shape = pair[0].shape[1:]
        stay, send = step(
            "split_fold", side_fold_kernel, plain(*pair), [(shaped(shape, BF), None)] * 2, us=2
        )
        return stay, swap(send, axis, bit)

    grad_rows, far_grads, far_backs = [None, None], [None, None], [None] * group
    backs, sums_so_far = [None, None], []

    def rows_of_gradients(g):
        first, count = parts[g]
        pieces = [value.reshape(count, 2, mine, local) for value in given[g]]
        slot = pl.BlockSpec((1, OUT_ROWS, lanes), lambda k, p: (first + k, 0, 0))
        any_spec = pl.BlockSpec(memory_space=pl.ANY)
        before = [(array, any_spec) for array in far_grads[0] or []]
        outs = step(
            "gradient_rows",
            gradient_rows_kernel,
            [(value, lead_block(2, mine, local)) for value in pieces]
            + [(kept[g], lead_block(4, 2, ACC_ROWS, lanes))]
            + before,
            [(bf(count, 4, 2, OUT_ROWS, lanes), lead_block(4, 2, OUT_ROWS, lanes))]
            + [(bf(group, OUT_ROWS, lanes), slot)] * 4,
            grid=(count,),
            aliases={3 + k: 1 + k for k in range(4)} if before else None,
            us=count,
        )
        grad_rows[g] = outs[0]
        far_grads[0] = outs[1:] if first == 0 else over_z(outs[1:])

    def near_backward(g, k, us=9.7):
        slide = parts[g][0] + k
        near_grads[slide] = step(
            "near_backward",
            partial(near_backward_kernel, slide=slide, factor=factor, scale=scale),
            [(qkvs[g], head_block(k, TRIPLE)), (valid, None), (grad_rows[g], head_block(k, OUT_ROWS))],
            [(bf(4, 2, TRIPLE, lanes), each_head(TRIPLE))],
            grid=(4,),
            scratch=[
                vm(2, lanes, AUG),
                vm(2, OUT_ROWS, lanes),
                vm(2, lanes, OUT_ROWS),
                vm(2, AUG, lanes),
                vm(2, OUT_ROWS, lanes),
                vm(2, lanes, OUT_ROWS),
                vm(2, lanes, OUT_ROWS),
            ],
            us=us,
        )[0]

    def far_backward(g, k):
        slide = parts[g][0] + k
        blocks_here = []
        for array, index in far_blocks[g]:
            shape = array.shape[-2:]
            if index is None:
                spec = pl.BlockSpec((1,) + shape, lambda i, p: (k, 0, 0))
            else:
                spec = pl.BlockSpec((None, 1) + shape, lambda i, p, n=index: (n, k, 0, 0))
            blocks_here.append((array, spec))
        grads_here = [
            (array, pl.BlockSpec((1, OUT_ROWS, lanes), lambda i, p: (slide, 0, 0)))
            for array, _ in far_grads[0]
        ]
        ins = blocks_here + grads_here + plain(valid)
        body = partial(
            far_backward_kernel, first_slide=slide, half=half, factor=factor, scale=scale
        )
        outs = step(
            "far_backward",
            paired(body, len(ins)),
            ins,
            [(bf(2, 1, TRIPLE, lanes), None)] * 2,
            scratch=[
                vm(4, lanes, AUG),
                vm(4, OUT_ROWS, lanes),
                vm(4, lanes, OUT_ROWS),
                vm(4, AUG, lanes),
                vm(4, AUG, lanes),
                vm(4, OUT_ROWS, lanes),
                vm(4, lanes, OUT_ROWS),
                vm(4, lanes, OUT_ROWS),
                vm(4, OUT_ROWS, lanes, dtype=F32),
                vm(4, TRIPLE, lanes),
            ],
            us=FA_US,
        )
        far_backs[slide] = over_z_first(outs)

    def project_back(g, ends):
        first, count = parts[g]
        begins = not ends
        if ends:
            wgrads = [(bf(width // 2, 3 * local + 64), None)] * 2
        else:
            wgrads = [(f32(3 * local, width), None)]
        back = bf(count, 2, 4, half, width)
        outs = step(
            "qkv_backward",
            partial(qkv_backward_kernel, count=count, begins=begins, ends=ends),
            plain(*near_grads[first : first + count])
            + [slot for slide in range(first, first + count) for slot in all_slides(far_backs[slide])]
            + plain(*blocks[g], weight, gains, *sums_so_far),
            wgrads + [(f32(8, 3 * local), None), (f32(8, width), None), (back, None), (back, None)],
            scratch=[vm(4, TRIPLE, lanes)] + ([vm(3 * local, width, dtype=F32)] if ends else []),
            us=2 + 4 * count,
        )
        sums_so_far[:] = outs[:-2]
        backs[g] = (outs[-2], swap(outs[-1], "head", 1))

    def fold_back(g, axis, bit):
        first, second = backs[g]
        count, _, blocks_here, _, _ = first.shape
        shape = bf(count, 2, blocks_here // 2, half, width)
        stay, send = step("fold", fold_kernel, plain(first, second), [(shape, None)] * 2, us=SMALL_US)
        backs[g] = (stay, swap(send, axis, bit))

    results = []

    def leave(g):
        first, count = parts[g]
        output, grad_mid = owned[g][:2]
        pieces = [value.reshape(count, 2, half, width) for value in backs[g]]
        piece = pl.BlockSpec((1, 2, half, width), lambda s, k, p: (k, 0, 0, 0))
        row = pl.BlockSpec((1, 1, rows, width), lambda s, k, p: (s, k, 0, 0))
        out = pl.BlockSpec((1, rows, width), lambda s, k, p: ((p[1] ^ s) * group + first + k, 0, 0))
        any_spec = pl.BlockSpec(memory_space=pl.ANY)
        results[:] = step(
            "leave",
            exit_kernel,
            [(value, piece) for value in pieces]
            + [(bases[g], row), (grad_mid, row), (output, row), (gains, None)]
            + [(value, any_spec) for value in results],
            [(bf(*tiles.shape), out)] * 2,
            grid=(2, count),
            aliases={6: 0, 7: 1} if results else None,
            us=1 + 1.3 * count,
        )

    def z_fold(pair, nearest):
        first, second = pair
        shape = bf(first.shape[0] // 2, first.shape[1])
        stay, send = step(
            "z_fold",
            partial(z_fold_kernel, nearest=nearest),
            plain(first, second),
            [(shape, None)] * 2,
            scratch=[vm(*first.shape)],
            us=SMALL_US,
        )
        return stay, swap(send, "seq", 2 if nearest else 4)

    def small_step(name, body, pair, bit=None):
        height = 8 if bit is None else 16
        made = step(name, body, plain(*pair), [(f32(height, width), None)], us=SMALL_US)[0]
        return made if bit is None else (made, swap(made, "seq", bit))

    narrow(0, "head", 2)
    sent_w = weight_grads(2, [])
    narrow(0, "head", 1)
    narrow(1, "head", 2)
    rows_of_gradients(0)
    near_backward(0, 0)
    narrow(1, "head", 1)
    rows_of_gradients(1)
    outs = weight_grads(0, [swap(value, "head", 1) for value in sent_w])
    first_w = (outs[0], swap(outs[1], "seq", 1))
    second_w = (outs[2], swap(outs[3], "head", 2))
    near_backward(1, 0, NB_US)
    far_backward(1, 0)
    far_backward(1, 1)
    second_w = split_fold(second_w, "seq", 1)
    first_w = split_fold(first_w, "head", 2)
    far_backward(0, 0)
    far_backs[1] = over_z_second(far_backs[1])
    far_backs[2] = over_z_second(far_backs[2])
    near_backward(1, 1, NB_US)
    stay, send = step(
        "z_fold_both",
        z_fold_both_kernel,
        plain(*first_w, *second_w),
        [(bf(tall // 2, FIRST_COLUMNS + width), None)] * 2,
        scratch=[vm(tall, FIRST_COLUMNS + width)],
        us=2,
    )
    folded = (stay, swap(send, "seq", 2))
    far_backs[0] = over_z_second(far_backs[0])
    project_back(1, False)
    project_back(0, True)
    stay, send, bias_sum, ln_sum = sums_so_far
    grad_in = (stay, swap(send, "seq", 1))
    stay, send = step(
        "small_start",
        small_start_kernel,
        plain(*[owned[g][2] for g in range(2)], *[owned[g][3] for g in range(2)], ln_sum, bias_sum),
        [(f32(16, width), None), (f32(8, width), None)],
        us=SMALL_US,
    )
    common = (stay, swap(send, "head", 1))
    fold_back(1, "head", 2)
    fold_back(0, "head", 2)
    common = small_step("small_first", small_first_kernel, common, 2)
    common = small_step("add", add_kernel, common, 4)
    common = small_step("add", add_kernel, common, 1)
    folded = z_fold(folded, False)
    grad_in = z_fold(grad_in, True)
    fold_back(1, "seq", 1)
    fold_back(0, "seq", 1)
    grad_in = z_fold(grad_in, False)
    stay, send = step(
        "small_middle", small_middle_kernel, plain(*common), [(f32(8, width), None)] * 2, us=SMALL_US
    )
    common = (stay, swap(send, "head", 2))
    w_fc1_grad, w_fc2_grad, w_out_grad = step(
        "weights_out",
        weights_out_kernel,
        plain(*folded),
        [
            (f32(width // 8, width), None),
            (f32(width, width // 8), None),
            (f32(local, width // 8), None),
        ],
        us=1.5,
    )
    leave(1)
    w_qkv_grad = step(
        "qkv_out",
        qkv_out_kernel,
        plain(*grad_in),
        [(f32(width // 8, 3, local), None)],
        us=1.5,
    )[0]
    common = small_step("add", add_kernel, common)
    leave(0)
    per_head = common[7, : 3 * local].reshape(4, 3, HEAD_DIM).transpose(1, 0, 2).reshape(3, local)
    tiles_grad, output = results
    return (
        output,
        tiles_grad,
        common[4],
        common[5],
        w_qkv_grad,
        jnp.stack([per_head[0], per_head[2]]),
        w_out_grad,
        common[0],
        common[1],
        common[2],
        w_fc1_grad,
        common[6],
        w_fc2_grad,
        common[3],
    )


def nests(mesh, tiles, padding_mask):
    sizes = (mesh.shape["seq"], mesh.shape["head"], tiles.shape[0])
    return sizes == (8, 4, 6) and padding_mask.shape[1] <= SEG2


def solution(mesh):
    def program(*args):
        one_span = nests(mesh, args[0], args[3])
        return spread_out(mesh, nested if one_span else on_device)(*args)

    return program


def spread_out(mesh, body):
    placed = (
        P(None, ("seq", "head"), None),
        P(None, ("seq", "head"), None),
        P(),
        P(),
        P(),
        P(),
        P(None, None, "head"),
        P(None, "head"),
        P("head", None),
        P(),
        P(),
        P(),
        P(None, "head"),
        P("head"),
        P("head", None),
        P(),
        P(None, ("seq", "head"), None),
    )
    return jax.shard_map(
        body,
        mesh=mesh,
        in_specs=placed,
        out_specs=(
            P(None, ("seq", "head"), None),
            P(None, ("seq", "head"), None),
            P(),
            P(),
            P("seq", None, "head"),
            P(None, "head"),
            P("head", "seq"),
            P(),
            P(),
            P(),
            P("seq", "head"),
            P("head"),
            P("head", "seq"),
            P(),
        ),
        check_vma=False,
    )
```

```python
from functools import partial
import math

import jax
import jax.numpy as jnp
import ml_dtypes
import numpy as np
from jax import lax
from jax.experimental import pallas as pl
from jax.experimental.pallas import tpu as pltpu
from jax.sharding import PartitionSpec as P

HEADS = 16
FF = 3072
SEG2 = 5792
RATIO = 16


NEG = -10000.0
FLOOR = -1e30
EPS = 1e-05


def partner(x, axis, stride):
    return lax.ppermute(x, axis, [(i, i ^ 1 << stride) for i in range(lax.axis_size(axis))])


def layer_norm(value, gain, shift):
    mean = jnp.mean(value, axis=-1, keepdims=True)
    centered = value - mean
    var = jnp.mean(centered * centered, axis=-1, keepdims=True)
    return centered * lax.rsqrt(var + EPS) * gain + shift


def position_table(coords, width):
    quarter = width // 4
    freq = jnp.exp(-jnp.log(10000.0) * jnp.arange(quarter, dtype=jnp.float32) / quarter)
    col_angle = coords[..., 0:1].astype(jnp.float32) * freq
    row_angle = coords[..., 1:2].astype(jnp.float32) * freq
    return jnp.concatenate(
        [jnp.sin(col_angle), jnp.cos(col_angle), jnp.sin(row_angle), jnp.cos(row_angle)], axis=-1
    )


def mask_shape(value, chosen):
    return (1, 1, chosen.shape[0]) + (1,) * (value.ndim - 4) + (chosen.shape[1], 1)


def pick(value, chosen):
    rate = chosen.shape[0]
    split = value.reshape((value.shape[0], value.shape[1] // rate, rate) + value.shape[2:])
    return jnp.sum(
        jnp.where(chosen.reshape(mask_shape(value, chosen)), split, jnp.zeros((), value.dtype)),
        axis=2,
    )


def spread(value, chosen):
    rate = chosen.shape[0]
    full = jnp.where(
        chosen.reshape(mask_shape(value, chosen)),
        jnp.expand_dims(value, 2),
        jnp.zeros((), value.dtype),
    )
    return full.reshape((value.shape[0], value.shape[1] * rate) + value.shape[2:])


def scores_of(query, keys, bias, pair, scale):
    raw = jnp.einsum("qhe,khe->hqk", query, keys, preferred_element_type=jnp.float32)
    return raw * scale + jnp.transpose(bias)[:, None, :] + pair


def attend_forward(query, keys, values, bias, pair, scale):
    scores = scores_of(query, keys, bias, pair, scale)
    total = jax.nn.logsumexp(scores, axis=-1)
    probs = jnp.exp(scores - total[..., None]).astype(jnp.bfloat16)
    result = jnp.einsum("hqk,khe->qhe", probs, values, preferred_element_type=jnp.float32)
    return (result, jnp.transpose(total)[..., None])


def attend_backward(query, keys, values, bias, pair, total, grad_out, grad_total, scale):
    scores = scores_of(query, keys, bias, pair, scale)
    probs = jnp.exp(scores - jnp.transpose(total[..., 0])[..., None])
    grad_probs = jnp.einsum("qhe,khe->hqk", grad_out, values, preferred_element_type=jnp.float32)
    delta = jnp.sum(probs * grad_probs, axis=-1) - jnp.transpose(grad_total[..., 0])
    grad_scores = (probs * (grad_probs - delta[..., None])).astype(jnp.bfloat16)
    grad_query = (
        jnp.einsum("hqk,khe->qhe", grad_scores, keys, preferred_element_type=jnp.float32) * scale
    )
    grad_keys = (
        jnp.einsum("hqk,qhe->khe", grad_scores, query, preferred_element_type=jnp.float32) * scale
    )
    grad_values = jnp.einsum(
        "hqk,qhe->khe", probs.astype(jnp.bfloat16), grad_out, preferred_element_type=jnp.float32
    )
    return (grad_query, grad_keys, grad_values)


def forward_slide(args, pair, scale):
    q_one, kv_one, bias_one = args
    return attend_forward(q_one, kv_one[:, 0], kv_one[:, 1], bias_one, pair, scale)


def backward_slide(args, pair, scale):
    q_one, kv_one, bias_one, total_one, grad_one, grad_total_one = args
    return attend_backward(
        q_one,
        kv_one[:, 0],
        kv_one[:, 1],
        bias_one,
        pair,
        total_one,
        grad_one,
        grad_total_one,
        scale,
    )


def on_device(
    tiles,
    coords,
    lengths,
    padding_mask,
    ln1_gain,
    ln1_bias,
    query_key_value_weight,
    qv_bias,
    attention_output_weight,
    attention_output_bias,
    ln2_gain,
    ln2_bias,
    mlp_entry_matrix,
    mlp_entry_offset,
    feed_output_weight,
    feed_output_bias,
    cotangent,
):
    slides, rows, width = tiles.shape
    head_count = lax.axis_size("head")
    local_width = query_key_value_weight.shape[2]
    local_heads = local_width * HEADS // width
    head_dim = width // HEADS
    hidden_local = mlp_entry_matrix.shape[1]
    scale = 1.0 / math.sqrt(head_dim)
    seg_rows = rows * head_count
    total_len = padding_mask.shape[1]
    seq_index = lax.axis_index("seq")
    head_index = lax.axis_index("head")
    dilations = (RATIO // 8, RATIO // 4, RATIO // 2, RATIO)
    reaches = (SEG2, total_len, total_len, total_len)
    positions = jnp.arange(total_len, dtype=jnp.int32)
    valid = (positions[None, :] < lengths[:, None]) & (padding_mask == 1)
    own_valid = lax.dynamic_slice_in_dim(valid, seq_index * seg_rows, seg_rows, 1)
    mate_valid = lax.dynamic_slice_in_dim(valid, (seq_index ^ 1) * seg_rows, seg_rows, 1)
    near_valid = jnp.concatenate([own_valid, mate_valid], axis=1)
    near_bias = jnp.broadcast_to(
        jnp.where(near_valid, 0.0, NEG)[..., None], (slides, 2 * seg_rows, local_heads)
    )
    global_heads = head_index * local_heads + jnp.arange(local_heads, dtype=jnp.int32)
    chosens = []
    far_biases = []
    selects = []
    pair_masks = []
    for dilation, reach in zip(dilations, reaches):
        chosen = (
            jnp.arange(dilation, dtype=jnp.int32)[:, None] == (global_heads % dilation)[None, :]
        )
        chosens.append(chosen)
        far_valid = jnp.any(
            valid.reshape(slides, total_len // dilation, dilation)[..., None] & chosen[None, None],
            axis=2,
        )
        far_biases.append(jnp.where(far_valid, 0.0, NEG))
        selects.append(
            (
                (jnp.arange(seg_rows, dtype=jnp.int32) % dilation)[:, None]
                == (global_heads % dilation)[None, :]
            )[None, :, :, None]
        )
        query_places = seq_index * seg_rows + dilation * jnp.arange(
            seg_rows // dilation, dtype=jnp.int32
        )
        key_places = dilation * jnp.arange(total_len // dilation, dtype=jnp.int32)
        pair_masks.append(
            jnp.where((query_places // reach)[:, None] == (key_places // reach)[None, :], 0.0, NEG)
        )
    base = tiles.astype(jnp.float32) + position_table(coords, width)
    first_normalized = layer_norm(base, ln1_gain, ln1_bias).astype(jnp.bfloat16)
    initial_tokens, cotangent_rows = (
        lax.all_gather(first_normalized, "head", axis=1, tiled=True),
        lax.all_gather(cotangent, "head", axis=1, tiled=True),
    )
    packed_projection_matrix = query_key_value_weight.reshape(width, 3 * local_width)
    triple_bias = jnp.concatenate([qv_bias[0], jnp.zeros_like(qv_bias[0]), qv_bias[1]])
    query_key_value = (
        jnp.einsum(
            "hmq,qn->hmn",
            initial_tokens,
            packed_projection_matrix,
            preferred_element_type=jnp.float32,
        )
        + triple_bias
    ).astype(jnp.bfloat16)
    query_key_value = query_key_value.reshape(slides, seg_rows, 3, local_heads, head_dim)
    query = query_key_value[:, :, 0]
    key_value = query_key_value[:, :, 1:3]
    mate_kv = partner(key_value, "seq", 0)
    near_kv = jnp.concatenate([key_value, mate_kv], axis=1)

    def collect(piece):
        return tuple((pick(piece, chosens[index]) for index in range(4)))

    far_kvs = collect(lax.all_gather(key_value, "seq", axis=1, tiled=True))
    far_queries = [pick(query, chosen) for chosen in chosens]
    near_out, near_total = lax.map(
        partial(forward_slide, pair=0.0, scale=scale), (query, near_kv, near_bias)
    )
    far_results = []
    for index in range(4):
        far_results.append(
            lax.map(
                partial(forward_slide, pair=pair_masks[index], scale=scale),
                (far_queries[index], far_kvs[index], far_biases[index]),
            )
        )
    outs_full = [near_out] + [spread(far_results[index][0], chosens[index]) for index in range(4)]
    totals_full = [near_total] + [
        jnp.where(selects[index], spread(far_results[index][1], chosens[index]), FLOOR)
        for index in range(4)
    ]
    stacked = jnp.stack(totals_full)
    highest = jnp.max(stacked, axis=0)
    raised = jnp.exp(stacked - highest)
    weights = raised / jnp.sum(raised, axis=0)
    combined_output = weights[0] * outs_full[0]
    for index in range(1, 5):
        combined_output = combined_output + weights[index] * outs_full[index]
    combined_lowered = combined_output.reshape(slides, seg_rows, local_width).astype(jnp.bfloat16)
    attention_piece = jnp.einsum(
        "mua,ah->muh", combined_lowered, attention_output_weight, preferred_element_type=jnp.float32
    )
    attn_rows = lax.psum_scatter(
        attention_piece.astype(jnp.bfloat16), "head", scatter_dimension=1, tiled=True
    ).astype(jnp.float32)
    mid = base + (attn_rows + attention_output_bias)
    later_layernormed = layer_norm(mid, ln2_gain, ln2_bias).astype(jnp.bfloat16)
    later_tokens = lax.all_gather(later_layernormed, "head", axis=1, tiled=True)
    before_nonlinearity = (
        jnp.einsum(
            "awq,qd->awd", later_tokens, mlp_entry_matrix, preferred_element_type=jnp.float32
        )
        + mlp_entry_offset
    )
    hidden_activation = jax.nn.gelu(before_nonlinearity, approximate=False).astype(jnp.bfloat16)
    feedforward_piece = jnp.einsum(
        "nrv,vk->nrk", hidden_activation, feed_output_weight, preferred_element_type=jnp.float32
    )
    mlp_rows_sum = lax.psum_scatter(
        feedforward_piece.astype(jnp.bfloat16), "head", scatter_dimension=1, tiled=True
    ).astype(jnp.float32)
    output = mid + (mlp_rows_sum + feed_output_bias)
    cot_float = cotangent.astype(jnp.float32)
    grad_fc2_bias = jnp.sum(cot_float, axis=(0, 1))
    hidden_gradient = jnp.einsum(
        "tvq,cq->tvc", cotangent_rows, feed_output_weight, preferred_element_type=jnp.float32
    )
    feed_output_weight_gradient = jnp.einsum(
        "gar,gai->ri", hidden_activation, cotangent_rows, preferred_element_type=jnp.float32
    )
    gelu_pull = jax.vjp(lambda v: jax.nn.gelu(v, approximate=False), before_nonlinearity)[1]
    preactivation_gradient = gelu_pull(hidden_gradient)[0].astype(jnp.bfloat16)
    feed_input_weight_gradient = jnp.einsum(
        "vxr,vxm->rm", later_tokens, preactivation_gradient, preferred_element_type=jnp.float32
    )
    grad_fc1_bias = jnp.sum(preactivation_gradient.astype(jnp.float32), axis=(0, 1))
    second_backward = jnp.einsum(
        "ivo,go->ivg", preactivation_gradient, mlp_entry_matrix, preferred_element_type=jnp.float32
    )
    back2_rows = lax.psum_scatter(
        second_backward.astype(jnp.bfloat16), "head", scatter_dimension=1, tiled=True
    ).astype(jnp.float32)
    norm2_pull = jax.vjp(layer_norm, mid, ln2_gain, ln2_bias)[1]
    grad_mid_norm, grad_ln2_gain, grad_ln2_bias = norm2_pull(back2_rows)
    grad_mid = cot_float + grad_mid_norm
    grad_attn = grad_mid.astype(jnp.bfloat16)
    grad_out_bias = jnp.sum(grad_attn.astype(jnp.float32), axis=(0, 1))
    attention_rows_gradient = lax.all_gather(grad_attn, "head", axis=1, tiled=True)
    grad_w_out = jnp.einsum(
        "fub,fui->bi", combined_lowered, attention_rows_gradient, preferred_element_type=jnp.float32
    )
    grad_merged = jnp.einsum(
        "tpq,jq->tpj",
        attention_rows_gradient,
        attention_output_weight,
        preferred_element_type=jnp.float32,
    )
    grad_merged = grad_merged.reshape(slides, seg_rows, local_heads, head_dim)
    grad_parts = [weights[index] * grad_merged for index in range(5)]
    gaps = [
        weights[index]
        * jnp.sum(grad_merged * (outs_full[index] - combined_output), axis=-1, keepdims=True)
        for index in range(5)
    ]
    grad_near = grad_parts[0].astype(jnp.bfloat16)
    near_dq, near_dk, near_dv = lax.map(
        partial(backward_slide, pair=0.0, scale=scale),
        (query, near_kv, near_bias, near_total, grad_near, gaps[0]),
    )
    own_grad = jnp.stack([near_dk[:, :seg_rows], near_dv[:, :seg_rows]], axis=2)
    mate_grad = jnp.stack([near_dk[:, seg_rows:], near_dv[:, seg_rows:]], axis=2)
    returned = partner(mate_grad.astype(jnp.bfloat16), "seq", 0).astype(mate_grad.dtype)
    far_grads = []
    grad_query = near_dq
    for index in range(4):
        grad_far = pick(grad_parts[index + 1], chosens[index]).astype(jnp.bfloat16)
        grad_far_total = pick(gaps[index + 1], chosens[index])
        far_dq, far_dk, far_dv = lax.map(
            partial(backward_slide, pair=pair_masks[index], scale=scale),
            (
                far_queries[index],
                far_kvs[index],
                far_biases[index],
                far_results[index][1],
                grad_far,
                grad_far_total,
            ),
        )
        far_grads.append(jnp.stack([far_dk, far_dv], axis=2))
        grad_query = grad_query + spread(far_dq, chosens[index])
    far_back = (
        lax.psum_scatter(
            far_grads[0].astype(jnp.bfloat16), "seq", scatter_dimension=1, tiled=True
        ).astype(jnp.float32),
        lax.psum_scatter(
            far_grads[1].astype(jnp.bfloat16), "seq", scatter_dimension=1, tiled=True
        ).astype(jnp.float32),
        lax.psum_scatter(
            far_grads[2].astype(jnp.bfloat16), "seq", scatter_dimension=1, tiled=True
        ).astype(jnp.float32),
        lax.psum_scatter(
            far_grads[3].astype(jnp.bfloat16), "seq", scatter_dimension=1, tiled=True
        ).astype(jnp.float32),
    )
    grad_kv = own_grad + returned
    for index in range(4):
        grad_kv = grad_kv + spread(far_back[index], chosens[index])
    query_key_value_gradient = jnp.concatenate([grad_query[:, :, None], grad_kv], axis=2).astype(
        jnp.bfloat16
    )
    query_key_value_gradient = query_key_value_gradient.reshape(slides, seg_rows, 3 * local_width)
    grad_w_qkv = jnp.einsum(
        "ymt,yma->ta", initial_tokens, query_key_value_gradient, preferred_element_type=jnp.float32
    ).reshape(width, 3, local_width)
    bias_sums = jnp.sum(query_key_value_gradient.astype(jnp.float32), axis=(0, 1)).reshape(
        3, local_width
    )
    grad_qv = jnp.stack([bias_sums[0], bias_sums[2]])
    first_backward = jnp.einsum(
        "kgw,aw->kga",
        query_key_value_gradient,
        packed_projection_matrix,
        preferred_element_type=jnp.float32,
    )
    back1_rows = lax.psum_scatter(
        first_backward.astype(jnp.bfloat16), "head", scatter_dimension=1, tiled=True
    ).astype(jnp.float32)
    norm1_pull = jax.vjp(layer_norm, base, ln1_gain, ln1_bias)[1]
    grad_base_norm, grad_ln1_gain, grad_ln1_bias = norm1_pull(back1_rows)
    tiles_grad = (grad_mid + grad_base_norm).astype(jnp.bfloat16)
    w_qkv_grad, w_out_grad, w_fc1_grad, w_fc2_grad = (
        lax.psum_scatter(
            grad_w_qkv.astype(jnp.bfloat16), "seq", scatter_dimension=0, tiled=True
        ).astype(jnp.float32),
        lax.psum_scatter(
            grad_w_out.astype(jnp.bfloat16), "seq", scatter_dimension=1, tiled=True
        ).astype(jnp.float32),
        lax.psum_scatter(
            feed_input_weight_gradient.astype(jnp.bfloat16), "seq", scatter_dimension=0, tiled=True
        ).astype(jnp.float32),
        lax.psum_scatter(
            feed_output_weight_gradient.astype(jnp.bfloat16), "seq", scatter_dimension=1, tiled=True
        ).astype(jnp.float32),
    )
    shared = jnp.stack(
        [grad_ln1_gain, grad_ln1_bias, grad_out_bias, grad_ln2_gain, grad_ln2_bias, grad_fc2_bias]
    )
    qv_full = lax.dynamic_update_slice_in_dim(
        jnp.zeros((2, width), jnp.float32), grad_qv, head_index * local_width, 1
    )
    fc1_full = lax.dynamic_update_slice_in_dim(
        jnp.zeros((FF,), jnp.float32), grad_fc1_bias, head_index * hidden_local, 0
    )
    shared_sum, qv_sum, fc1_sum = lax.psum((shared, qv_full, fc1_full), ("seq", "head"))
    qv_bias_grad = lax.dynamic_slice_in_dim(qv_sum, head_index * local_width, local_width, 1)
    fc1_bias_grad = lax.dynamic_slice_in_dim(fc1_sum, head_index * hidden_local, hidden_local, 0)
    return (
        output.astype(jnp.bfloat16),
        tiles_grad,
        shared_sum[0],
        shared_sum[1],
        w_qkv_grad,
        qv_bias_grad,
        w_out_grad,
        shared_sum[2],
        shared_sum[3],
        shared_sum[4],
        w_fc1_grad,
        fc1_bias_grad,
        w_fc2_grad,
        shared_sum[5],
    )


HEAD_DIM = 48
TRIPLE = 144
META = 32
AUG = 128
OUT_ROWS = 64
ACC_ROWS = 56
SLOT_ORDER = (0, 2, 1, 3)
LOG2E = math.log2(math.e)
COST = 2.5
NEAR_US = 6.6
WG_US = 12
NB_US = 0.2
FA_US = 3
QB_US = 4
SMALL_US = 0.5
FIRST_COLUMNS = 1024
BF = jnp.bfloat16
F32 = jnp.float32


def dot(a, b):
    return lax.dot_general(a, b, (((1,), (0,)), ((), ())), preferred_element_type=F32)


def dot_nt(a, b):
    return lax.dot_general(a, b, (((1,), (1,)), ((), ())), preferred_element_type=F32)


def split3(value):
    high = value.astype(BF)
    rest = value - high.astype(F32)
    middle = rest.astype(BF)
    low = (rest - middle.astype(F32)).astype(BF)
    return high, middle, low


def split3_constant(value):
    pieces = []
    rest = np.float32(value)
    for _ in range(3):
        piece = np.float32(rest.astype(ml_dtypes.bfloat16))
        pieces.append(float(piece))
        rest = np.float32(rest - piece)
    return pieces


def joined(rows):
    wide = rows.astype(F32)
    return wide[0:1] + wide[1:2] + wide[2:3]


def rows_of(shape, first, pieces):
    row = lax.broadcasted_iota(jnp.int32, shape, 0)
    out = jnp.zeros(shape, F32)
    for index, piece in enumerate(pieces):
        out = jnp.where(row == first + index, piece, out)
    return out


def rows_between(shape, first, count):
    row = lax.broadcasted_iota(jnp.int32, shape, 0)
    return jnp.where((row >= first) & (row < first + count), 1.0, 0.0)


def query_rows(query, meta, factor):
    wide = query.astype(F32) * factor
    high = wide.astype(BF)
    low = (wide - high.astype(F32)).astype(BF)
    return jnp.concatenate([high, low, meta], 0)


def key_rows(keys, meta):
    return jnp.concatenate([keys, keys, meta], 0)


def ones_below(value, count):
    width = value.shape[-1]
    return jnp.concatenate([value, rows_between((16, width), 0, count).astype(BF)], 0)


def plain64(value):
    return jnp.concatenate([value, jnp.zeros((16, value.shape[-1]), value.dtype)], 0)


def padded_turn(value):
    height, width = value.shape
    missing = -height % 128
    full = jnp.concatenate([value, jnp.zeros((missing, width), value.dtype)], 0)
    return full.T


def turned_out(value):
    height = value.shape[0]
    return jnp.concatenate([value, jnp.zeros((height, 64), F32)], 1).T[0:HEAD_DIM]


def bias_rows(valid):
    shape = (META, valid.shape[-1])
    return rows_of(shape, 0, [(1.0 - valid) * part for part in split3_constant(NEG * LOG2E)])


def near_key_meta(valid):
    shape = (META, valid.shape[-1])
    return (bias_rows(valid) + rows_between(shape, 15, 3)).astype(BF)


def far_levels(place, width, half):
    head = 4 * (2 * place[2] + place[3]) + place[0]
    lane = lax.broadcasted_iota(jnp.int32, (1, width), 1)
    spot = (2 * (lane & (half - 1)) + (place[0] & 1)) & 15
    return jnp.where(
        spot == (head & 15),
        4,
        jnp.where((spot & 7) == (head & 7), 3, jnp.where((spot & 3) == (head & 3), 2, 1)),
    )


def far_tables(level):
    pieces = {0: [], 1: []}
    for extra in (0, 1):
        for part in range(3):
            for kind in range(1, 5):
                row = jnp.zeros(level.shape, F32)
                for there in range(1, 5):
                    amount = split3_constant(math.log2(min(kind, there) + extra))[part]
                    row = jnp.where(level == there, amount, row)
                pieces[extra].append(row)
    shape = (META, level.shape[-1])
    return rows_of(shape, 3, pieces[0]) + rows_between(shape, 15, 3) + rows_of(shape, 18, pieces[1])


def far_queries(level):
    shape = (META, level.shape[-1])
    chosen = [jnp.where(level == kind, 1.0, 0.0) for kind in range(1, 5)] * 3
    ones = rows_between(shape, 0, 3)
    return (ones + rows_of(shape, 18, chosen)).astype(BF), (ones + rows_of(shape, 3, chosen)).astype(BF)


def softmax_out(keys, values, queries, stage):
    top = None
    for index, key in enumerate(keys):
        scores = dot(key(), queries[index])
        stage[index] = scores
        peak = jnp.max(scores, axis=0, keepdims=True)
        top = peak if top is None else jnp.maximum(top, peak)
    acc = None
    for index, value in enumerate(values):
        probs = jnp.exp2(stage[index] - top).astype(BF)
        part = dot(value(), probs)
        acc = part if acc is None else acc + part
    total = acc[HEAD_DIM : HEAD_DIM + 1]
    return acc[0:HEAD_DIM] * (1.0 / total), top + jnp.log2(total)


def moments(value):
    mean = jnp.mean(value, axis=-1, keepdims=True)
    centered = value - mean
    var = jnp.mean(centered * centered, axis=-1, keepdims=True)
    rate = lax.rsqrt(var + EPS)
    return centered * rate, rate


def norm_back(xhat, rate, gain, upstream):
    a = upstream * gain
    return rate * (
        a - jnp.mean(a, axis=-1, keepdims=True) - xhat * jnp.mean(a * xhat, axis=-1, keepdims=True)
    )


def parity_order(rows, back):
    first = lax.broadcasted_iota(jnp.int32, (rows, rows), 1 if back else 0)
    second = lax.broadcasted_iota(jnp.int32, (rows, rows), 0 if back else 1)
    half = rows // 2
    source = jnp.where(first < half, 2 * first, 2 * (first - half) + 1)
    return (source == second).astype(F32).astype(BF)


def entry_kernel(
    place, tiles_a, tiles_b, coords_a, coords_b, cot_a, cot_b, table, base, cot_out, own, other
):
    rows = tiles_a.shape[1]
    half = rows // 2
    order = parity_order(rows, False)
    lane = lax.broadcasted_iota(jnp.int32, (rows, 256), 1).astype(F32)
    sides = ((tiles_a, coords_a, cot_a, own), (tiles_b, coords_b, cot_b, other))
    for side, (tiles, coords, cot, out) in enumerate(sides):
        spots = dot(order, coords[0].astype(F32).astype(BF))
        parts = []
        for axis in range(2):
            hot = (spots[:, axis : axis + 1] == lane).astype(F32).astype(BF)
            parts.append(dot(hot, table[0]) + dot(hot, table[1]) + dot(hot, table[2]))
        value = dot(order, tiles[0]) + jnp.concatenate(parts, 1)
        base[side, 0] = value
        xhat = moments(value)[0].astype(BF)
        out[0, 0] = xhat[:half]
        out[0, 1] = xhat[half:]
        cot_out[side, 0] = dot(order, cot[0]).astype(BF)


def join_kernel(place, first, second, out):
    here = first.shape[2]
    out[:, :, :here] = first[...]
    out[:, :, here:] = second[...]


def widen_kernel(place, first, second, stay, send):
    half = first.shape[2] // 2
    stay[...] = jnp.concatenate([first[:, :, :half], second[:, :, :half]], -1)
    send[...] = jnp.concatenate([first[:, :, half:], second[:, :, half:]], -1)


def narrow_kernel(place, first, second, stay, send):
    here = first.shape[2]
    columns = first.shape[-1] // 2
    for ref, part in ((first, slice(0, here)), (second, slice(here, 2 * here))):
        stay[:, :, part] = ref[..., :columns]
        send[:, :, part] = ref[..., columns:]


def fold_kernel(place, first, second, stay, send):
    half = first.shape[2] // 2
    total = (first[...].astype(F32) + second[...].astype(F32)).astype(BF)
    stay[...] = total[:, :, :half]
    send[...] = total[:, :, half:]


def z_halves(place, total, stay, send, nearest):
    piece = total.shape[0] // (4 if nearest else 2)
    side = place[0] % 2 if nearest else place[0] // 2
    for lead in range(2 if nearest else 1):
        rows = slice(lead * piece, (lead + 1) * piece)
        for ref, here in ((stay, side), (send, 1 - side)):
            at = pl.multiple_of((2 * lead + here) * piece, 32)
            ref[rows] = total[pl.ds(at, piece)]


def z_fold_kernel(place, first, second, stay, send, total, *, nearest):
    total[...] = (first[...].astype(F32) + second[...].astype(F32)).astype(BF)
    z_halves(place, total, stay, send, nearest)


def weights_out_kernel(place, first, second, fc1, fc2, out):
    total = first[...].astype(F32) + second[...].astype(F32)
    width = fc1.shape[1]
    rows = total.shape[0]
    fc1[...] = total[:, :width]
    out[...] = padded_turn(total[:, width:FIRST_COLUMNS])[: out.shape[0], :rows]
    fc2[...] = padded_turn(total[:, FIRST_COLUMNS:])[:, :rows]


def qkv_out_kernel(place, first, second, out):
    total = first[...].astype(F32) + second[...].astype(F32)
    for head in range(4):
        for part in range(3):
            at = (head * 3 + part) * HEAD_DIM
            out[:, part, head * HEAD_DIM : (head + 1) * HEAD_DIM] = total[:, at : at + HEAD_DIM]


def small_start_kernel(place, sums_a, sums_b, fc1_a, fc1_b, ln_sum, bias_sum, stay, send):
    width = sums_a.shape[1]
    common = [sums_a[index : index + 1] + sums_b[index : index + 1] for index in range(4)]
    common += [ln_sum[0:1], ln_sum[1:2]]
    slots = [fc1_a[slot, 0:1] + fc1_b[slot, 0:1] for slot in range(4)]
    missing = width - bias_sum.shape[1]
    last = jnp.concatenate([bias_sum[0:1], jnp.zeros((1, missing), F32)], 1)
    stay[...] = rows_of((16, width), 0, common + slots[0:2] + [last])
    send[...] = rows_of((8, width), 0, common + slots[2:4])


def small_first_kernel(place, first, second, out):
    out[0:8] = first[0:8] + second[...]
    out[8:16] = first[8:16]


def small_middle_kernel(place, first, second, stay, send):
    total = first[...] + second[...]
    row = lax.broadcasted_iota(jnp.int32, stay.shape, 0)
    stay[...] = jnp.where(row == 7, total[8:9], total[0:8])
    send[...] = jnp.where(row == 6, total[7:8], jnp.where(row == 7, 0.0, total[0:8]))


def add_kernel(place, first, second, out):
    out[...] = first[...] + second[...]


def normed_of(xhat, gains):
    return (xhat.astype(F32) * gains[0:1] + gains[1:2]).astype(BF)


def qkv_kernel(place, first, second, weight, bias, gains, near, s0, s1, s2, s3):
    width = first.shape[2]
    for parity in range(2):
        for part, ref in enumerate((first, second)):
            made = dot_nt(weight[...], normed_of(ref[0, parity], gains)) + bias[...]
            made = made.astype(BF)
            for head in range(4):
                near[0, head, parity, :, part * width : (part + 1) * width] = made[
                    head * TRIPLE : (head + 1) * TRIPLE
                ]
    for slot, ref in enumerate((s0, s1, s2, s3)):
        head = place[0] ^ slot
        ref[0] = near[0, head, head & 1]


def near_forward_kernel(place, qkv, valid, out, key_aug, value_aug, stage, *, slide, factor):
    width = qkv.shape[-1]
    own = lax.rem(pl.program_id(0), 2)
    queries = []
    ones = rows_between((META, width), 0, 3).astype(BF)
    for role in range(2):
        parity = own if role == 0 else 1 - own
        block = qkv[0, 0, parity]
        there = valid[place[1] * 3 + slide, pl.ds(place[0] * 2 + parity, 1)]
        key_aug[role] = key_rows(block[48:96], near_key_meta(there)).T
        value_aug[role] = ones_below(block[96:144], 1)
        queries.append(query_rows(block[0:48], ones, factor))
    for role, used in ((0, (1,)), (1, (0, 1))):
        result, total = softmax_out(
            [lambda r=r: key_aug[r] for r in used],
            [lambda r=r: value_aug[r] for r in used],
            [queries[role]] * len(used),
            stage,
        )
        out[0, role] = jnp.concatenate([result, rows_of((8, width), 0, [total])], 0)


def far_forward_kernel(
    place, b0, b1, b2, b3, valid, o0, o1, o2, o3, key_aug, value_aug, q_same, q_other, stage, out,
    *, first_slide, half, factor,
):
    width = b0.shape[-1]
    slide = first_slide + pl.program_id(0)
    level = far_levels(place, width, half)
    tail = far_tables(level)
    same, other = far_queries(level)
    for slot, block in enumerate((b0, b1, b2, b3)):
        row = (place[0] ^ slot) * 2 + (place[0] & 1)
        there = valid[place[1] * 3 + slide, pl.ds(row, 1)]
        key_aug[slot] = key_rows(block[0, 48:96], (tail + bias_rows(there)).astype(BF)).T
        value_aug[slot] = ones_below(block[0, 96:144], 1)
        q_same[slot] = query_rows(block[0, 0:48], same, factor)
        q_other[slot] = query_rows(block[0, 0:48], other, factor)

    def step(slot, carry):
        places = [lax.rem(slot + shift, 4) for shift in range(4)]
        result, total = softmax_out(
            [lambda p=p: key_aug[p] for p in places],
            [lambda p=p: value_aug[p] for p in places],
            [q_same[slot], q_other[slot], q_other[slot], q_other[slot]],
            stage,
        )
        ending = rows_of((16, width), 0, [part.astype(F32) for part in split3(total)])
        out[slot] = jnp.concatenate([result, ending], 0).astype(BF)
        return carry

    lax.fori_loop(0, 4, step, 0)
    for slot, ref in enumerate((o0, o1, o2, o3)):
        ref[0] = out[slot]


def merge_kernel(place, *refs):
    count = refs[-2].shape[0]
    nears = refs[:count]
    f0, f1, f2, f3, kept, stay, send, far = refs[count:]
    width = kept.shape[-1]
    for slide, near in enumerate(nears):
        for slot, ref in enumerate((f0, f1, f2, f3)):
            far[place[0] ^ slot] = ref[slide]
        by_parity = [[], []]
        for head in range(4):
            own = head & 1
            there = far[head]
            far_total = joined(there[48:51])
            near_total = near[head, 0, 48:49]
            top = jnp.maximum(far_total, near_total)
            total = top + jnp.log2(jnp.exp2(far_total - top) + jnp.exp2(near_total - top))
            both = there[0:48].astype(F32) * jnp.exp2(far_total - total) + near[
                head, 0, 0:48
            ] * jnp.exp2(near_total - total)
            kept[slide, head, own] = jnp.concatenate([both, rows_of((8, width), 0, [total])], 0)
            kept[slide, head, 1 - own] = near[head, 1]
            by_parity[own].append(both)
            by_parity[1 - own].append(near[head, 1, 0:48])
        for parity in range(2):
            turned = padded_turn(jnp.concatenate(by_parity[parity], 0))[:, 0:192].astype(BF)
            for block in range(4):
                rows = slice(block * width // 8, (block + 1) * width // 8)
                stay[slide, parity, block] = turned[rows]
                rows = slice((block + 4) * width // 8, (block + 5) * width // 8)
                send[slide, parity, block] = turned[rows]


def gradient_rows_kernel(place, first, second, kept, *refs):
    near, s0, s1, s2, s3 = refs[-5:]
    half = first.shape[2]
    width = kept.shape[-1]
    for parity in range(2):
        turned = jnp.concatenate(
            [
                jnp.concatenate([ref[0, parity], jnp.zeros((half, 64), BF)], 1).T
                for ref in (first, second)
            ],
            1,
        )
        for head in range(4):
            part = turned[head * 48 : (head + 1) * 48]
            inner = jnp.sum(part.astype(F32) * kept[0, head, parity, 0:48], axis=0, keepdims=True)
            total = kept[0, head, parity, 48:49]
            rows = [piece.astype(F32) for piece in split3(total) + split3(inner)]
            ending = rows_of((16, width), 0, rows).astype(BF)
            near[0, head, parity] = jnp.concatenate([part, ending], 0)
    for slot, ref in enumerate((s0, s1, s2, s3)):
        head = place[0] ^ slot
        ref[0] = near[0, head, head & 1]


def negated_total(grad_block, base):
    tail = grad_block[48:64].astype(F32)
    row = lax.broadcasted_iota(jnp.int32, base.shape, 0)
    out = base.astype(F32)
    for index in range(3):
        out = jnp.where(row == 15 + index, -tail[index : index + 1], out)
    return out.astype(BF)


def gradient_aug(grad_block):
    width = grad_block.shape[-1]
    tail = grad_block[48:64].astype(F32)
    rows = rows_of((16, width), 0, [-tail[index : index + 1] for index in (3, 4, 5)])
    return jnp.concatenate([grad_block[0:48], rows.astype(BF)], 0)


def pair_block(key_aug, value_aug, queries, grads):
    probs = jnp.exp2(dot(key_aug, queries))
    slopes = (probs * dot(value_aug, grads)).astype(BF)
    return probs.astype(BF), slopes


def near_backward_kernel(
    place, qkv, valid, grad, out, key_aug, key_t, value_aug, q_aug, g_aug, q_nat, g_nat,
    *, slide, factor, scale,
):
    width = qkv.shape[-1]
    own = lax.rem(pl.program_id(0), 2)
    ones = rows_between((META, width), 0, 3)
    for role in range(2):
        parity = own if role == 0 else 1 - own
        block = qkv[0, 0, parity]
        given = grad[0, 0, parity]
        there = valid[place[1] * 3 + slide, pl.ds(place[0] * 2 + parity, 1)]
        key_aug[role] = key_rows(block[48:96], near_key_meta(there)).T
        key_t[role] = plain64(block[48:96])
        value_aug[role] = padded_turn(ones_below(block[96:144], 3))[:, 0:64]
        q_aug[role] = query_rows(block[0:48], negated_total(given, ones), factor)
        g_aug[role] = gradient_aug(given)
        q_nat[role] = padded_turn(plain64(block[0:48]))[:, 0:64]
        g_nat[role] = padded_turn(plain64(given[0:48]))[:, 0:64]
    dq = [None, None]
    for key_role, users in ((0, (1,)), (1, (0, 1))):
        dk = None
        dv = None
        for role in users:
            probs, slopes = pair_block(
                key_aug[key_role], value_aug[key_role], q_aug[role], g_aug[role]
            )
            add_v = dot(probs, g_nat[role])
            add_k = dot(slopes, q_nat[role])
            add_q = dot(key_t[key_role], slopes)
            dv = add_v if dv is None else dv + add_v
            dk = add_k if dk is None else dk + add_k
            dq[role] = add_q if dq[role] is None else dq[role] + add_q
        parity = own if key_role == 0 else 1 - own
        out[0, parity, 48:96] = (turned_out(dk) * scale).astype(BF)
        out[0, parity, 96:144] = turned_out(dv).astype(BF)
    for role in range(2):
        parity = own if role == 0 else 1 - own
        out[0, parity, 0:48] = (dq[role][0:48] * scale).astype(BF)


def far_backward_kernel(
    place, b0, b1, b2, b3, g0, g1, g2, g3, valid, o0, o1, o2, o3,
    key_aug, key_t, value_aug, q_same, q_other, g_aug, q_nat, g_nat, dq, out,
    *, first_slide, half, factor, scale,
):
    width = b0.shape[-1]
    slide = first_slide + pl.program_id(0)
    level = far_levels(place, width, half)
    tail = far_tables(level)
    same, other = far_queries(level)
    for slot, (block, given) in enumerate(((b0, g0), (b1, g1), (b2, g2), (b3, g3))):
        grad = given[0]
        row = (place[0] ^ slot) * 2 + (place[0] & 1)
        there = valid[place[1] * 3 + slide, pl.ds(row, 1)]
        key_aug[slot] = key_rows(block[0, 48:96], (tail + bias_rows(there)).astype(BF)).T
        key_t[slot] = plain64(block[0, 48:96])
        value_aug[slot] = padded_turn(ones_below(block[0, 96:144], 3))[:, 0:64]
        q_same[slot] = query_rows(block[0, 0:48], negated_total(grad, same), factor)
        q_other[slot] = query_rows(block[0, 0:48], negated_total(grad, other), factor)
        g_aug[slot] = gradient_aug(grad)
        q_nat[slot] = padded_turn(plain64(block[0, 0:48]))[:, 0:64]
        g_nat[slot] = padded_turn(plain64(grad[0:48]))[:, 0:64]
    dq[...] = jnp.zeros_like(dq)

    def step(slot, carry):
        dk = None
        dv = None
        for shift in range(4):
            there = lax.rem(slot + shift, 4)
            queries = q_same[there] if shift == 0 else q_other[there]
            probs, slopes = pair_block(key_aug[slot], value_aug[slot], queries, g_aug[there])
            add_v = dot(probs, g_nat[there])
            add_k = dot(slopes, q_nat[there])
            dv = add_v if dv is None else dv + add_v
            dk = add_k if dk is None else dk + add_k
            dq[there] += dot(key_t[slot], slopes)
        out[slot, 48:96] = (turned_out(dk) * scale).astype(BF)
        out[slot, 96:144] = turned_out(dv).astype(BF)
        return carry

    lax.fori_loop(0, 4, step, 0)
    for slot, ref in enumerate((o0, o1, o2, o3)):
        ref[0] = out[slot]
        ref[0, 0:48] = (dq[slot, 0:48] * scale).astype(BF)


def qkv_backward_kernel(place, *refs, count, begins, ends):
    refs = list(refs)
    nears = [refs.pop(0) for _ in range(count)]
    fars = [[refs.pop(0) for _ in range(4)] for _ in range(count)]
    first, second, weight, gains = [refs.pop(0) for _ in range(4)]
    before = [] if begins else [refs.pop(0) for _ in range(3)]
    wgrads = [refs.pop(0) for _ in range(2 if ends else 1)]
    bias_sum, ln_sum, stay, send, far = refs[:5]
    acc = refs[5] if ends else wgrads[0]
    if begins:
        for ref in (acc, bias_sum, ln_sum):
            ref[...] = jnp.zeros_like(ref)
    else:
        for ref, old in zip((acc, bias_sum, ln_sum), before):
            ref[...] = old[...]
    half = first.shape[2]
    piece_rows = half // 4
    gain_row = jnp.zeros((1, gains.shape[1]), F32)
    bias_row = jnp.zeros((1, gains.shape[1]), F32)
    ones = jnp.ones((8, 2 * half), BF)
    for slide, near in enumerate(nears):
        for slot, ref in enumerate(fars[slide]):
            far[place[0] ^ slot] = ref[0]
        for parity in range(2):
            pieces = []
            for head in range(4):
                piece = near[head, parity]
                if head & 1 == parity:
                    piece = (piece.astype(F32) + far[head].astype(F32)).astype(BF)
                pieces.append(piece)
            total = jnp.concatenate(pieces, 0)
            bias_sum[...] += dot_nt(ones, total)
            turned = padded_turn(total)[:, 0 : total.shape[0]]
            for part, ref, out in ((0, first, stay), (1, second, send)):
                xhat = ref[slide, parity]
                here = slice(part * half, (part + 1) * half)
                acc[...] += dot(total[:, here], normed_of(xhat, gains))
                back = dot(turned[here], weight[...])
                low = back.astype(BF)
                for block in range(4):
                    out[slide, parity, block] = low[block * piece_rows : (block + 1) * piece_rows]
                gain_row = gain_row + jnp.sum(back * xhat.astype(F32), axis=0, keepdims=True)
                bias_row = bias_row + jnp.sum(back, axis=0, keepdims=True)
    ln_sum[...] += rows_of(ln_sum.shape, 0, [gain_row, bias_row])
    if ends:
        missing = wgrads[0].shape[1] - acc.shape[0]
        full = jnp.concatenate([acc[...], jnp.zeros((missing, acc.shape[1]), F32)], 0)
        turned = full.T.astype(BF)
        rows = turned.shape[0] // 8
        for index in range(8):
            part = turned[index * rows : (index + 1) * rows]
            where = slice(index // 2 * rows, (index // 2 + 1) * rows)

            @pl.when(place[1] == index % 2)
            def _():
                wgrads[0][where] = part

            @pl.when(place[1] != index % 2)
            def _():
                wgrads[1][where] = part


def exit_kernel(place, first, second, base, grad_mid, out_rows, gains, *refs):
    tiles_grad, output = refs[-2:]
    rows = base.shape[2]
    half = rows // 2
    xhat, rate = moments(base[0, 0])
    side = pl.program_id(0)
    upstream = jnp.concatenate(
        [jnp.where(side == 0, first[0, part], second[0, part]) for part in range(2)], 0
    ).astype(F32)
    grad = grad_mid[0, 0] + norm_back(xhat, rate, gains[0:1], upstream)
    undo = parity_order(rows, True)
    tiles_grad[0] = dot(undo, grad.astype(BF)).astype(BF)
    output[0] = dot(undo, out_rows[0, 0]).astype(BF)


def mlp_kernel(
    place, base, own, other, cot, w1, w2, wo0, wo1, wo2, wo3, offset, small,
    output, grad_mid, grad_own, grad_other, hidden_out, g_pre_out, normed_t, cot_t, attn_t,
    merged_out, sums, fc1_sum,
    w_out, mid, merged, normed, ff, back,
):
    step = pl.program_id(0)
    rows, width = mid.shape
    part = 256
    half = part // 4

    def cot_at(first):
        slide = first // part
        return jnp.concatenate([cot[0, slide], cot[1, slide]], 0)

    @pl.when(step == 0)
    def _():
        for index, ref in enumerate((wo0, wo1, wo2, wo3)):
            w_out[index * 192 : (index + 1) * 192] = ref[0]
        for first in range(0, rows, part):
            here = pl.ds(first, part)
            slide = first // part
            for side, ref in enumerate((own, other)):
                for parity in range(2):
                    at = first + (2 * side + parity) * half
                    merged[at : at + half] = ref[slide, parity]
            value = jnp.concatenate([base[0, slide], base[1, slide]], 0)
            value = value + (dot(merged[here], w_out[...]) + small[0:1])
            mid[here] = value
            xhat, _ = moments(value)
            low = (xhat * small[1:2] + small[2:3]).astype(BF)
            normed[here] = low
            normed_t[:, first : first + part] = low.T
            cot_t[:, first : first + part] = cot_at(first).T
        for index, slot in enumerate(SLOT_ORDER):
            merged_out[slot] = merged[:, index * 192 : (index + 1) * 192]

    shift = joined(offset[0, 0:3])
    fc1 = jnp.zeros((1, width), F32)
    for first in range(0, rows, part):
        here = pl.ds(first, part)
        pre = dot(normed[here], w1[0]) + shift
        cdf = 0.5 * (1.0 + lax.erf(pre * math.sqrt(0.5)))
        hidden = (pre * cdf).astype(BF)
        slope = cdf + pre * (jnp.exp(-0.5 * pre * pre) * (1.0 / math.sqrt(2.0 * math.pi)))
        g_pre = (dot_nt(cot_at(first), w2[0]) * slope).astype(BF)
        hidden_out[0, here] = hidden
        g_pre_out[0, here] = g_pre
        add_ff = dot(hidden, w2[0])
        add_back = dot_nt(g_pre, w1[0])

        @pl.when(step == 0)
        def _():
            ff[here] = add_ff
            back[here] = add_back

        @pl.when(step != 0)
        def _():
            ff[here] += add_ff
            back[here] += add_back

        fc1 = fc1 + jnp.sum(g_pre.astype(F32), axis=0, keepdims=True)
    fc1_sum[0] = jnp.broadcast_to(fc1, (8, width))

    @pl.when(step == pl.num_programs(0) - 1)
    def _():
        totals = [jnp.zeros((1, width), F32)] * 4
        for first in range(0, rows, part):
            here = pl.ds(first, part)
            slide = first // part
            value = mid[here]
            result = (value + (ff[here] + small[3:4])).astype(BF)
            xhat, rate = moments(value)
            upstream = back[here]
            cot_wide = cot_at(first).astype(F32)
            grad = cot_wide + norm_back(xhat, rate, small[1:2], upstream)
            low = grad.astype(BF)
            back_rows = dot_nt(low, w_out[...]).astype(BF)
            for side, ref in enumerate((grad_own, grad_other)):
                output[side, slide] = result[2 * side * half : 2 * (side + 1) * half]
                grad_mid[side, slide] = grad[2 * side * half : 2 * (side + 1) * half]
                for parity in range(2):
                    at = (2 * side + parity) * half
                    ref[slide, parity, 0] = back_rows[at : at + half]
            attn_t[:, first : first + part] = low.T
            wide = low.astype(F32)
            for index, piece in enumerate((wide, upstream * xhat, upstream, cot_wide)):
                totals[index] = totals[index] + jnp.sum(piece, axis=0, keepdims=True)
        sums[...] = rows_of((8, width), 0, totals)


def weight_grad_kernel(place, *refs, partner):
    groups = [refs[0:6], refs[6:12]]
    outs = refs[12 + 2 * partner :]
    width = refs[0].shape[0]
    piece = width // 8
    slot = pl.program_id(0)

    def rows(index):
        return slice(index // 2 * piece, (index // 2 + 1) * piece)

    def over(index, other):
        return sum(dot(group[index][...], group[other][0]) for group in groups)

    second = over(1, 4)
    for index in range(8):
        side = (index % 2) ^ place[1]
        part = second[index * piece : (index + 1) * piece]
        if not partner:
            outs[1][0, side, rows(index)] = part.astype(BF)
            continue
        part = (part + refs[13][0, side, rows(index)].astype(F32)).astype(BF)
        for here, ref in enumerate(outs[2:]):

            @pl.when(slot == here)
            def _():
                ref[side, rows(index)] = part

    rest = over(2, 5)
    missing = FIRST_COLUMNS - width - rest.shape[1]
    rest = jnp.concatenate([rest, jnp.zeros((width, missing), F32)], 1)
    for first, value in ((0, over(0, 3)), (width, rest)):
        columns = slice(first, first + value.shape[1])
        for index in range(8):
            part = value[index * piece : (index + 1) * piece]
            if not partner:
                outs[0][(index % 2) ^ place[1], 0, rows(index), columns] = part.astype(BF)
                continue
            for side, ref in enumerate(outs[:2]):

                @pl.when((index % 2) ^ place[1] == side)
                def _():
                    there = part + refs[12][side, 0, rows(index), columns].astype(F32)
                    ref[0, rows(index), columns] = there.astype(BF)


def side_fold_kernel(place, first, second, stay, send):
    total = (first[...].astype(F32) + second[...].astype(F32)).astype(BF)
    stay[...] = total[0]
    send[...] = total[1]


def z_fold_both_kernel(place, first, second, third, fourth, stay, send, total):
    columns = first.shape[1]
    total[:, :columns] = (first[...].astype(F32) + second[...].astype(F32)).astype(BF)
    total[:, columns:] = (third[...].astype(F32) + fourth[...].astype(F32)).astype(BF)
    z_halves(place, total, stay, send, True)


def hold_kernel(place, w1, w2, wo, offset, out):
    width = w1.shape[1]
    out[0:width] = w1[...]
    out[width : 2 * width] = w2[...]
    out[2 * width : 2 * width + wo.shape[0]] = wo[...]
    rows = [part.astype(F32) for part in split3(offset[...])]
    out[2 * width + wo.shape[0] :] = rows_of((16, width), 0, rows).astype(BF)


def whole(shape):
    return pl.BlockSpec(tuple(shape), lambda *_: (0,) * len(shape))


def shaped(shape, dtype):
    return jax.ShapeDtypeStruct(tuple(shape), dtype)


def run(name, body, place, ins, outs, grid=(1,), scratch=(), tokens=(), aliases=None, mib=48, us=5):
    arrays = [pair[0] for pair in ins]
    in_specs = [whole(a.shape) if s is None else s for a, s in ins]
    in_specs += [pl.BlockSpec(memory_space=pl.ANY)] * len(tokens)
    out_specs = [whole(o.shape) if s is None else s for o, s in outs]
    given, extra = len(ins), len(tokens)

    def kernel(place_ref, *refs):
        body(place_ref, *refs[:given], *refs[given + extra :])

    return pl.pallas_call(
        kernel,
        grid_spec=pltpu.PrefetchScalarGridSpec(
            num_scalar_prefetch=1,
            grid=grid,
            in_specs=in_specs,
            out_specs=out_specs,
            scratch_shapes=list(scratch),
        ),
        out_shape=[o for o, _ in outs],
        input_output_aliases={k + 1: v for k, v in (aliases or {}).items()},
        compiler_params=pltpu.CompilerParams(vmem_limit_bytes=mib * 1024 * 1024),
        cost_estimate=pl.CostEstimate(
            flops=int(COST * us * 1.1e9), transcendentals=0, bytes_accessed=int(COST * us * 3.6e6)
        ),
        name=name,
    )(place, *arrays, *tokens)


def swap(value, axis, bit):
    return lax.ppermute(value, axis, [(i, i ^ bit) for i in range(lax.axis_size(axis))])


def paired(body, given):
    def kernel(place, *refs):
        near, away = refs[given : given + 2]
        slots = (near.at[0], near.at[1], away.at[0], away.at[1])
        body(place, *refs[:given], *slots, *refs[given + 2 :])

    return kernel


def pair_kernel(place, near, away, out):
    out[0] = near[1]
    out[1] = away[1]


def nested(
    tiles,
    coords,
    lengths,
    padding_mask,
    ln1_gain,
    ln1_bias,
    query_key_value_weight,
    qv_bias,
    attention_output_weight,
    attention_output_bias,
    ln2_gain,
    ln2_bias,
    mlp_entry_matrix,
    mlp_entry_offset,
    feed_output_weight,
    feed_output_bias,
    cotangent,
):
    slides, rows, width = tiles.shape
    group = slides // 2
    half = rows // 2
    lanes = 8 * half
    mine = lanes // 2
    local = query_key_value_weight.shape[2]
    scale = 1.0 / math.sqrt(HEAD_DIM)
    factor = scale * LOG2E
    seq_index = lax.axis_index("seq")
    head_index = lax.axis_index("head")
    z, y = seq_index // 2, seq_index % 2
    x, core = head_index // 2, head_index % 2
    place = jnp.stack([z, y, x, core]).astype(jnp.int32)
    parts = ((0, 1), (1, group - 1))
    token = []

    def step(name, body, ins, outs, **options):
        made = run(name, body, place, ins, outs, tokens=list(token), **options)
        token[:] = [made[-1]]
        return made

    def vm(*shape, dtype=BF):
        return pltpu.VMEM(shape, dtype)

    def bf(*shape):
        return shaped(shape, BF)

    def f32(*shape):
        return shaped(shape, F32)

    def plain(*arrays):
        return [(array, None) for array in arrays]

    def lead_block(*shape):
        return pl.BlockSpec((1,) + shape, lambda k, p: (k,) + (0,) * len(shape))

    def over_z(pieces):
        return [(pieces[0], None)] + [(swap(pieces[k], "seq", 2 * k), None) for k in (1, 2, 3)]

    def over_z_first(pair):
        return pair[0], swap(pair[1], "seq", 4)

    def over_z_second(pair):
        near, away = pair
        send = step("pair", pair_kernel, plain(near, away), [(shaped(near.shape, BF), None)], us=SMALL_US)[0]
        got = swap(send, "seq", 2)
        return [(near, 0), (got, 0), (away, 0), (got, 1)]

    def by_slide(slots):
        out = []
        for array, index in slots:
            shape = array.shape[-2:]
            if index is None:
                out.append((array, lead_block(*shape)))
            else:
                out.append((array, pl.BlockSpec((None, 1) + shape, lambda k, p, i=index: (i, k, 0, 0))))
        return out

    def all_slides(slots):
        out = []
        for array, index in slots:
            if index is None:
                out.append((array, None))
            else:
                shape = array.shape[1:]
                out.append((array, pl.BlockSpec((None,) + shape, lambda k, p, i=index: (i, 0, 0, 0))))
        return out

    total_len = padding_mask.shape[1]
    positions = jnp.arange(total_len, dtype=jnp.int32)
    valid = (positions[None, :] < lengths[:, None]) & (padding_mask == 1)
    valid = valid.astype(BF).reshape(slides * 4, total_len // 4)
    spot = jnp.arange(total_len // 4, dtype=jnp.int32)
    lane = spot % lanes
    chip = lane // half
    there = (
        (y ^ (chip & 1)) * lanes
        + (x ^ ((chip >> 1) & 1)) * (lanes // 2)
        + (core ^ (chip >> 2)) * rows
        + 2 * (lane % half)
        + spot // lanes
    )
    taken = (spot[:, None] == there[None, :]).astype(BF)
    valid = jnp.einsum("rp,pl->rl", valid, taken, preferred_element_type=F32)
    valid = valid.reshape(slides, 8, lanes)

    weight = query_key_value_weight.reshape(width, 3, 4, HEAD_DIM).transpose(2, 1, 3, 0)
    weight = weight.reshape(3 * local, width)
    triple = jnp.stack([qv_bias[0], jnp.zeros_like(qv_bias[0]), qv_bias[1]])
    triple = triple.reshape(3, 4, HEAD_DIM).transpose(1, 0, 2).reshape(3 * local, 1)
    gains = jnp.concatenate([jnp.stack([ln1_gain, ln1_bias]), jnp.zeros((6, width), F32)], 0)
    small = jnp.concatenate(
        [
            jnp.stack([attention_output_bias, ln2_gain, ln2_bias, feed_output_bias]),
            jnp.zeros((4, width), F32),
        ],
        0,
    )
    quarter = width // 4
    freq = jnp.exp(-jnp.log(10000.0) * jnp.arange(quarter, dtype=F32) / quarter)
    angle = jnp.arange(256, dtype=F32)[:, None] * freq
    table = jnp.stack(split3(jnp.concatenate([jnp.sin(angle), jnp.cos(angle)], axis=-1)))

    bases, cots, blocks = [], [], []
    pending = []
    for first, count in parts:

        def at_side(side, depth, first=first):
            return pl.BlockSpec(
                (1, rows, depth), lambda k, p: ((p[1] ^ side) * group + first + k, 0, 0)
            )

        both = pl.BlockSpec((2, 1, rows, width), lambda k, p: (0, k, 0, 0))
        piece = pl.BlockSpec((1, 2, half, width), lambda k, p: (k, 0, 0, 0))
        pair = (2, count, rows, width)
        ins = []
        for array, depth in ((tiles, width), (coords, 2), (cotangent, width)):
            ins += [(array, at_side(0, depth)), (array, at_side(1, depth))]
        base, cot, own, other = step(
            "entry",
            entry_kernel,
            ins + plain(table),
            [
                (f32(*pair), both),
                (bf(*pair), both),
                (bf(count, 2, half, width), piece),
                (bf(count, 2, half, width), piece),
            ],
            grid=(count,),
            us=2.2 * count,
        )
        bases.append(base)
        cots.append(cot)
        shape = (count, 2, 1, half, width)
        pending.append((own.reshape(shape), swap(other, "seq", 1).reshape(shape)))

    def join(first, second):
        shape = first.shape[:2] + (2 * first.shape[2],) + first.shape[3:]
        return step("join", join_kernel, plain(first, second), [(shaped(shape, BF), None)], us=1)[0]

    pending = [join(*pair) for pair in pending]
    pending = [(block, swap(block, "head", 2)) for block in pending]

    qkvs, far_blocks = [None, None], [None, None]
    near_outs, near_grads = [None] * group, [None] * group

    def project(g):
        first, count = parts[g]
        outs = step(
            "qkv",
            qkv_kernel,
            [(blocks[g][0], lead_block(2, mine, width)), (blocks[g][1], lead_block(2, mine, width))]
            + plain(weight, triple, gains),
            [(bf(count, 4, 2, TRIPLE, lanes), lead_block(4, 2, TRIPLE, lanes))]
            + [(bf(count, TRIPLE, lanes), lead_block(TRIPLE, lanes))] * 4,
            grid=(count,),
            us=2.2 * count,
        )
        qkvs[g] = outs[0]
        far_blocks[g] = over_z(outs[1:])

    def spread_columns(g):
        block = join(*pending[g])
        shape = (parts[g][1], 2, mine, width)
        blocks.append((block.reshape(shape), swap(block, "head", 1).reshape(shape)))

    def head_block(k, height):
        return pl.BlockSpec((1, 1, 2, height, lanes), lambda i, p: (k, i, 0, 0, 0))

    def each_head(height):
        return pl.BlockSpec((1, 2, height, lanes), lambda i, p: (i, 0, 0, 0))

    def near_forward(g, k):
        slide = parts[g][0] + k
        near_outs[slide] = step(
            "near_forward",
            partial(near_forward_kernel, slide=slide, factor=factor),
            [(qkvs[g], head_block(k, TRIPLE)), (valid, None)],
            [(f32(4, 2, ACC_ROWS, lanes), each_head(ACC_ROWS))],
            grid=(4,),
            scratch=[vm(2, lanes, AUG), vm(2, OUT_ROWS, lanes), vm(2, lanes, lanes, dtype=F32)],
            us=NEAR_US,
        )[0]

    far_outs, kept, merged = [None, None], [None, None], [None, None]

    def far_kernel(name, body, g, ins, height, scratch, two_steps, us, **options):
        first, count = parts[g]
        body = partial(body, first_slide=first, half=half, factor=factor, **options)
        if two_steps:
            body = paired(body, len(ins))
            block = pl.BlockSpec((2, 1, height, lanes), lambda k, p: (0, k, 0, 0))
            outs = [(bf(2, count, height, lanes), block)] * 2
        else:
            outs = [(bf(count, height, lanes), lead_block(height, lanes))] * 4
        outs = step(name, body, ins, outs, grid=(count,), scratch=scratch, us=us * count)
        return over_z_first(outs) if two_steps else over_z(outs)

    def far_forward(g, two_steps):
        far_outs[g] = far_kernel(
            "far_forward",
            far_forward_kernel,
            g,
            by_slide(far_blocks[g]) + plain(valid),
            OUT_ROWS,
            [
                vm(4, lanes, AUG),
                vm(4, OUT_ROWS, lanes),
                vm(4, AUG, lanes),
                vm(4, AUG, lanes),
                vm(4, lanes, lanes, dtype=F32),
                vm(4, OUT_ROWS, lanes),
            ],
            two_steps,
            8,
        )

    def merge(g):
        first, count = parts[g]
        turned = bf(count, 2, 4, half, local)
        kept[g], stay, send = step(
            "merge",
            merge_kernel,
            plain(*near_outs[first : first + count]) + all_slides(far_outs[g]),
            [(f32(count, 4, 2, ACC_ROWS, lanes), None), (turned, None), (turned, None)],
            scratch=[vm(4, OUT_ROWS, lanes)],
            us=count,
        )
        merged[g] = (stay, swap(send, "head", 1))

    def widen(g, axis, bit):
        pieces = [(a, None) for a in merged[g]]
        count, _, blocks_here, _, columns = merged[g][0].shape
        shape = bf(count, 2, blocks_here // 2, half, 2 * columns)
        stay, send = step("widen", widen_kernel, pieces, [(shape, None)] * 2, us=1)
        merged[g] = (stay, swap(send, axis, bit))

    spread_columns(0)
    project(0)
    near_forward(0, 0)
    far_forward(0, True)
    spread_columns(1)
    packed = step(
        "hold",
        hold_kernel,
        plain(
            mlp_entry_matrix,
            feed_output_weight,
            attention_output_weight,
            mlp_entry_offset[None],
        ),
        [(bf(2 * width + local + 16, width), None)],
        us=2,
    )[0]
    packed = lax.all_gather(packed, "head")
    project(1)
    near_forward(1, 0)
    far_outs[0] = over_z_second(far_outs[0])
    near_forward(1, 1)
    merge(0)
    far_forward(1, False)
    widen(0, "head", 2)

    def last_widen(g):
        first, second = merged[g]
        count = first.shape[0]
        shape = bf(count, 2, 1, half, width)
        stay, send = step("widen", widen_kernel, plain(first, second), [(shape, None)] * 2, us=1)
        shape = (count, 2, half, width)
        merged[g] = (stay.reshape(shape), swap(send, "seq", 1).reshape(shape))

    last_widen(0)
    merge(1)
    widen(1, "head", 2)

    def head_of(i, p):
        return (p[2] ^ (i % 2)) * 2 + (p[3] ^ (i // 2))

    def weight_spec(height, index, slot=None):
        if slot is None:
            return pl.BlockSpec((1, height, width), lambda i, p: (head_of(i, p), index, 0))
        return pl.BlockSpec((1, height, width), lambda i, p: (head_of(slot, p), index, 0))

    def slot_block(*shape):
        return pl.BlockSpec((1,) + shape, lambda i, p: (i,) + (0,) * len(shape))

    owned, given, grads = [None, None], [None, None], [None, None]

    def feed_forward(g):
        count = parts[g][1]
        here = 2 * count * rows
        pair = (2, count, rows, width)
        turned = bf(width, here)
        piece = bf(count, 2, 1, half, width)
        outs = step(
            "mlp",
            mlp_kernel,
            plain(bases[g], *merged[g], cots[g])
            + [(packed, weight_spec(width, 0)), (packed, weight_spec(width, 1))]
            + [(packed, weight_spec(local, 2 * width // local, slot)) for slot in SLOT_ORDER]
            + [(packed, weight_spec(16, (2 * width + local) // 16)), (small, None)],
            [
                (bf(*pair), None),
                (f32(*pair), None),
                (piece, None),
                (piece, None),
                (bf(4, here, width), slot_block(here, width)),
                (bf(4, here, width), slot_block(here, width)),
                (turned, None),
                (turned, None),
                (turned, None),
                (bf(4, here, local), None),
                (f32(8, width), None),
                (f32(4, 8, width), slot_block(8, width)),
            ],
            grid=(4,),
            scratch=[
                vm(width, width),
                vm(here, width, dtype=F32),
                vm(here, width),
                vm(here, width),
                vm(here, width, dtype=F32),
                vm(here, width, dtype=F32),
            ],
            mib=60,
            us=5 + 10 * count,
        )
        output, grad_mid, own, other, hidden, g_pre, normed_t, cot_t, attn_t, slots, sums, fc1 = outs
        owned[g] = (output, grad_mid, sums, fc1)
        grads[g] = (normed_t, cot_t, attn_t, g_pre, hidden, slots)
        given[g] = (own, swap(other, "seq", 1))

    def narrow(g, axis, bit):
        first, second = given[g]
        count, _, blocks_here, _, columns = first.shape
        shape = bf(count, 2, 2 * blocks_here, half, columns // 2)
        stay, send = step("narrow", narrow_kernel, plain(first, second), [(shape, None)] * 2, us=1)
        given[g] = (stay, swap(send, axis, bit))

    feed_forward(0)
    last_widen(1)
    feed_forward(1)

    tall = width // 2
    sent = [
        (bf(2, 2, tall, FIRST_COLUMNS), pl.BlockSpec((2, 1, tall, FIRST_COLUMNS), lambda i, p: (0, i, 0, 0))),
        (bf(2, 2, tall, width), pl.BlockSpec((1, 2, tall, width), lambda i, p: (i, 0, 0, 0))),
    ]
    kept_w = [(bf(2, tall, FIRST_COLUMNS), slot_block(tall, FIRST_COLUMNS))] * 2
    kept_w += [(bf(2, tall, width), None)] * 2

    def weight_grads(first, partner):
        def at(*shape):
            return pl.BlockSpec((1,) + shape, lambda i, p: (i + first, 0, 0))

        ins = []
        for (_, count), (normed_t, cot_t, attn_t, g_pre, hidden, slots) in zip(parts, grads):
            here = 2 * count * rows
            ins += plain(normed_t, cot_t, attn_t)
            ins += [(g_pre, at(here, width)), (hidden, at(here, width)), (slots, at(here, local))]
        return step(
            "weight_grads",
            partial(weight_grad_kernel, partner=len(partner) // 2),
            ins + [(value, spec) for value, (_, spec) in zip(partner, sent)],
            kept_w if partner else sent,
            grid=(2,),
            mib=56,
            us=WG_US,
        )

    def split_fold(pair, axis, bit):
        shape = pair[0].shape[1:]
        stay, send = step(
            "split_fold", side_fold_kernel, plain(*pair), [(shaped(shape, BF), None)] * 2, us=2
        )
        return stay, swap(send, axis, bit)

    grad_rows, far_grads, far_backs = [None, None], [None, None], [None] * group
    backs, sums_so_far = [None, None], []

    def rows_of_gradients(g):
        first, count = parts[g]
        pieces = [value.reshape(count, 2, mine, local) for value in given[g]]
        slot = pl.BlockSpec((1, OUT_ROWS, lanes), lambda k, p: (first + k, 0, 0))
        any_spec = pl.BlockSpec(memory_space=pl.ANY)
        before = [(array, any_spec) for array in far_grads[0] or []]
        outs = step(
            "gradient_rows",
            gradient_rows_kernel,
            [(value, lead_block(2, mine, local)) for value in pieces]
            + [(kept[g], lead_block(4, 2, ACC_ROWS, lanes))]
            + before,
            [(bf(count, 4, 2, OUT_ROWS, lanes), lead_block(4, 2, OUT_ROWS, lanes))]
            + [(bf(group, OUT_ROWS, lanes), slot)] * 4,
            grid=(count,),
            aliases={3 + k: 1 + k for k in range(4)} if before else None,
            us=count,
        )
        grad_rows[g] = outs[0]
        far_grads[0] = outs[1:] if first == 0 else over_z(outs[1:])

    def near_backward(g, k, us=9.7):
        slide = parts[g][0] + k
        near_grads[slide] = step(
            "near_backward",
            partial(near_backward_kernel, slide=slide, factor=factor, scale=scale),
            [(qkvs[g], head_block(k, TRIPLE)), (valid, None), (grad_rows[g], head_block(k, OUT_ROWS))],
            [(bf(4, 2, TRIPLE, lanes), each_head(TRIPLE))],
            grid=(4,),
            scratch=[
                vm(2, lanes, AUG),
                vm(2, OUT_ROWS, lanes),
                vm(2, lanes, OUT_ROWS),
                vm(2, AUG, lanes),
                vm(2, OUT_ROWS, lanes),
                vm(2, lanes, OUT_ROWS),
                vm(2, lanes, OUT_ROWS),
            ],
            us=us,
        )[0]

    def far_backward(g, k):
        slide = parts[g][0] + k
        blocks_here = []
        for array, index in far_blocks[g]:
            shape = array.shape[-2:]
            if index is None:
                spec = pl.BlockSpec((1,) + shape, lambda i, p: (k, 0, 0))
            else:
                spec = pl.BlockSpec((None, 1) + shape, lambda i, p, n=index: (n, k, 0, 0))
            blocks_here.append((array, spec))
        grads_here = [
            (array, pl.BlockSpec((1, OUT_ROWS, lanes), lambda i, p: (slide, 0, 0)))
            for array, _ in far_grads[0]
        ]
        ins = blocks_here + grads_here + plain(valid)
        body = partial(
            far_backward_kernel, first_slide=slide, half=half, factor=factor, scale=scale
        )
        outs = step(
            "far_backward",
            paired(body, len(ins)),
            ins,
            [(bf(2, 1, TRIPLE, lanes), None)] * 2,
            scratch=[
                vm(4, lanes, AUG),
                vm(4, OUT_ROWS, lanes),
                vm(4, lanes, OUT_ROWS),
                vm(4, AUG, lanes),
                vm(4, AUG, lanes),
                vm(4, OUT_ROWS, lanes),
                vm(4, lanes, OUT_ROWS),
                vm(4, lanes, OUT_ROWS),
                vm(4, OUT_ROWS, lanes, dtype=F32),
                vm(4, TRIPLE, lanes),
            ],
            us=FA_US,
        )
        far_backs[slide] = over_z_first(outs)

    def project_back(g, ends):
        first, count = parts[g]
        begins = not ends
        if ends:
            wgrads = [(bf(width // 2, 3 * local + 64), None)] * 2
        else:
            wgrads = [(f32(3 * local, width), None)]
        back = bf(count, 2, 4, half, width)
        outs = step(
            "qkv_backward",
            partial(qkv_backward_kernel, count=count, begins=begins, ends=ends),
            plain(*near_grads[first : first + count])
            + [slot for slide in range(first, first + count) for slot in all_slides(far_backs[slide])]
            + plain(*blocks[g], weight, gains, *sums_so_far),
            wgrads + [(f32(8, 3 * local), None), (f32(8, width), None), (back, None), (back, None)],
            scratch=[vm(4, TRIPLE, lanes)] + ([vm(3 * local, width, dtype=F32)] if ends else []),
            us=QB_US * count,
        )
        sums_so_far[:] = outs[:-2]
        backs[g] = (outs[-2], swap(outs[-1], "head", 1))

    def fold_back(g, axis, bit):
        first, second = backs[g]
        count, _, blocks_here, _, _ = first.shape
        shape = bf(count, 2, blocks_here // 2, half, width)
        stay, send = step("fold", fold_kernel, plain(first, second), [(shape, None)] * 2, us=SMALL_US)
        backs[g] = (stay, swap(send, axis, bit))

    results = []

    def leave(g):
        first, count = parts[g]
        output, grad_mid = owned[g][:2]
        pieces = [value.reshape(count, 2, half, width) for value in backs[g]]
        piece = pl.BlockSpec((1, 2, half, width), lambda s, k, p: (k, 0, 0, 0))
        row = pl.BlockSpec((1, 1, rows, width), lambda s, k, p: (s, k, 0, 0))
        out = pl.BlockSpec((1, rows, width), lambda s, k, p: ((p[1] ^ s) * group + first + k, 0, 0))
        any_spec = pl.BlockSpec(memory_space=pl.ANY)
        results[:] = step(
            "leave",
            exit_kernel,
            [(value, piece) for value in pieces]
            + [(bases[g], row), (grad_mid, row), (output, row), (gains, None)]
            + [(value, any_spec) for value in results],
            [(bf(*tiles.shape), out)] * 2,
            grid=(2, count),
            aliases={6: 0, 7: 1} if results else None,
            us=1 + 1.3 * count,
        )

    def z_fold(pair, nearest):
        first, second = pair
        shape = bf(first.shape[0] // 2, first.shape[1])
        stay, send = step(
            "z_fold",
            partial(z_fold_kernel, nearest=nearest),
            plain(first, second),
            [(shape, None)] * 2,
            scratch=[vm(*first.shape)],
            us=SMALL_US,
        )
        return stay, swap(send, "seq", 2 if nearest else 4)

    def small_step(name, body, pair, bit=None):
        height = 8 if bit is None else 16
        made = step(name, body, plain(*pair), [(f32(height, width), None)], us=SMALL_US)[0]
        return made if bit is None else (made, swap(made, "seq", bit))

    narrow(0, "head", 2)
    sent_w = weight_grads(2, [])
    narrow(0, "head", 1)
    narrow(1, "head", 2)
    rows_of_gradients(0)
    near_backward(0, 0)
    narrow(1, "head", 1)
    rows_of_gradients(1)
    outs = weight_grads(0, [swap(value, "head", 1) for value in sent_w])
    first_w = (outs[0], swap(outs[1], "seq", 1))
    second_w = (outs[2], swap(outs[3], "head", 2))
    near_backward(1, 0, NB_US)
    far_backward(1, 0)
    far_backward(1, 1)
    second_w = split_fold(second_w, "seq", 1)
    first_w = split_fold(first_w, "head", 2)
    far_backward(0, 0)
    far_backs[1] = over_z_second(far_backs[1])
    far_backs[2] = over_z_second(far_backs[2])
    near_backward(1, 1, NB_US)
    stay, send = step(
        "z_fold_both",
        z_fold_both_kernel,
        plain(*first_w, *second_w),
        [(bf(tall // 2, FIRST_COLUMNS + width), None)] * 2,
        scratch=[vm(tall, FIRST_COLUMNS + width)],
        us=2,
    )
    folded = (stay, swap(send, "seq", 2))
    far_backs[0] = over_z_second(far_backs[0])
    project_back(1, False)
    fold_back(1, "head", 2)
    project_back(0, True)
    stay, send, bias_sum, ln_sum = sums_so_far
    grad_in = (stay, swap(send, "seq", 1))
    stay, send = step(
        "small_start",
        small_start_kernel,
        plain(*[owned[g][2] for g in range(2)], *[owned[g][3] for g in range(2)], ln_sum, bias_sum),
        [(f32(16, width), None), (f32(8, width), None)],
        us=SMALL_US,
    )
    common = (stay, swap(send, "head", 1))
    fold_back(0, "head", 2)
    common = small_step("small_first", small_first_kernel, common, 2)
    fold_back(1, "seq", 1)
    common = small_step("add", add_kernel, common, 4)
    fold_back(0, "seq", 1)
    grad_in = z_fold(grad_in, True)
    common = small_step("add", add_kernel, common, 1)
    folded = z_fold(folded, False)
    leave(1)
    grad_in = z_fold(grad_in, False)
    stay, send = step(
        "small_middle", small_middle_kernel, plain(*common), [(f32(8, width), None)] * 2, us=SMALL_US
    )
    common = (stay, swap(send, "head", 2))
    leave(0)
    w_fc1_grad, w_fc2_grad, w_out_grad = step(
        "weights_out",
        weights_out_kernel,
        plain(*folded),
        [
            (f32(width // 8, width), None),
            (f32(width, width // 8), None),
            (f32(local, width // 8), None),
        ],
        us=1.5,
    )
    w_qkv_grad = step(
        "qkv_out",
        qkv_out_kernel,
        plain(*grad_in),
        [(f32(width // 8, 3, local), None)],
        us=1.5,
    )[0]
    common = small_step("add", add_kernel, common)
    per_head = common[7, : 3 * local].reshape(4, 3, HEAD_DIM).transpose(1, 0, 2).reshape(3, local)
    tiles_grad, output = results
    return (
        output,
        tiles_grad,
        common[4],
        common[5],
        w_qkv_grad,
        jnp.stack([per_head[0], per_head[2]]),
        w_out_grad,
        common[0],
        common[1],
        common[2],
        w_fc1_grad,
        common[6],
        w_fc2_grad,
        common[3],
    )


def nests(mesh, tiles, padding_mask):
    sizes = (mesh.shape["seq"], mesh.shape["head"], tiles.shape[0])
    return sizes == (8, 4, 6) and padding_mask.shape[1] <= SEG2


def solution(mesh):
    def program(*args):
        one_span = nests(mesh, args[0], args[3])
        return spread_out(mesh, nested if one_span else on_device)(*args)

    return program


def spread_out(mesh, body):
    placed = (
        P(None, ("seq", "head"), None),
        P(None, ("seq", "head"), None),
        P(),
        P(),
        P(),
        P(),
        P(None, None, "head"),
        P(None, "head"),
        P("head", None),
        P(),
        P(),
        P(),
        P(None, "head"),
        P("head"),
        P("head", None),
        P(),
        P(None, ("seq", "head"), None),
    )
    return jax.shard_map(
        body,
        mesh=mesh,
        in_specs=placed,
        out_specs=(
            P(None, ("seq", "head"), None),
            P(None, ("seq", "head"), None),
            P(),
            P(),
            P("seq", None, "head"),
            P(None, "head"),
            P("head", "seq"),
            P(),
            P(),
            P(),
            P("seq", "head"),
            P("head"),
            P("head", "seq"),
            P(),
        ),
        check_vma=False,
    )
```
